512 devices in a mesh: seq: 64 (over z, x_lo, core), head: 8 (over x_hi, y).
Axes of the slice: x: 4 (x_hi: 2, x_lo: 2; x = x_hi * 2 + x_lo), y: 4, z: 16, core: 2. Of those that a mesh axis runs over, the one named last changes fastest.
Arguments:
- queries: bfloat16 [16384, 8192], P('seq', 'head'), may hold values from -200 to 200
- layer_key_rows: bfloat16 [16384, 1024], P('seq', 'head'), may hold values from -7 to 7
- layer_value_rows: bfloat16 [16384, 1024], P('seq', 'head'), may hold values from -6 to 6
- output_gradient: bfloat16 [16384, 8192], P('seq', 'head'), may hold values from -24 to 24
- output_row_sums: float32 [64, 16384], P('head', 'seq'), may hold values from -72 to 72
- shifted_head_flags: int32 [64], P('head'), may hold values from 0 to 1, as said below
- inputs: bfloat16 [16384, 8192], P('seq', 'head'), may hold values from -6 to 6
- adapter_down_weight: bfloat16 [3, 16, 8192], P(None, None, 'head'), may hold values from -0.0625 to 0.0625
- query_up_weight: bfloat16 [16, 8192], P(None, 'head'), may hold values from -0.75 to 0.75
- key_value_up_weight: bfloat16 [2, 16, 1024], P(None, None, 'head'), may hold values from -0.75 to 0.75
Outputs:
- grad_inputs: bfloat16 [16384, 8192], P('seq', 'head')
- key_value_gradient: bfloat16 [2, 16384, 1024], P(None, 'seq', 'head')
- down_gradient: float32 [3, 16, 8192], P(None, None, 'head')
- grad_up_q: float32 [16, 8192], P(None, 'head')
- grad_up_kv: float32 [2, 16, 1024], P(None, None, 'head')
The draws below stay inside these ranges and needn't reach their ends.
Inputs may be any that keep to these rules, and one draw needn't show every extreme that they name: `shifted_head_flags`: exactly half of the 64 heads have 1.
All inputs are finite; a program needn't handle non-finite values.
Results may differ from the reference program's by a relative error of at most 0.013.
Values may be sent and summed in bfloat16 or wider, within the bound.
A program may use at most 64 MiB of HBM per device.

```python
import math
import jax
import jax.numpy as jnp
from jax import lax

MODEL_WIDTH = 8192
QUERY_HEADS = 64
KEY_VALUE_HEADS = 8
HEAD_SIZE = 128
ADAPTER_RANK = 16
GROUP = 1024
SHIFT = 512
TOKENS = 16384


def shared_rows(key):
    base = jnp.clip(jax.random.normal(jax.random.fold_in(key, 101), (TOKENS, KEY_VALUE_HEADS * HEAD_SIZE), jnp.float32), -6.0, 6.0)
    return base


def draw_layer_key_rows(key, part):
    base = shared_rows(key)
    return base.astype(jnp.bfloat16)


def draw_queries(key, part):
    key = jax.random.fold_in(key, 2)
    return jnp.clip(jax.random.normal(key, (TOKENS, QUERY_HEADS * HEAD_SIZE), jnp.float32), -6.0, 6.0).astype(jnp.bfloat16)


def draw_shifted_head_flags(key, part):
    key = jax.random.fold_in(key, 3)
    order = jax.random.permutation(key, QUERY_HEADS)
    return (order < QUERY_HEADS // 2).astype(jnp.int32)


def steps_of(stream_key, extent, split, low, high):
    factor_of, own = 1.0, jax.random.fold_in(stream_key, 6)
    for dim, blocks in split:
        draws = jnp.exp(jax.random.uniform(jax.random.fold_in(own, dim), (blocks,), jnp.float32, low / len(split), high / len(split)))
        factor_of = factor_of * jnp.repeat(draws, extent[dim] // blocks).reshape([-1 if axis == dim else 1 for axis in range(len(extent))])
    return factor_of


def centred(rng, shape, scale, bound, shards=(), kind=jnp.bfloat16):
    loudness = steps_of(rng, shape, shards, -0.22, 0.18) if shards else 1.0
    values = jax.random.normal(rng, shape, jnp.float32) * scale * loudness
    return jnp.minimum(jnp.maximum(values, -bound), bound).astype(kind)


def setup_inputs(seed: int = 0) -> dict:
    splits = jax.random.split(jax.random.key(seed), 11)
    queries = draw_queries(jax.random.fold_in(splits[10], 71), 0)
    layer_key_rows = draw_layer_key_rows(jax.random.fold_in(splits[10], 71), 0)
    layer_value_rows = centred(splits[2], (TOKENS, KEY_VALUE_HEADS * HEAD_SIZE), 1.0, 6.0, ((0, 64), (1, 8)))
    output_gradient = centred(splits[3], (TOKENS, QUERY_HEADS * HEAD_SIZE), 4.0, 24.0, ((0, 64), (1, 8)))
    output_row_sums = centred(splits[4], (QUERY_HEADS, TOKENS), 12.0, 72.0, ((0, 8), (1, 64)), jnp.float32)
    shifted_head_flags = draw_shifted_head_flags(jax.random.fold_in(splits[10], 71), 0)
    inputs = centred(splits[6], (TOKENS, MODEL_WIDTH), 1.0, 6.0, ((0, 64), (1, 8)))
    adapter_down_weight = centred(splits[7], (3, ADAPTER_RANK, MODEL_WIDTH), MODEL_WIDTH ** -0.5, 0.0625, ((2, 8),))
    query_up_weight = centred(splits[8], (ADAPTER_RANK, QUERY_HEADS * HEAD_SIZE), (4 * ADAPTER_RANK) ** -0.5, 0.75, ((1, 8),))
    key_value_up_weight = centred(splits[9], (2, ADAPTER_RANK, KEY_VALUE_HEADS * HEAD_SIZE), (4 * ADAPTER_RANK) ** -0.5, 0.75, ((2, 8),))
    return {"queries": queries, "layer_key_rows": layer_key_rows, "layer_value_rows": layer_value_rows, "output_gradient": output_gradient, "output_row_sums": output_row_sums, "shifted_head_flags": shifted_head_flags, "inputs": inputs, "adapter_down_weight": adapter_down_weight, "query_up_weight": query_up_weight, "key_value_up_weight": key_value_up_weight}


adapter_scale = 2.0
masked_score = -1e+30

def to_bf16_f32(values):
    return lax.optimization_barrier(values.astype(jnp.bfloat16)).astype(jnp.float32)

def head_backward(query_head, key_head, value_head, grad_head, row_term, shifted):
    score_scale = HEAD_SIZE ** (-0.5)
    group_count = TOKENS // GROUP

    def roll_in(array):
        return jnp.where(shifted > 0, jnp.roll(array, -SHIFT, axis=0), array)

    def roll_out(array):
        return jnp.where(shifted > 0, jnp.roll(array, SHIFT, axis=0), array)
    query_g = roll_in(query_head).reshape(group_count, GROUP, HEAD_SIZE).astype(jnp.float32)
    key_g = roll_in(key_head).reshape(group_count, GROUP, HEAD_SIZE).astype(jnp.float32)
    value_g = roll_in(value_head).reshape(group_count, GROUP, HEAD_SIZE).astype(jnp.float32)
    grad_g = roll_in(grad_head).reshape(group_count, GROUP, HEAD_SIZE).astype(jnp.float32)
    term_g = roll_in(row_term).reshape(group_count, GROUP)
    causal = jnp.tril(jnp.ones((GROUP, GROUP), dtype=bool))
    scores = jnp.einsum('gid,gjd->gij', query_g, key_g) * score_scale
    scores = jnp.where(causal, scores, masked_score)
    row_max = lax.optimization_barrier(jnp.max(scores, axis=2, keepdims=True))
    weights = jnp.where(causal, jnp.exp(scores - row_max), 0.0)
    prob_rows = weights / lax.optimization_barrier(jnp.sum(weights, axis=2, keepdims=True))
    prob_low = to_bf16_f32(prob_rows)
    grad_values = jnp.einsum('gij,gid->gjd', prob_low, grad_g)
    grad_probs = jnp.einsum('gid,gjd->gij', grad_g, value_g)
    grad_scores = to_bf16_f32(prob_rows * (grad_probs - term_g[:, :, None]))
    grad_query = (jnp.einsum('gij,gjd->gid', grad_scores, key_g) * score_scale).astype(jnp.bfloat16)
    grad_keys = jnp.einsum('gij,gid->gjd', grad_scores, query_g) * score_scale
    return (roll_out(grad_query.reshape(TOKENS, HEAD_SIZE)), roll_out(grad_keys.reshape(TOKENS, HEAD_SIZE)), roll_out(grad_values.reshape(TOKENS, HEAD_SIZE)))

def reference(queries, layer_key_rows, layer_value_rows, output_gradient, output_row_sums, shifted_head_flags, inputs, adapter_down_weight, query_up_weight, key_value_up_weight):
    per_kv = QUERY_HEADS // KEY_VALUE_HEADS
    query_heads = queries.reshape(TOKENS, KEY_VALUE_HEADS, per_kv, HEAD_SIZE).transpose(1, 2, 0, 3)
    grad_heads = output_gradient.reshape(TOKENS, KEY_VALUE_HEADS, per_kv, HEAD_SIZE).transpose(1, 2, 0, 3)
    key_heads = layer_key_rows.reshape(TOKENS, KEY_VALUE_HEADS, HEAD_SIZE).transpose(1, 0, 2)
    value_heads = layer_value_rows.reshape(TOKENS, KEY_VALUE_HEADS, HEAD_SIZE).transpose(1, 0, 2)
    term_heads = output_row_sums.reshape(KEY_VALUE_HEADS, per_kv, TOKENS)
    shift_heads = shifted_head_flags.reshape(KEY_VALUE_HEADS, per_kv)

    def per_group(bundle):
        group_queries, group_grads, key_head, value_head, group_terms, group_shifts = bundle

        def one_head(running, head_item):
            query_head, grad_head, row_term, shifted = head_item
            grad_query, grad_keys, grad_values = head_backward(query_head, key_head, value_head, grad_head, row_term, shifted)
            return ((running[0] + grad_keys, running[1] + grad_values), grad_query)
        zeros_init = jnp.zeros((TOKENS, HEAD_SIZE), jnp.float32)
        (key_total, value_total), query_gradient_rows = lax.scan(one_head, (zeros_init, zeros_init), (group_queries, group_grads, group_terms, group_shifts))
        return (query_gradient_rows, key_total, value_total)
    grad_q_heads, key_totals, value_totals = lax.map(per_group, (query_heads, grad_heads, key_heads, value_heads, term_heads, shift_heads))
    query_gradient_rows = grad_q_heads.transpose(2, 0, 1, 3).reshape(TOKENS, QUERY_HEADS * HEAD_SIZE)
    key_value_gradient = jnp.stack([key_totals.transpose(1, 0, 2).reshape(TOKENS, KEY_VALUE_HEADS * HEAD_SIZE), value_totals.transpose(1, 0, 2).reshape(TOKENS, KEY_VALUE_HEADS * HEAD_SIZE)]).astype(jnp.bfloat16)
    flattened_down = adapter_down_weight.reshape(3 * ADAPTER_RANK, MODEL_WIDTH)
    down_in = jnp.dot(inputs, flattened_down.T, preferred_element_type=jnp.float32)
    down_low = down_in.astype(jnp.bfloat16)
    up_backward_term = jnp.concatenate([jnp.dot(query_gradient_rows, query_up_weight.T, preferred_element_type=jnp.float32), jnp.dot(key_value_gradient[0], key_value_up_weight[0].T, preferred_element_type=jnp.float32), jnp.dot(key_value_gradient[1], key_value_up_weight[1].T, preferred_element_type=jnp.float32)], axis=1)
    up_low = up_backward_term.astype(jnp.bfloat16)
    grad_inputs = (adapter_scale * jnp.dot(up_low, flattened_down, preferred_element_type=jnp.float32)).astype(jnp.bfloat16)
    multiplier = adapter_scale / math.sqrt(TOKENS)
    down_gradient = multiplier * jnp.dot(up_low.T, inputs, preferred_element_type=jnp.float32).reshape(3, ADAPTER_RANK, MODEL_WIDTH)
    grad_up_q = multiplier * jnp.dot(down_low[:, :ADAPTER_RANK].T, query_gradient_rows, preferred_element_type=jnp.float32)
    grad_up_kv = multiplier * jnp.stack([jnp.dot(down_low[:, ADAPTER_RANK:2 * ADAPTER_RANK].T, key_value_gradient[0], preferred_element_type=jnp.float32), jnp.dot(down_low[:, 2 * ADAPTER_RANK:].T, key_value_gradient[1], preferred_element_type=jnp.float32)])
    return (grad_inputs, key_value_gradient, down_gradient, grad_up_q, grad_up_kv)
```

```python
import functools
import math

import jax
import jax.numpy as jnp
from jax import lax
from jax.experimental import pallas as pl
from jax.experimental.pallas import tpu as pltpu
from jax.sharding import PartitionSpec as P

HEAD_SIZE = 128
GROUP = 1024
RANK = 16
QUAD = 4
UNITS = 16
LOG2E = 1.4426950408889634
BIG = 1e30
ADAPTER_SCALE = 2.0

MESH = pl.DeviceIdType.MESH
F32 = jnp.float32
BF16 = jnp.bfloat16


def dot_nn(a, b):
    return lax.dot_general(a, b, (((1,), (0,)), ((), ())), preferred_element_type=F32)


def dot_nt(a, b):
    return lax.dot_general(a, b, (((1,), (1,)), ((), ())), preferred_element_type=F32)


def kernel(
    seq_count,
    head_count,
    q_hbm, k_hbm, v_hbm, do_hbm, rs_hbm, flags, x_hbm, wd_hbm, wq_hbm, wkv_hbm,
    kv_out, up_out, g_out, c_out,
    q_v, do_v, x_v, wd_v, wq_v, wkv_v, rs_v,
    kwin, vwin, k_t, probs, dscores, own_kv, kv_send, kv_recv,
    down_send, down_recv, down_low, upq_send, upq_recv, upkv_send, upkv_recv,
    g_full, g_send, g_recv, c_full, c_recv, units, z_recv, cz,
    load_sem, win_send, win_recv, down_ss, down_rs, upq_ss, upq_rs, upkv_ss, upkv_rs,
    kv_ss, kv_rs, quad_ss, quad_rs, quadc_ss, quadc_rs, z_ss, z_rs, cz_ss, cz_rs,
    ag_ss, ag_rs, fin_ss, fin_rs, finc_ss, finc_rs,
):
    tokens = q_v.shape[0]
    heads = q_v.shape[1] // HEAD_SIZE
    nz = seq_count // QUAD
    per_owner = UNITS // nz
    s = lax.axis_index("seq")
    hd = lax.axis_index("head")
    zi = s // QUAD
    b = s % QUAD
    core = s % 2
    x_lo = b // 2
    scale = HEAD_SIZE ** -0.5
    multiplier = ADAPTER_SCALE / math.sqrt(tokens * seq_count)

    def seq_at(by):
        return lax.rem(s + by + seq_count, seq_count)

    def head_at(by):
        return lax.rem(hd + by + head_count, head_count)

    def z_at(by):
        return lax.rem(zi + by + nz, nz)

    def quad_at(by):
        return lax.rem(b + by + QUAD, QUAD)

    def z_peer(by):
        return z_at(by) * QUAD + b

    def quad_peer(by):
        return zi * QUAD + quad_at(by)

    loads = [
        pltpu.make_async_copy(src, dst, load_sem.at[i])
        for i, (src, dst) in enumerate([
            (k_hbm, kwin.at[3]), (v_hbm, vwin.at[3]), (x_hbm, x_v), (wd_hbm, wd_v), (q_hbm, q_v),
            (do_hbm, do_v), (rs_hbm, rs_v), (wq_hbm, wq_v), (wkv_hbm, wkv_v),
        ])
    ]
    for copy in loads:
        copy.start()

    barrier = pltpu.get_barrier_semaphore()
    near = [-3, -2, -1, 1, 2, 3]
    for by in near:
        pl.semaphore_signal(barrier, inc=1, device_id={"seq": seq_at(by)}, device_id_type=MESH)
    for by in range(1, head_count):
        pl.semaphore_signal(barrier, inc=1, device_id={"head": head_at(by)}, device_id_type=MESH)

    def greet(by, _):
        pl.semaphore_signal(barrier, inc=1, device_id={"seq": z_peer(by)}, device_id_type=MESH)
        return 0

    lax.fori_loop(1, nz, greet, 0)
    pl.semaphore_wait(barrier, len(near) + head_count - 1 + nz - 1)

    def window_copy(which, by):
        src, dst = ((k_hbm, kwin), (v_hbm, vwin))[which]
        return pltpu.make_async_remote_copy(
            src_ref=src, dst_ref=dst.at[3 - by],
            send_sem=win_send.at[which, by], recv_sem=win_recv.at[which, 3 - by],
            device_id={"seq": seq_at(by)}, device_id_type=MESH,
        )

    for which in range(2):
        window_copy(which, 1).start()
        window_copy(which, 2).start()

        @pl.when(core == 0)
        def _():
            window_copy(which, 3).start()

    def head_copy(src, dst, ss, rs, by):
        return pltpu.make_async_remote_copy(
            src_ref=src, dst_ref=dst.at[by], send_sem=ss.at[by], recv_sem=rs.at[by],
            device_id={"head": head_at(by)}, device_id_type=MESH,
        )

    loads[2].wait()
    loads[3].wait()
    down_part = dot_nt(wd_v[...], x_v[...])
    down_send[...] = down_part.astype(BF16)
    for by in range(1, head_count):
        head_copy(down_send, down_recv, down_ss, down_rs, by).start()

    for i in (0, 1, 4, 5, 6, 7, 8):
        loads[i].wait()

    row_id = lax.broadcasted_iota(jnp.int32, (tokens, tokens), 0)
    col_id = lax.broadcasted_iota(jnp.int32, (tokens, tokens), 1)
    causal = jnp.where(row_id <= col_id, 0.0, -BIG).astype(F32)
    want = (1 - x_lo).astype(F32)
    even = (1 - core).astype(F32)
    c2 = scale * LOG2E

    def head_cols(ref, h):
        return ref[:, pl.ds(pl.multiple_of(h * HEAD_SIZE, HEAD_SIZE), HEAD_SIZE)]

    def attention(slots):
        def rows(j):
            return pl.ds(j * tokens, tokens)

        for j in slots:
            if j < 3:
                window_copy(0, 3 - j).wait_recv()
            k_t[:, j * tokens : (j + 1) * tokens] = kwin[j].astype(F32).T.astype(BF16)

        def forward(h, _):
            q = head_cols(q_v, h)
            differs = flags[h].astype(F32) - want
            far = differs * differs * BIG
            bias = {0: far, 1: far, 2: far * even, 3: 0.0}
            score = {}
            top = None
            for j in slots:
                score[j] = dot_nt(kwin[j], q)
                if j == 3:
                    score[j] = score[j] + causal
                high = jnp.max(score[j], axis=0, keepdims=True) - bias[j]
                top = high if top is None else jnp.maximum(top, high)
            weight = {}
            total = None
            for j in slots:
                weight[j] = jnp.exp2(score[j] * c2 - (top * c2 + bias[j]))
                part = jnp.sum(weight[j], axis=0, keepdims=True)
                total = part if total is None else total + part
            inverse = 1.0 / total
            for j in slots:
                probs[h, rows(j), :] = (weight[j] * inverse).astype(BF16)
            return 0

        lax.fori_loop(0, heads, forward, 0)

        for j in slots:
            if j < 3:
                window_copy(1, 3 - j).wait_recv()

            def backward(h, acc):
                dk, dv = acc
                q = head_cols(q_v, h)
                do = head_cols(do_v, h)
                p = probs[h, rows(j), :]
                dp = dot_nt(vwin[j], do)
                ds = (p.astype(F32) * (dp - rs_v[pl.ds(h, 1), :])).astype(BF16)
                dscores[h, rows(j), :] = ds
                return dk + dot_nn(ds, q), dv + dot_nn(p, do)

            zero = jnp.zeros((tokens, HEAD_SIZE), F32)
            dk, dv = lax.fori_loop(0, heads, backward, (zero, zero))
            if j == 3:
                own_kv[0] = dk * scale
                own_kv[1] = dv
            else:
                kv_send[j, 0] = (dk * scale).astype(BF16)
                kv_send[j, 1] = dv.astype(BF16)
                grad_copy(3 - j).start()

    def grad_copy(by):
        return pltpu.make_async_remote_copy(
            src_ref=kv_send.at[3 - by], dst_ref=kv_recv.at[by],
            send_sem=kv_ss.at[by], recv_sem=kv_rs.at[by],
            device_id={"seq": seq_at(-by)}, device_id_type=MESH,
        )

    @pl.when(core == 1)
    def _():
        attention((0, 1, 2, 3))

    @pl.when(core == 0)
    def _():
        attention((1, 2, 3))

    down = down_part
    for by in range(1, head_count):
        head_copy(down_send, down_recv, down_ss, down_rs, by).wait_recv()
        down = down + down_recv[by].astype(F32)
    down_low[...] = down.astype(BF16)

    def query_grads(first):
        def one(h, acc):
            dq = (dot_nn(k_t[:, first:], dscores[h, first:, :]) * scale).astype(BF16)
            a = dot_nt(down_low[:RANK, :], dq)
            g_col = pl.ds(pl.multiple_of((h % 2) * HEAD_SIZE, HEAD_SIZE), HEAD_SIZE)
            g_full[h // 2, 3 * RANK :, g_col] = a
            return acc + dot_nn(head_cols(wq_v, h), dq)

        upq_send_f32 = lax.fori_loop(0, heads, one, jnp.zeros((RANK, tokens), F32))
        upq_send[...] = upq_send_f32.astype(BF16)

    @pl.when(core == 1)
    def _():
        query_grads(0)

    @pl.when(core == 0)
    def _():
        query_grads(tokens)

    for by in range(1, head_count):
        head_copy(upq_send, upq_recv, upq_ss, upq_rs, by).start()

    grad_copy(1).wait_recv()
    grad_copy(2).wait_recv()

    @pl.when(core == 0)
    def _():
        grad_copy(3).wait_recv()
        own_kv[...] = own_kv[...] + kv_recv[3].astype(F32)

    dkv = (own_kv[...] + kv_recv[1].astype(F32) + kv_recv[2].astype(F32)).astype(BF16)
    kv_out[...] = dkv
    for c in range(2):
        upkv_send[c * RANK : (c + 1) * RANK, :] = dot_nt(
            wkv_v[c * RANK : (c + 1) * RANK, :], dkv[c]
        ).astype(BF16)
    for by in range(1, head_count):
        head_copy(upkv_send, upkv_recv, upkv_ss, upkv_rs, by).start()
    for c in range(2):
        part = dot_nn(down_low[(c + 1) * RANK : (c + 2) * RANK, :], dkv[c])
        c_full[2 * c] = part[:8]
        c_full[2 * c + 1] = part[8:]

    up = upq_send[...].astype(F32)
    for by in range(1, head_count):
        head_copy(upq_send, upq_recv, upq_ss, upq_rs, by).wait_recv()
        up = up + upq_recv[by].astype(F32)
    up_out[:RANK, :] = up.astype(BF16)
    up = upkv_send[...].astype(F32)
    for by in range(1, head_count):
        head_copy(upkv_send, upkv_recv, upkv_ss, upkv_rs, by).wait_recv()
        up = up + upkv_recv[by].astype(F32)
    up_out[RANK:, :] = up.astype(BF16)
    width = x_v.shape[1] // QUAD
    for c in range(QUAD):
        g_full[c, : 3 * RANK, :] = dot_nn(up_out[...], x_v[:, c * width : (c + 1) * width])
    g_send[...] = g_full[...].astype(BF16)

    def quad_copy(by):
        return pltpu.make_async_remote_copy(
            src_ref=g_send.at[quad_at(by)], dst_ref=g_recv.at[by],
            send_sem=quad_ss.at[by], recv_sem=quad_rs.at[by],
            device_id={"seq": quad_peer(by)}, device_id_type=MESH,
        )

    def quad_copy_c(by):
        return pltpu.make_async_remote_copy(
            src_ref=c_full.at[quad_at(by)], dst_ref=c_recv.at[by],
            send_sem=quadc_ss.at[by], recv_sem=quadc_rs.at[by],
            device_id={"seq": quad_peer(by)}, device_id_type=MESH,
        )

    for by in range(1, QUAD):
        quad_copy(by).start()
        quad_copy_c(by).start()
    g = g_full[b]
    c_sum = c_full[b]
    for by in range(1, QUAD):
        quad_copy(by).wait_recv()
        quad_copy_c(by).wait_recv()
        g = g + g_recv[by].astype(F32)
        c_sum = c_sum + c_recv[by]
    for u in range(UNITS):
        r, col = u // 2, u % 2
        units[u // per_owner, u % per_owner] = g[r * 8 : r * 8 + 8, col * 128 : col * 128 + 128]
    cz[zi] = c_sum

    def z_copy(by):
        return pltpu.make_async_remote_copy(
            src_ref=units.at[z_at(by)], dst_ref=z_recv.at[by],
            send_sem=z_ss.at[by], recv_sem=z_rs.at[by],
            device_id={"seq": z_peer(by)}, device_id_type=MESH,
        )

    def cz_copy(by, slot):
        return pltpu.make_async_remote_copy(
            src_ref=cz.at[slot], dst_ref=cz.at[slot],
            send_sem=cz_ss.at[by], recv_sem=cz_rs.at[slot],
            device_id={"seq": z_peer(by)}, device_id_type=MESH,
        )

    def send_z(by, _):
        z_copy(by).start()
        return 0

    def send_cz(by, _):
        cz_copy(by, zi).start()
        return 0

    lax.fori_loop(1, nz, send_z, 0)
    lax.fori_loop(1, nz, send_cz, 0)

    def add_z(by, acc):
        z_copy(by).wait_recv()
        return acc + z_recv[by]

    total = lax.fori_loop(1, nz, add_z, units[zi]) * multiplier

    def unit_slice(u, quad):
        return (
            pl.ds(pl.multiple_of((u // 2) * 8, 8), 8),
            pl.ds(pl.multiple_of(quad * width + (u % 2) * 128, 128), 128),
        )

    for i in range(per_owner):
        at = unit_slice(zi * per_owner + i, b)
        g_out[at[0], at[1]] = total[i]

    def gather_copy(by, owner, i):
        u = owner * per_owner + i
        at = unit_slice(u, b)
        return pltpu.make_async_remote_copy(
            src_ref=g_out.at[at[0], at[1]], dst_ref=g_out.at[at[0], at[1]],
            send_sem=ag_ss.at[by * per_owner + i], recv_sem=ag_rs.at[u],
            device_id={"seq": z_peer(by)}, device_id_type=MESH,
        )

    def send_gather(by, _):
        for i in range(per_owner):
            gather_copy(by, zi, i).start()
        return 0

    lax.fori_loop(1, nz, send_gather, 0)

    def wait_cz(by, _):
        cz_copy(by, z_at(-by)).wait_recv()
        return 0

    lax.fori_loop(1, nz, wait_cz, 0)
    c_total = jnp.sum(cz[...], axis=0) * multiplier
    c_at = pl.ds(pl.multiple_of(b * 8, 8), 8)
    c_out[c_at, :] = c_total

    def wait_gather(by, _):
        for i in range(per_owner):
            gather_copy(by, z_at(-by), i).wait_recv()
        return 0

    lax.fori_loop(1, nz, wait_gather, 0)

    def final_copy(by, quad):
        cols = pl.ds(pl.multiple_of(quad * width, 128), width)
        return pltpu.make_async_remote_copy(
            src_ref=g_out.at[:, cols], dst_ref=g_out.at[:, cols],
            send_sem=fin_ss.at[by], recv_sem=fin_rs.at[by],
            device_id={"seq": quad_peer(by)}, device_id_type=MESH,
        )

    def final_copy_c(by, quad):
        at = pl.ds(pl.multiple_of(quad * 8, 8), 8)
        return pltpu.make_async_remote_copy(
            src_ref=c_out.at[at, :], dst_ref=c_out.at[at, :],
            send_sem=finc_ss.at[by], recv_sem=finc_rs.at[by],
            device_id={"seq": quad_peer(by)}, device_id_type=MESH,
        )

    for by in range(1, QUAD):
        final_copy(by, b).start()
        final_copy_c(by, b).start()

    for which in range(2):
        window_copy(which, 1).wait_send()
        window_copy(which, 2).wait_send()

        @pl.when(core == 0)
        def _():
            window_copy(which, 3).wait_send()

    grad_copy(1).wait_send()
    grad_copy(2).wait_send()

    @pl.when(core == 1)
    def _():
        grad_copy(3).wait_send()

    for by in range(1, head_count):
        head_copy(down_send, down_recv, down_ss, down_rs, by).wait_send()
        head_copy(upq_send, upq_recv, upq_ss, upq_rs, by).wait_send()
        head_copy(upkv_send, upkv_recv, upkv_ss, upkv_rs, by).wait_send()
    for by in range(1, QUAD):
        quad_copy(by).wait_send()
        quad_copy_c(by).wait_send()

    def wait_z(by, _):
        z_copy(by).wait_send()
        cz_copy(by, zi).wait_send()
        for i in range(per_owner):
            gather_copy(by, zi, i).wait_send()
        return 0

    lax.fori_loop(1, nz, wait_z, 0)
    for by in range(1, QUAD):
        final_copy(by, quad_at(-by)).wait_recv()
        final_copy_c(by, quad_at(-by)).wait_recv()
        final_copy(by, b).wait_send()
        final_copy_c(by, b).wait_send()


def per_device(
    queries, layer_key_rows, layer_value_rows, output_gradient, output_row_sums,
    shifted_head_flags, inputs, adapter_down_weight, query_up_weight, key_value_up_weight,
):
    seq_count = lax.axis_size("seq")
    head_count = lax.axis_size("head")
    tokens, columns = queries.shape
    heads = columns // HEAD_SIZE
    width = inputs.shape[1]
    nz = seq_count // QUAD
    per_owner = UNITS // nz
    flat_down = adapter_down_weight.reshape(3 * RANK, width)
    flat_kv_up = key_value_up_weight.reshape(2 * RANK, HEAD_SIZE)
    vmem = pltpu.VMEM
    sem = pltpu.SemaphoreType.DMA
    anywhere = pl.BlockSpec(memory_space=pl.ANY)
    in_vmem = pl.BlockSpec(memory_space=pltpu.VMEM)
    kv_out, up_out, g_out, c_out = pl.pallas_call(
        functools.partial(kernel, seq_count, head_count),
        out_shape=(
            jax.ShapeDtypeStruct((2, tokens, HEAD_SIZE), BF16),
            jax.ShapeDtypeStruct((3 * RANK, tokens), BF16),
            jax.ShapeDtypeStruct((4 * RANK, width), F32),
            jax.ShapeDtypeStruct((2 * RANK, HEAD_SIZE), F32),
        ),
        in_specs=[anywhere] * 5 + [pl.BlockSpec(memory_space=pltpu.SMEM)] + [anywhere] * 4,
        out_specs=(in_vmem,) * 4,
        scratch_shapes=[
            vmem((tokens, columns), BF16),
            vmem((tokens, columns), BF16),
            vmem((tokens, width), BF16),
            vmem((3 * RANK, width), BF16),
            vmem((RANK, columns), BF16),
            vmem((2 * RANK, HEAD_SIZE), BF16),
            vmem((heads, tokens), F32),
            vmem((4, tokens, HEAD_SIZE), BF16),
            vmem((4, tokens, HEAD_SIZE), BF16),
            vmem((HEAD_SIZE, 4 * tokens), BF16),
            vmem((heads, 4 * tokens, tokens), BF16),
            vmem((heads, 4 * tokens, tokens), BF16),
            vmem((2, tokens, HEAD_SIZE), F32),
            vmem((3, 2, tokens, HEAD_SIZE), BF16),
            vmem((4, 2, tokens, HEAD_SIZE), BF16),
            vmem((3 * RANK, tokens), BF16),
            vmem((head_count, 3 * RANK, tokens), BF16),
            vmem((3 * RANK, tokens), BF16),
            vmem((RANK, tokens), BF16),
            vmem((head_count, RANK, tokens), BF16),
            vmem((2 * RANK, tokens), BF16),
            vmem((head_count, 2 * RANK, tokens), BF16),
            vmem((QUAD, 4 * RANK, width // QUAD), F32),
            vmem((QUAD, 4 * RANK, width // QUAD), BF16),
            vmem((QUAD, 4 * RANK, width // QUAD), BF16),
            vmem((QUAD, 8, HEAD_SIZE), F32),
            vmem((QUAD, 8, HEAD_SIZE), F32),
            vmem((nz, per_owner, 8, 128), F32),
            vmem((nz, per_owner, 8, 128), F32),
            vmem((nz, 8, HEAD_SIZE), F32),
            sem((9,)),
            sem((2, 4)), sem((2, 4)),
            sem((head_count,)), sem((head_count,)),
            sem((head_count,)), sem((head_count,)),
            sem((head_count,)), sem((head_count,)),
            sem((4,)), sem((4,)),
            sem((QUAD,)), sem((QUAD,)),
            sem((QUAD,)), sem((QUAD,)),
            sem((nz,)), sem((nz,)),
            sem((nz,)), sem((nz,)),
            sem((UNITS,)), sem((UNITS,)),
            sem((QUAD,)), sem((QUAD,)),
            sem((QUAD,)), sem((QUAD,)),
        ],
        compiler_params=pltpu.CompilerParams(
            collective_id=0, has_side_effects=True, vmem_limit_bytes=48 * 1024 * 1024
        ),
    )(
        queries, layer_key_rows, layer_value_rows, output_gradient, output_row_sums,
        shifted_head_flags, inputs, flat_down, query_up_weight, flat_kv_up,
    )
    grad_inputs = (
        ADAPTER_SCALE
        * lax.dot_general(
            up_out, flat_down, (((0,), (0,)), ((), ())), preferred_element_type=F32
        )
    ).astype(BF16)
    return (
        grad_inputs,
        kv_out,
        g_out[: 3 * RANK].reshape(3, RANK, width),
        g_out[3 * RANK :],
        c_out.reshape(2, RANK, HEAD_SIZE),
    )


def solution(mesh):
    placed = (
        P("seq", "head"),
        P("seq", "head"),
        P("seq", "head"),
        P("seq", "head"),
        P("head", "seq"),
        P("head"),
        P("seq", "head"),
        P(None, None, "head"),
        P(None, "head"),
        P(None, None, "head"),
    )
    return jax.shard_map(
        per_device,
        mesh=mesh,
        in_specs=placed,
        out_specs=(
            P("seq", "head"),
            P(None, "seq", "head"),
            P(None, None, "head"),
            P(None, "head"),
            P(None, None, "head"),
        ),
        check_vma=False,
    )
```

```python
import functools
import math

import jax
import jax.numpy as jnp
from jax import lax
from jax.experimental import pallas as pl
from jax.experimental.pallas import tpu as pltpu
from jax.sharding import PartitionSpec as P

HEAD_SIZE = 128
GROUP = 1024
RANK = 16
QUAD = 4
UNITS = 16
LOG2E = 1.4426950408889634
BIG = 1e30
ADAPTER_SCALE = 2.0
VMEM_BYTES = 63 * 1024 * 1024

MESH = pl.DeviceIdType.MESH
F32 = jnp.float32
BF16 = jnp.bfloat16


def dot_nn(a, b):
    return lax.dot_general(a, b, (((1,), (0,)), ((), ())), preferred_element_type=F32)


def dot_nt(a, b):
    return lax.dot_general(a, b, (((1,), (1,)), ((), ())), preferred_element_type=F32)


def kernel(
    seq_count,
    head_count,
    q_hbm, k_hbm, v_hbm, do_hbm, rs_hbm, flags, x_hbm, wd_hbm, wq_hbm, wkv_hbm,
    kv_out, x_out, g_out, c_out,
    up_out, q_v, do_v, x_v, wd_v, wq_v, wkv_v, rs_v,
    kwin, vwin, k_t, probs, dscores, own_kv, kv_send, kv_recv,
    down_send, down_recv, down_low, upq_send, upq_recv, upkv_send, upkv_recv,
    g_full, g_send, g_recv, c_full, c_recv, units, z_recv, cz,
    load_sem, win_send, win_recv, down_ss, down_rs, upq_ss, upq_rs, upkv_ss, upkv_rs,
    kv_ss, kv_rs, quad_ss, quad_rs, quadc_ss, quadc_rs, z_ss, z_rs, cz_ss, cz_rs,
    ag_ss, ag_rs, fin_ss, fin_rs, finc_ss, finc_rs,
):
    tokens = q_v.shape[0]
    heads = q_v.shape[1] // HEAD_SIZE
    nz = seq_count // QUAD
    per_owner = UNITS // nz
    s = lax.axis_index("seq")
    hd = lax.axis_index("head")
    zi = s // QUAD
    b = s % QUAD
    core = s % 2
    x_lo = b // 2
    scale = HEAD_SIZE ** -0.5
    multiplier = ADAPTER_SCALE / math.sqrt(tokens * seq_count)

    def seq_at(by):
        return lax.rem(s + by + seq_count, seq_count)

    def head_at(by):
        return lax.rem(hd + by + head_count, head_count)

    def z_at(by):
        return lax.rem(zi + by + nz, nz)

    def quad_at(by):
        return lax.rem(b + by + QUAD, QUAD)

    def z_peer(by):
        return z_at(by) * QUAD + b

    def quad_peer(by):
        return zi * QUAD + quad_at(by)

    pending = []

    loads = [
        pltpu.make_async_copy(src, dst, load_sem.at[i])
        for i, (src, dst) in enumerate([
            (k_hbm, kwin.at[3]), (v_hbm, vwin.at[3]), (x_hbm, x_v), (wd_hbm, wd_v), (q_hbm, q_v),
            (do_hbm, do_v), (rs_hbm, rs_v), (wq_hbm, wq_v), (wkv_hbm, wkv_v),
        ])
    ]
    for copy in loads:
        copy.start()

    barrier = pltpu.get_barrier_semaphore()
    near = [-3, -2, -1, 1, 2, 3]
    for by in near:
        pl.semaphore_signal(barrier, inc=1, device_id={"seq": seq_at(by)}, device_id_type=MESH)
    for by in range(1, head_count):
        pl.semaphore_signal(barrier, inc=1, device_id={"head": head_at(by)}, device_id_type=MESH)

    def greet(by, _):
        pl.semaphore_signal(barrier, inc=1, device_id={"seq": z_peer(by)}, device_id_type=MESH)
        return 0

    lax.fori_loop(1, nz, greet, 0)
    pl.semaphore_wait(barrier, len(near) + head_count - 1 + nz - 1)

    def window_copy(which, by):
        src, dst = ((k_hbm, kwin), (v_hbm, vwin))[which]
        return pltpu.make_async_remote_copy(
            src_ref=src, dst_ref=dst.at[3 - by],
            send_sem=win_send.at[which, by], recv_sem=win_recv.at[which, 3 - by],
            device_id={"seq": seq_at(by)}, device_id_type=MESH,
        )

    for which in range(2):
        window_copy(which, 1).start()
        window_copy(which, 2).start()

        @pl.when(core == 0)
        def _():
            window_copy(which, 3).start()

    def window_sent():
        for which in range(2):
            window_copy(which, 1).wait_send()
            window_copy(which, 2).wait_send()

            @pl.when(core == 0)
            def _():
                window_copy(which, 3).wait_send()

    pending.append(window_sent)

    def head_copy(src, dst, ss, rs, by):
        return pltpu.make_async_remote_copy(
            src_ref=src, dst_ref=dst.at[by], send_sem=ss.at[by], recv_sem=rs.at[by],
            device_id={"head": head_at(by)}, device_id_type=MESH,
        )

    loads[2].wait()
    loads[3].wait()
    down_part = dot_nt(wd_v[...], x_v[...])
    down_send[...] = down_part.astype(BF16)
    for by in range(1, head_count):
        head_copy(down_send, down_recv, down_ss, down_rs, by).start()

    def head_sent(*args):
        def wait():
            for by in range(1, head_count):
                head_copy(*args, by).wait_send()

        pending.append(wait)

    head_sent(down_send, down_recv, down_ss, down_rs)

    for i in (0, 1, 4, 5, 6, 7, 8):
        loads[i].wait()

    row_id = lax.broadcasted_iota(jnp.int32, (tokens, tokens), 0)
    col_id = lax.broadcasted_iota(jnp.int32, (tokens, tokens), 1)
    causal = jnp.where(row_id <= col_id, 0.0, -BIG).astype(F32)
    want = (1 - x_lo).astype(F32)
    even = (1 - core).astype(F32)
    c2 = scale * LOG2E

    def head_cols(ref, h):
        return ref[:, pl.ds(pl.multiple_of(h * HEAD_SIZE, HEAD_SIZE), HEAD_SIZE)]

    def attention(slots):
        def rows(j):
            return pl.ds(j * tokens, tokens)

        for j in slots:
            if j < 3:
                window_copy(0, 3 - j).wait_recv()
            k_t[:, j * tokens : (j + 1) * tokens] = kwin[j].astype(F32).T.astype(BF16)

        def forward(h, _):
            q = head_cols(q_v, h)
            differs = flags[h].astype(F32) - want
            far = differs * differs * BIG
            bias = {0: far, 1: far, 2: far * even, 3: 0.0}
            score = {}
            top = None
            for j in slots:
                score[j] = dot_nt(kwin[j], q)
                if j == 3:
                    score[j] = score[j] + causal
                high = jnp.max(score[j], axis=0, keepdims=True) - bias[j]
                top = high if top is None else jnp.maximum(top, high)
            weight = {}
            total = None
            for j in slots:
                weight[j] = jnp.exp2(score[j] * c2 - (top * c2 + bias[j]))
                part = jnp.sum(weight[j], axis=0, keepdims=True)
                total = part if total is None else total + part
            inverse = 1.0 / total
            for j in slots:
                probs[h, rows(j), :] = (weight[j] * inverse).astype(BF16)
            return 0

        lax.fori_loop(0, heads, forward, 0)

        for j in slots:
            if j < 3:
                window_copy(1, 3 - j).wait_recv()

            def backward(h, acc):
                dk, dv = acc
                q = head_cols(q_v, h)
                do = head_cols(do_v, h)
                p = probs[h, rows(j), :]
                dp = dot_nt(vwin[j], do)
                ds = (p.astype(F32) * (dp - rs_v[pl.ds(h, 1), :])).astype(BF16)
                dscores[h, rows(j), :] = ds
                return dk + dot_nn(ds, q), dv + dot_nn(p, do)

            zero = jnp.zeros((tokens, HEAD_SIZE), F32)
            dk, dv = lax.fori_loop(0, heads, backward, (zero, zero))
            if j == 3:
                own_kv[0] = dk * scale
                own_kv[1] = dv
            else:
                kv_send[j, 0] = (dk * scale).astype(BF16)
                kv_send[j, 1] = dv.astype(BF16)
                grad_copy(3 - j).start()

    def grad_copy(by):
        return pltpu.make_async_remote_copy(
            src_ref=kv_send.at[3 - by], dst_ref=kv_recv.at[by],
            send_sem=kv_ss.at[by], recv_sem=kv_rs.at[by],
            device_id={"seq": seq_at(-by)}, device_id_type=MESH,
        )

    @pl.when(core == 1)
    def _():
        attention((0, 1, 2, 3))

    @pl.when(core == 0)
    def _():
        attention((1, 2, 3))

    def grads_sent():
        grad_copy(1).wait_send()
        grad_copy(2).wait_send()

        @pl.when(core == 1)
        def _():
            grad_copy(3).wait_send()

    pending.append(grads_sent)

    down = down_part
    for by in range(1, head_count):
        head_copy(down_send, down_recv, down_ss, down_rs, by).wait_recv()
        down = down + down_recv[by].astype(F32)
    down_low[...] = down.astype(BF16)

    def query_grads(first):
        def one(h, acc):
            dq = (dot_nn(k_t[:, first:], dscores[h, first:, :]) * scale).astype(BF16)
            a = dot_nt(down_low[:RANK, :], dq)
            g_col = pl.ds(pl.multiple_of((h % 2) * HEAD_SIZE, HEAD_SIZE), HEAD_SIZE)
            g_full[h // 2, 3 * RANK :, g_col] = a
            return acc + dot_nn(head_cols(wq_v, h), dq)

        upq_send_f32 = lax.fori_loop(0, heads, one, jnp.zeros((RANK, tokens), F32))
        upq_send[...] = upq_send_f32.astype(BF16)

    @pl.when(core == 1)
    def _():
        query_grads(0)

    @pl.when(core == 0)
    def _():
        query_grads(tokens)

    for by in range(1, head_count):
        head_copy(upq_send, upq_recv, upq_ss, upq_rs, by).start()
    head_sent(upq_send, upq_recv, upq_ss, upq_rs)

    grad_copy(1).wait_recv()
    grad_copy(2).wait_recv()

    @pl.when(core == 0)
    def _():
        grad_copy(3).wait_recv()
        own_kv[...] = own_kv[...] + kv_recv[3].astype(F32)

    dkv = (own_kv[...] + kv_recv[1].astype(F32) + kv_recv[2].astype(F32)).astype(BF16)
    kv_out[...] = dkv
    for c in range(2):
        upkv_send[c * RANK : (c + 1) * RANK, :] = dot_nt(
            wkv_v[c * RANK : (c + 1) * RANK, :], dkv[c]
        ).astype(BF16)
    for by in range(1, head_count):
        head_copy(upkv_send, upkv_recv, upkv_ss, upkv_rs, by).start()
    head_sent(upkv_send, upkv_recv, upkv_ss, upkv_rs)
    for c in range(2):
        part = dot_nn(down_low[(c + 1) * RANK : (c + 2) * RANK, :], dkv[c])
        c_full[2 * c] = part[:8]
        c_full[2 * c + 1] = part[8:]


    up = upq_send[...].astype(F32)
    for by in range(1, head_count):
        head_copy(upq_send, upq_recv, upq_ss, upq_rs, by).wait_recv()
        up = up + upq_recv[by].astype(F32)
    up_out[:RANK, :] = up.astype(BF16)
    up = upkv_send[...].astype(F32)
    for by in range(1, head_count):
        head_copy(upkv_send, upkv_recv, upkv_ss, upkv_rs, by).wait_recv()
        up = up + upkv_recv[by].astype(F32)
    up_out[RANK:, :] = up.astype(BF16)
    width = x_v.shape[1] // QUAD
    for c in range(QUAD):
        g_full[c, : 3 * RANK, :] = dot_nn(up_out[...], x_v[:, c * width : (c + 1) * width])
    g_send[...] = g_full[...].astype(BF16)


    def quad_copy(by):
        return pltpu.make_async_remote_copy(
            src_ref=g_send.at[quad_at(by)], dst_ref=g_recv.at[by],
            send_sem=quad_ss.at[by], recv_sem=quad_rs.at[by],
            device_id={"seq": quad_peer(by)}, device_id_type=MESH,
        )

    def quad_copy_c(by):
        return pltpu.make_async_remote_copy(
            src_ref=c_full.at[quad_at(by)], dst_ref=c_recv.at[by],
            send_sem=quadc_ss.at[by], recv_sem=quadc_rs.at[by],
            device_id={"seq": quad_peer(by)}, device_id_type=MESH,
        )

    for by in range(1, QUAD):
        quad_copy(by).start()
        quad_copy_c(by).start()

    def quad_sent():
        for by in range(1, QUAD):
            quad_copy(by).wait_send()
            quad_copy_c(by).wait_send()

    pending.append(quad_sent)
    for c in range(QUAD):
        cols = slice(c * width, (c + 1) * width)
        part = lax.dot_general(
            up_out[...], wd_v[:, cols], (((0,), (0,)), ((), ())), preferred_element_type=F32
        )
        x_out[:, cols] = (ADAPTER_SCALE * part).astype(BF16)
    g = g_full[b]
    c_sum = c_full[b]
    for by in range(1, QUAD):
        quad_copy(by).wait_recv()
        quad_copy_c(by).wait_recv()
        g = g + g_recv[by].astype(F32)
        c_sum = c_sum + c_recv[by]
    for u in range(UNITS):
        r, col = u // 2, u % 2
        units[u // per_owner, u % per_owner] = g[r * 8 : r * 8 + 8, col * 128 : col * 128 + 128]
    cz[zi] = c_sum


    def z_copy(by):
        return pltpu.make_async_remote_copy(
            src_ref=units.at[z_at(by)], dst_ref=z_recv.at[by],
            send_sem=z_ss.at[by], recv_sem=z_rs.at[by],
            device_id={"seq": z_peer(by)}, device_id_type=MESH,
        )

    def cz_copy(by, slot):
        return pltpu.make_async_remote_copy(
            src_ref=cz.at[slot], dst_ref=cz.at[slot],
            send_sem=cz_ss.at[by], recv_sem=cz_rs.at[slot],
            device_id={"seq": z_peer(by)}, device_id_type=MESH,
        )

    def send_z(by, _):
        z_copy(by).start()
        return 0

    def send_cz(by, _):
        cz_copy(by, zi).start()
        return 0

    lax.fori_loop(1, nz, send_z, 0)
    lax.fori_loop(1, nz, send_cz, 0)

    def wait_z(by, _):
        z_copy(by).wait_send()
        cz_copy(by, zi).wait_send()
        return 0

    pending.append(lambda: lax.fori_loop(1, nz, wait_z, 0))

    def add_z(by, acc):
        z_copy(by).wait_recv()
        return acc + z_recv[by]

    total = lax.fori_loop(1, nz, add_z, units[zi]) * multiplier


    def unit_slice(u, quad):
        return (
            pl.ds(pl.multiple_of((u // 2) * 8, 8), 8),
            pl.ds(pl.multiple_of(quad * width + (u % 2) * 128, 128), 128),
        )

    for i in range(per_owner):
        at = unit_slice(zi * per_owner + i, b)
        g_out[at[0], at[1]] = total[i]

    def gather_copy(by, owner, i):
        u = owner * per_owner + i
        at = unit_slice(u, b)
        return pltpu.make_async_remote_copy(
            src_ref=g_out.at[at[0], at[1]], dst_ref=g_out.at[at[0], at[1]],
            send_sem=ag_ss.at[by * per_owner + i], recv_sem=ag_rs.at[u],
            device_id={"seq": z_peer(by)}, device_id_type=MESH,
        )

    def send_gather(by, _):
        for i in range(per_owner):
            gather_copy(by, zi, i).start()
        return 0

    lax.fori_loop(1, nz, send_gather, 0)

    def wait_gather_sent(by, _):
        for i in range(per_owner):
            gather_copy(by, zi, i).wait_send()
        return 0

    pending.append(lambda: lax.fori_loop(1, nz, wait_gather_sent, 0))

    def wait_cz(by, _):
        cz_copy(by, z_at(-by)).wait_recv()
        return 0

    lax.fori_loop(1, nz, wait_cz, 0)
    c_total = jnp.sum(cz[...], axis=0) * multiplier
    c_at = pl.ds(pl.multiple_of(b * 8, 8), 8)
    c_out[c_at, :] = c_total

    def wait_gather(by, _):
        for i in range(per_owner):
            gather_copy(by, z_at(-by), i).wait_recv()
        return 0

    lax.fori_loop(1, nz, wait_gather, 0)


    def final_copy(by, quad):
        cols = pl.ds(pl.multiple_of(quad * width, 128), width)
        return pltpu.make_async_remote_copy(
            src_ref=g_out.at[:, cols], dst_ref=g_out.at[:, cols],
            send_sem=fin_ss.at[by], recv_sem=fin_rs.at[by],
            device_id={"seq": quad_peer(by)}, device_id_type=MESH,
        )

    def final_copy_c(by, quad):
        at = pl.ds(pl.multiple_of(quad * 8, 8), 8)
        return pltpu.make_async_remote_copy(
            src_ref=c_out.at[at, :], dst_ref=c_out.at[at, :],
            send_sem=finc_ss.at[by], recv_sem=finc_rs.at[by],
            device_id={"seq": quad_peer(by)}, device_id_type=MESH,
        )

    for by in range(1, QUAD):
        final_copy(by, b).start()
        final_copy_c(by, b).start()

    for by in range(1, QUAD):
        final_copy(by, quad_at(-by)).wait_recv()
        final_copy_c(by, quad_at(-by)).wait_recv()
        final_copy(by, b).wait_send()
        final_copy_c(by, b).wait_send()

    for wait in pending:
        wait()


def place(
    kv, x, g, c, down_o, up_q_o, up_kv_o, kv_o, x_o, kv_v, x_v, g_v, c_v, in_sems, out_sems
):
    ways = [
        (x, x_v, [(x_v, x_o)]),
        (g, g_v, [(g_v.at[: 3 * RANK], down_o), (g_v.at[3 * RANK :], up_q_o)]),
        (kv, kv_v, [(kv_v, kv_o)]),
        (c, c_v, [(c_v, up_kv_o)]),
    ]
    arriving = [
        pltpu.make_async_copy(src, dst, in_sems.at[i]) for i, (src, dst, _) in enumerate(ways)
    ]
    for copy in arriving:
        copy.start()
    leaving = []
    for copy, (_, _, targets) in zip(arriving, ways):
        copy.wait()
        for src, dst in targets:
            leaving.append(pltpu.make_async_copy(src, dst, out_sems.at[len(leaving)]))
            leaving[-1].start()
    for copy in leaving:
        copy.wait()


def per_device(
    queries, layer_key_rows, layer_value_rows, output_gradient, output_row_sums,
    shifted_head_flags, inputs, adapter_down_weight, query_up_weight, key_value_up_weight,
):
    seq_count = lax.axis_size("seq")
    head_count = lax.axis_size("head")
    tokens, columns = queries.shape
    heads = columns // HEAD_SIZE
    width = inputs.shape[1]
    nz = seq_count // QUAD
    per_owner = UNITS // nz
    flat_down = adapter_down_weight.reshape(3 * RANK, width)
    flat_kv_up = key_value_up_weight.reshape(2 * RANK, HEAD_SIZE)
    vmem = pltpu.VMEM
    sem = pltpu.SemaphoreType.DMA
    anywhere = pl.BlockSpec(memory_space=pltpu.HBM)
    in_vmem = pl.BlockSpec(memory_space=pltpu.VMEM)
    parts = pl.pallas_call(
        functools.partial(kernel, seq_count, head_count),
        out_shape=(
            jax.ShapeDtypeStruct((2, tokens, HEAD_SIZE), BF16),
            jax.ShapeDtypeStruct((tokens, width), BF16),
            jax.ShapeDtypeStruct((4 * RANK, width), F32),
            jax.ShapeDtypeStruct((2 * RANK, HEAD_SIZE), F32),
        ),
        in_specs=[anywhere] * 5 + [pl.BlockSpec(memory_space=pltpu.SMEM)] + [anywhere] * 4,
        out_specs=(in_vmem,) * 4,
        scratch_shapes=[
            vmem((3 * RANK, tokens), BF16),
            vmem((tokens, columns), BF16),
            vmem((tokens, columns), BF16),
            vmem((tokens, width), BF16),
            vmem((3 * RANK, width), BF16),
            vmem((RANK, columns), BF16),
            vmem((2 * RANK, HEAD_SIZE), BF16),
            vmem((heads, tokens), F32),
            vmem((4, tokens, HEAD_SIZE), BF16),
            vmem((4, tokens, HEAD_SIZE), BF16),
            vmem((HEAD_SIZE, 4 * tokens), BF16),
            vmem((heads, 4 * tokens, tokens), BF16),
            vmem((heads, 4 * tokens, tokens), BF16),
            vmem((2, tokens, HEAD_SIZE), F32),
            vmem((3, 2, tokens, HEAD_SIZE), BF16),
            vmem((4, 2, tokens, HEAD_SIZE), BF16),
            vmem((3 * RANK, tokens), BF16),
            vmem((head_count, 3 * RANK, tokens), BF16),
            vmem((3 * RANK, tokens), BF16),
            vmem((RANK, tokens), BF16),
            vmem((head_count, RANK, tokens), BF16),
            vmem((2 * RANK, tokens), BF16),
            vmem((head_count, 2 * RANK, tokens), BF16),
            vmem((QUAD, 4 * RANK, width // QUAD), F32),
            vmem((QUAD, 4 * RANK, width // QUAD), BF16),
            vmem((QUAD, 4 * RANK, width // QUAD), BF16),
            vmem((QUAD, 8, HEAD_SIZE), F32),
            vmem((QUAD, 8, HEAD_SIZE), F32),
            vmem((nz, per_owner, 8, 128), F32),
            vmem((nz, per_owner, 8, 128), F32),
            vmem((nz, 8, HEAD_SIZE), F32),
            sem((9,)),
            sem((2, 4)), sem((2, 4)),
            sem((head_count,)), sem((head_count,)),
            sem((head_count,)), sem((head_count,)),
            sem((head_count,)), sem((head_count,)),
            sem((4,)), sem((4,)),
            sem((QUAD,)), sem((QUAD,)),
            sem((QUAD,)), sem((QUAD,)),
            sem((nz,)), sem((nz,)),
            sem((nz,)), sem((nz,)),
            sem((UNITS,)), sem((UNITS,)),
            sem((QUAD,)), sem((QUAD,)),
            sem((QUAD,)), sem((QUAD,)),
        ],
        compiler_params=pltpu.CompilerParams(
            collective_id=0, has_side_effects=True, vmem_limit_bytes=VMEM_BYTES
        ),
    )(
        queries, layer_key_rows, layer_value_rows, output_gradient, output_row_sums,
        shifted_head_flags, inputs, flat_down, query_up_weight, flat_kv_up,
    )
    down_gradient, grad_up_q, grad_up_kv, kv_gradient, grad_inputs = pl.pallas_call(
        place,
        out_shape=(
            jax.ShapeDtypeStruct((3 * RANK, width), F32),
            jax.ShapeDtypeStruct((RANK, columns), F32),
            jax.ShapeDtypeStruct((2 * RANK, HEAD_SIZE), F32),
            jax.ShapeDtypeStruct((2, tokens, HEAD_SIZE), BF16),
            jax.ShapeDtypeStruct((tokens, width), BF16),
        ),
        in_specs=[anywhere] * 4,
        out_specs=(anywhere,) * 5,
        scratch_shapes=[
            vmem((2, tokens, HEAD_SIZE), BF16),
            vmem((tokens, width), BF16),
            vmem((4 * RANK, width), F32),
            vmem((2 * RANK, HEAD_SIZE), F32),
            sem((4,)),
            sem((5,)),
        ],
        compiler_params=pltpu.CompilerParams(vmem_limit_bytes=VMEM_BYTES),
    )(*parts)
    return (
        grad_inputs,
        kv_gradient,
        down_gradient.reshape(3, RANK, width),
        grad_up_q,
        grad_up_kv.reshape(2, RANK, HEAD_SIZE),
    )


def solution(mesh):
    placed = (
        P("seq", "head"),
        P("seq", "head"),
        P("seq", "head"),
        P("seq", "head"),
        P("head", "seq"),
        P("head"),
        P("seq", "head"),
        P(None, None, "head"),
        P(None, "head"),
        P(None, None, "head"),
    )
    return jax.shard_map(
        per_device,
        mesh=mesh,
        in_specs=placed,
        out_specs=(
            P("seq", "head"),
            P(None, "seq", "head"),
            P(None, None, "head"),
            P(None, "head"),
            P(None, None, "head"),
        ),
        check_vma=False,
    )
```

```python
import functools
import math

import jax
import jax.numpy as jnp
from jax import lax
from jax.experimental import pallas as pl
from jax.experimental.pallas import tpu as pltpu
from jax.sharding import PartitionSpec as P

HEAD_SIZE = 128
GROUP = 1024
RANK = 16
QUAD = 4
UNITS = 16
LOG2E = 1.4426950408889634
BIG = 1e30
ADAPTER_SCALE = 2.0
VMEM_BYTES = 63 * 1024 * 1024

MESH = pl.DeviceIdType.MESH
F32 = jnp.float32
BF16 = jnp.bfloat16


def dot_nn(a, b):
    return lax.dot_general(a, b, (((1,), (0,)), ((), ())), preferred_element_type=F32)


def dot_nt(a, b):
    return lax.dot_general(a, b, (((1,), (1,)), ((), ())), preferred_element_type=F32)


def kernel(
    seq_count,
    head_count,
    q_hbm, k_hbm, v_hbm, do_hbm, rs_hbm, flags, x_hbm, wd_hbm, wq_hbm, wkv_hbm,
    kv_out, x_out, g_out, c_out,
    up_out, q_v, do_v, x_v, wd_v, wq_v, wkv_v, rs_v,
    kwin, vwin, k_t, scores, tops, probs, dscores, own_kv, kv_send, kv_recv, relay,
    down_send, down_recv, down_low, upq_send, upq_recv, upkv_send, upkv_recv,
    g_full, g_pair, c_full, c_pair, units, slots, c_sum, c_slots,
    load_sem, win_ss, win_rs, down_ss, down_rs, upq_ss, upq_rs, upkv_ss, upkv_rs,
    relay_ss, relay_rs, kv_ss, kv_rs, pair_ss, pair_rs, rs_ss, rs_rs, c_ss, c_rs,
    ag_ss, ag_rs, cag_ss, cag_rs, fin_ss, fin_rs, known,
):
    tokens = q_v.shape[0]
    heads = q_v.shape[1] // HEAD_SIZE
    nz = seq_count // QUAD
    per_owner = UNITS // nz
    half = x_v.shape[1] // 2
    s = lax.axis_index("seq")
    hd = lax.axis_index("head")
    zi = s // QUAD
    core = s % 2
    x_lo = (s % QUAD) // 2
    sibling = s + 1 - 2 * core
    scale = HEAD_SIZE ** -0.5
    multiplier = ADAPTER_SCALE / math.sqrt(tokens * seq_count)
    pending = []

    def seq_at(by):
        return lax.rem(s + by + seq_count, seq_count)

    def head_at(by):
        return lax.rem(hd + by + head_count, head_count)

    def z_at(by):
        return lax.rem(zi + by + nz, nz)

    def chip(by, x):
        return z_at(by) * QUAD + x * 2 + core

    def remote(src, dst, ss, rs, target):
        return pltpu.make_async_remote_copy(
            src_ref=src, dst_ref=dst, send_sem=ss, recv_sem=rs,
            device_id={"seq": target}, device_id_type=MESH,
        )

    loads = [
        pltpu.make_async_copy(src, dst, load_sem.at[i])
        for i, (src, dst) in enumerate([
            (k_hbm, kwin.at[3]), (q_hbm, q_v), (x_hbm, x_v), (wd_hbm, wd_v), (v_hbm, vwin.at[3]),
            (do_hbm, do_v), (rs_hbm, rs_v), (wq_hbm, wq_v), (wkv_hbm, wkv_v),
        ])
    ]
    for copy in loads:
        copy.start()

    barrier = pltpu.get_barrier_semaphore()
    near = [sibling, seq_at(2), seq_at(-2), seq_at(4), seq_at(-4)]
    for target in near:
        pl.semaphore_signal(barrier, inc=1, device_id={"seq": target}, device_id_type=MESH)
    for by in range(1, head_count):
        pl.semaphore_signal(barrier, inc=1, device_id={"head": head_at(by)}, device_id_type=MESH)
    pl.semaphore_wait(barrier, len(near) + head_count - 1)

    rounds = []
    step = 2
    while step < nz:
        rounds.append(step)
        step *= 2

    def tell(i):
        if i < len(rounds):
            for by in (2 * rounds[i], -2 * rounds[i]):
                pl.semaphore_signal(
                    known.at[i], inc=1, device_id={"seq": seq_at(by)}, device_id_type=MESH
                )

    def hear(i):
        if i < len(rounds):
            pl.semaphore_wait(known.at[i], 2)

    own = (k_hbm, v_hbm)
    win = (kwin, vwin)

    def cross(c):
        return remote(own[c], win[c].at[1], win_ss.at[c, 0], win_rs.at[c, 1], seq_at(2))

    def give(c):
        return remote(own[c], win[c].at[2], win_ss.at[c, 1], win_rs.at[c, 2], sibling)

    def forward(c, slot):
        return remote(win[c].at[1], win[c].at[slot], win_ss.at[c, 2], win_rs.at[c, slot], sibling)

    for c in range(2):
        cross(c).start()

        @pl.when(core == 0)
        def _():
            give(c).start()

    tell(0)

    def head_copy(src, dst, ss, rs, by):
        return pltpu.make_async_remote_copy(
            src_ref=src, dst_ref=dst.at[by], send_sem=ss.at[by], recv_sem=rs.at[by],
            device_id={"head": head_at(by)}, device_id_type=MESH,
        )

    def head_start(*args):
        for by in range(1, head_count):
            head_copy(*args, by).start()

        def wait():
            for by in range(1, head_count):
                head_copy(*args, by).wait_send()

        pending.append(wait)

    row_id = lax.broadcasted_iota(jnp.int32, (tokens, tokens), 0)
    col_id = lax.broadcasted_iota(jnp.int32, (tokens, tokens), 1)
    causal = jnp.where(row_id <= col_id, 0.0, -BIG).astype(F32)
    want = (1 - x_lo).astype(F32)
    even = (1 - core).astype(F32)
    c2 = scale * LOG2E

    def head_cols(ref, h):
        return ref[:, pl.ds(pl.multiple_of(h * HEAD_SIZE, HEAD_SIZE), HEAD_SIZE)]

    def rows(j):
        return pl.ds(j * tokens, tokens)

    def over_heads(body, at_once=2):
        def some(i, _):
            for k in range(at_once):
                body(i * at_once + k)
            return 0

        lax.fori_loop(0, heads // at_once, some, 0)

    def score_block(j):
        def one(h):
            score = dot_nt(kwin[j], head_cols(q_v, h))
            if j == 3:
                score = score + causal
            scores[h, rows(j), :] = score
            tops[j, pl.ds(h, 1), :] = jnp.max(score, axis=0, keepdims=True)

        over_heads(one)
        k_t[:, j * tokens : (j + 1) * tokens] = kwin[j].astype(F32).T.astype(BF16)

    loads[0].wait()
    loads[1].wait()
    score_block(3)
    loads[2].wait()
    loads[3].wait()
    down_part = dot_nt(wd_v[...], x_v[...])
    down_send[...] = down_part.astype(BF16)
    hear(0)
    tell(1)

    def rest_of_scores(odd):
        if odd:
            give(0).wait_recv()
            score_block(2)
            cross(0).wait_recv()
            forward(0, 2).start()
            score_block(1)
            forward(0, 0).wait_recv()
            score_block(0)
        else:
            cross(0).wait_recv()
            forward(0, 0).start()
            score_block(1)
            forward(0, 2).wait_recv()
            score_block(2)

    def pass_values_on(odd):
        cross(1).wait_recv()
        forward(1, 2 if odd else 0).start()

    def relay_copy(slot):
        return remote(kv_send.at[slot], relay, relay_ss, relay_rs, sibling)

    def back_copy():
        return remote(kv_send.at[1], kv_recv.at[0], kv_ss.at[0], kv_rs.at[0], seq_at(-2))

    def home_copy():
        return remote(kv_send.at[2], kv_recv.at[1], kv_ss.at[1], kv_rs.at[1], sibling)

    def attention(odd):
        order = (0, 1, 2, 3) if odd else (2, 1, 3)

        def weights(h):
            differs = flags[h].astype(F32) - want
            far = differs * differs * BIG
            bias = {0: far, 1: far, 2: 0.0 if odd else far, 3: 0.0}
            at = pl.ds(h, 1)
            top = None
            for j in order:
                high = tops[j, at, :] - bias[j]
                top = high if top is None else jnp.maximum(top, high)
            weight = {}
            total = None
            for j in order:
                weight[j] = jnp.exp2(scores[h, rows(j), :] * c2 - (top * c2 + bias[j]))
                part = jnp.sum(weight[j], axis=0, keepdims=True)
                total = part if total is None else total + part
            inverse = 1.0 / total
            for j in order:
                probs[h, rows(j), :] = (weight[j] * inverse).astype(BF16)

        over_heads(weights, 1)

        if odd:
            give(1).wait_recv()
            forward(1, 0).wait_recv()
        else:
            forward(1, 2).wait_recv()
        for j in order:

            def backward(i, acc):
                dk, dv = acc
                for k in range(2):
                    h = i * 2 + k
                    q = head_cols(q_v, h)
                    do = head_cols(do_v, h)
                    p = probs[h, rows(j), :]
                    dp = dot_nt(vwin[j], do)
                    ds = (p.astype(F32) * (dp - rs_v[pl.ds(h, 1), :])).astype(BF16)
                    dscores[h, rows(j), :] = ds
                    dk = dk + dot_nn(ds, q)
                    dv = dv + dot_nn(p, do)
                return dk, dv

            zero = jnp.zeros((tokens, HEAD_SIZE), F32)
            dk, dv = lax.fori_loop(0, heads // 2, backward, (zero, zero))
            dk = dk * scale
            if j == 3:
                own_kv[0] = dk
                own_kv[1] = dv
            elif j == 1:
                relay_copy(2).wait_recv()
                kv_send[1, 0] = (dk + relay[0].astype(F32)).astype(BF16)
                kv_send[1, 1] = (dv + relay[1].astype(F32)).astype(BF16)
                back_copy().start()
            else:
                kv_send[j, 0] = dk.astype(BF16)
                kv_send[j, 1] = dv.astype(BF16)
                if j == 0 or not odd:
                    relay_copy(j).start()
                else:
                    home_copy().start()

    def split(fn):
        @pl.when(core == 1)
        def _():
            fn(True)

        @pl.when(core == 0)
        def _():
            fn(False)

    split(rest_of_scores)
    head_start(down_send, down_recv, down_ss, down_rs)
    hear(1)
    tell(2)
    for i in range(4, 9):
        loads[i].wait()
    split(pass_values_on)

    def window_sent(odd):
        for c in range(2):
            cross(c).wait_send()
            forward(c, 2 if odd else 0).wait_send()
            if not odd:
                give(c).wait_send()

    pending.append(lambda: split(window_sent))
    split(attention)

    def grads_sent(odd):
        relay_copy(0 if odd else 2).wait_send()
        back_copy().wait_send()
        if odd:
            home_copy().wait_send()

    pending.append(lambda: split(grads_sent))

    down = down_part
    for by in range(1, head_count):
        head_copy(down_send, down_recv, down_ss, down_rs, by).wait_recv()
        down = down + down_recv[by].astype(F32)
    down_low[...] = down.astype(BF16)

    def query_grads(odd):
        first = 0 if odd else tokens
        per_half = heads // 2

        def one(i, acc):
            for k in range(2):
                h = i * 2 + k
                dq = (dot_nn(k_t[:, first:], dscores[h, first:, :]) * scale).astype(BF16)
                cols = pl.ds(pl.multiple_of((h % per_half) * HEAD_SIZE, HEAD_SIZE), HEAD_SIZE)
                g_full[h // per_half, :RANK, cols] = dot_nt(down_low[:RANK, :], dq)
                acc = acc + dot_nn(head_cols(wq_v, h), dq)
            return acc

        acc = lax.fori_loop(0, heads // 2, one, jnp.zeros((RANK, tokens), F32))
        upq_send[...] = acc.astype(BF16)

    split(query_grads)
    head_start(upq_send, upq_recv, upq_ss, upq_rs)
    hear(2)

    back_copy().wait_recv()

    @pl.when(core == 0)
    def _():
        home_copy().wait_recv()
        own_kv[...] = own_kv[...] + kv_recv[1].astype(F32)

    dkv = (own_kv[...] + kv_recv[0].astype(F32)).astype(BF16)
    kv_out[...] = dkv
    for c in range(2):
        upkv_send[c * RANK : (c + 1) * RANK, :] = dot_nt(
            wkv_v[c * RANK : (c + 1) * RANK, :], dkv[c]
        ).astype(BF16)
    head_start(upkv_send, upkv_recv, upkv_ss, upkv_rs)
    for c in range(2):
        c_full[c] = dot_nn(down_low[(c + 1) * RANK : (c + 2) * RANK, :], dkv[c])

    part_rows = 2 * RANK

    def pair_copy(p):
        at = pl.ds(p * part_rows, part_rows)
        return remote(
            g_full.at[1 - core, at], g_pair.at[at], pair_ss.at[p], pair_rs.at[p], sibling
        )

    def pair_copy_c():
        return remote(c_full.at[1 - core], c_pair, pair_ss.at[2], pair_rs.at[2], sibling)

    pair_copy_c().start()
    pending.append(lambda: pair_copy_c().wait_send())

    def head_total(send, recv, ss, rs):
        total = send[...].astype(F32)
        for by in range(1, head_count):
            head_copy(send, recv, ss, rs, by).wait_recv()
            total = total + recv[by].astype(F32)
        return total.astype(BF16)

    def down_rows(first, last):
        for c in range(2):
            g_full[c, RANK + first : RANK + last, :] = dot_nn(
                up_out[first:last, :], x_v[:, c * half : (c + 1) * half]
            )

    def far_first(i):
        return nz // 2 + lax.rem(i + 1, 2) * (i // 2) - lax.rem(i, 2) * ((i + 1) // 2)

    def scatter_copy(p, by, x):
        slot = x * nz + by
        return remote(
            units.at[p, z_at(by)], slots.at[slot], rs_ss.at[p, by], rs_rs.at[slot], chip(by, p)
        )

    def loop(first, last, fn):
        def body(i, _):
            fn(i)
            return 0

        lax.fori_loop(first, last, body, 0)

    def at_x(p, fn):
        @pl.when(x_lo == p)
        def _():
            fn(nz - 1)

        @pl.when(x_lo != p)
        def _():
            fn(nz)

    def scatter(p):
        pair_copy(p).wait_recv()
        at = pl.ds(p * part_rows, part_rows)
        g = g_full[core, at, :] + g_pair[at, :]
        for u in range(UNITS):
            r, col = (u // 4) * 8, (u % 4) * 128
            units[p, u // per_owner, u % per_owner] = g[r : r + 8, col : col + 128]
        at_x(p, lambda n: loop(0, n, lambda i: scatter_copy(p, far_first(i), x_lo).start()))
        pending.append(
            lambda: at_x(
                p, lambda n: loop(0, n, lambda i: scatter_copy(p, far_first(i), x_lo).wait_send())
            )
        )

    up_out[:RANK, :] = head_total(upq_send, upq_recv, upq_ss, upq_rs)
    down_rows(0, RANK)
    pair_copy(0).start()
    pending.append(lambda: pair_copy(0).wait_send())
    scatter(0)

    c_owner = (nz // 2) * QUAD + 2 + core
    is_c_owner = s == c_owner

    def c_copy(slot):
        return remote(c_sum, c_slots.at[slot], c_ss, c_rs.at[slot], c_owner)

    pair_copy_c().wait_recv()
    c_sum[...] = c_full[core] + c_pair[...]

    @pl.when(jnp.logical_not(is_c_owner))
    def _():
        c_copy(x_lo * nz + zi).start()

    def c_sent():
        @pl.when(jnp.logical_not(is_c_owner))
        def _():
            c_copy(x_lo * nz + zi).wait_send()

    pending.append(c_sent)

    up_out[RANK:, :] = head_total(upkv_send, upkv_recv, upkv_ss, upkv_rs)
    down_rows(RANK, 3 * RANK)
    pair_copy(1).start()
    pending.append(lambda: pair_copy(1).wait_send())
    scatter(1)

    for c in range(4):
        cols = slice(c * half // 2, (c + 1) * half // 2)
        part = lax.dot_general(
            up_out[...], wd_v[:, cols], (((0,), (0,)), ((), ())), preferred_element_type=F32
        )
        x_out[:, cols] = (ADAPTER_SCALE * part).astype(BF16)

    def unit_ref(p, u):
        return g_out.at[
            pl.ds(pl.multiple_of(p * part_rows + (u // 4) * 8, 8), 8),
            pl.ds(pl.multiple_of(core * half + (u % 4) * 128, 128), 128),
        ]

    def gather_copy(p, owner, i, by, x):
        u = owner * per_owner + i
        ref = unit_ref(p, u)
        return remote(
            ref, ref, ag_ss.at[(x * nz + by) * per_owner + i], ag_rs.at[p, u], chip(by, x)
        )

    def each_target(p, fn):
        loop(0, nz - 1, lambda i: (fn(far_first(i), 0), fn(far_first(i), 1)))
        fn(0, 1 - p)

    def gather(p):
        @pl.when(x_lo == p)
        def _():
            total = units[p, zi]
            for by in range(0, nz):
                for x in (p, 1 - p):
                    if by == 0 and x == p:
                        continue
                    scatter_copy(p, by, x).wait_recv()
                    total = total + slots[x * nz + by]
            total = total * multiplier
            for i in range(per_owner):
                unit_ref(p, zi * per_owner + i)[...] = total[i]

            def start(by, x):
                for i in range(per_owner):
                    gather_copy(p, zi, i, by, x).start()

            each_target(p, start)

    def gather_sent():
        for p in range(2):

            @pl.when(x_lo == p)
            def _():
                def wait(by, x):
                    for i in range(per_owner):
                        gather_copy(p, zi, i, by, x).wait_send()

                each_target(p, wait)

    def c_ref():
        return c_out.at[pl.ds(pl.multiple_of(core * RANK, RANK), RANK), :]

    def c_gather_copy(by, x):
        return remote(c_ref(), c_ref(), cag_ss.at[x * nz + by], cag_rs, chip(by, x))

    gather(0)

    @pl.when(is_c_owner)
    def _():
        total = c_sum[...]
        for by in range(0, nz):
            for x in (1, 0):
                if by == 0 and x == 1:
                    continue
                slot = x * nz + z_at(by)
                c_copy(slot).wait_recv()
                total = total + c_slots[slot]
        c_out[pl.ds(pl.multiple_of(core * RANK, RANK), RANK), :] = total * multiplier
        each_target(1, lambda by, x: c_gather_copy(by, x).start())

    def c_gather_sent():
        @pl.when(is_c_owner)
        def _():
            each_target(1, lambda by, x: c_gather_copy(by, x).wait_send())

    gather(1)
    pending.append(gather_sent)
    pending.append(c_gather_sent)

    def wait_gathered(p):
        def wait(by):
            for i in range(per_owner):
                gather_copy(p, z_at(by), i, by, 0).wait_recv()

        loop(1, nz, wait)

        @pl.when(x_lo != p)
        def _():
            wait(0)

    def final_copy(p, side):
        ref = g_out.at[
            pl.ds(p * part_rows, part_rows), pl.ds(pl.multiple_of(side * half, 128), half)
        ]
        return remote(ref, ref, fin_ss.at[p], fin_rs.at[p], sibling)

    def final_copy_c(side):
        ref = c_out.at[pl.ds(pl.multiple_of(side * RANK, RANK), RANK), :]
        return remote(ref, ref, fin_ss.at[2], fin_rs.at[2], sibling)

    wait_gathered(0)
    final_copy(0, core).start()

    @pl.when(jnp.logical_not(is_c_owner))
    def _():
        c_gather_copy(0, 0).wait_recv()

    final_copy_c(core).start()
    wait_gathered(1)
    final_copy(1, core).start()

    for wait in pending:
        wait()
    final_copy_c(1 - core).wait_recv()
    final_copy_c(core).wait_send()
    for p in range(2):
        final_copy(p, 1 - core).wait_recv()
        final_copy(p, core).wait_send()


def place(
    kv, x, g, c, down_o, up_q_o, up_kv_o, kv_o, x_o, kv_v, x_v, g_v, c_v, in_sems, out_sems
):
    ways = [
        (x, x_v, [(x_v, x_o)]),
        (g, g_v, [(g_v.at[RANK:], down_o), (g_v.at[:RANK], up_q_o)]),
        (kv, kv_v, [(kv_v, kv_o)]),
        (c, c_v, [(c_v, up_kv_o)]),
    ]
    arriving = [
        pltpu.make_async_copy(src, dst, in_sems.at[i]) for i, (src, dst, _) in enumerate(ways)
    ]
    for copy in arriving:
        copy.start()
    leaving = []
    for copy, (_, _, targets) in zip(arriving, ways):
        copy.wait()
        for src, dst in targets:
            leaving.append(pltpu.make_async_copy(src, dst, out_sems.at[len(leaving)]))
            leaving[-1].start()
    for copy in leaving:
        copy.wait()


def per_device(
    queries, layer_key_rows, layer_value_rows, output_gradient, output_row_sums,
    shifted_head_flags, inputs, adapter_down_weight, query_up_weight, key_value_up_weight,
):
    seq_count = lax.axis_size("seq")
    head_count = lax.axis_size("head")
    tokens, columns = queries.shape
    heads = columns // HEAD_SIZE
    width = inputs.shape[1]
    nz = seq_count // QUAD
    per_owner = UNITS // nz
    flat_down = adapter_down_weight.reshape(3 * RANK, width)
    flat_kv_up = key_value_up_weight.reshape(2 * RANK, HEAD_SIZE)
    vmem = pltpu.VMEM
    sem = pltpu.SemaphoreType.DMA
    anywhere = pl.BlockSpec(memory_space=pltpu.HBM)
    in_vmem = pl.BlockSpec(memory_space=pltpu.VMEM)
    parts = pl.pallas_call(
        functools.partial(kernel, seq_count, head_count),
        out_shape=(
            jax.ShapeDtypeStruct((2, tokens, HEAD_SIZE), BF16),
            jax.ShapeDtypeStruct((tokens, width), BF16),
            jax.ShapeDtypeStruct((4 * RANK, width), F32),
            jax.ShapeDtypeStruct((2 * RANK, HEAD_SIZE), F32),
        ),
        in_specs=[anywhere] * 5 + [pl.BlockSpec(memory_space=pltpu.SMEM)] + [anywhere] * 4,
        out_specs=(in_vmem,) * 4,
        scratch_shapes=[
            vmem((3 * RANK, tokens), BF16),
            vmem((tokens, columns), BF16),
            vmem((tokens, columns), BF16),
            vmem((tokens, width), BF16),
            vmem((3 * RANK, width), BF16),
            vmem((RANK, columns), BF16),
            vmem((2 * RANK, HEAD_SIZE), BF16),
            vmem((heads, tokens), F32),
            vmem((4, tokens, HEAD_SIZE), BF16),
            vmem((4, tokens, HEAD_SIZE), BF16),
            vmem((HEAD_SIZE, 4 * tokens), BF16),
            vmem((heads, 4 * tokens, tokens), F32),
            vmem((4, heads, tokens), F32),
            vmem((heads, 4 * tokens, tokens), BF16),
            vmem((heads, 4 * tokens, tokens), BF16),
            vmem((2, tokens, HEAD_SIZE), F32),
            vmem((3, 2, tokens, HEAD_SIZE), BF16),
            vmem((2, 2, tokens, HEAD_SIZE), BF16),
            vmem((2, tokens, HEAD_SIZE), BF16),
            vmem((3 * RANK, tokens), BF16),
            vmem((head_count, 3 * RANK, tokens), BF16),
            vmem((3 * RANK, tokens), BF16),
            vmem((RANK, tokens), BF16),
            vmem((head_count, RANK, tokens), BF16),
            vmem((2 * RANK, tokens), BF16),
            vmem((head_count, 2 * RANK, tokens), BF16),
            vmem((2, 4 * RANK, width // 2), F32),
            vmem((4 * RANK, width // 2), F32),
            vmem((2, RANK, HEAD_SIZE), F32),
            vmem((RANK, HEAD_SIZE), F32),
            vmem((2, nz, per_owner, 8, 128), F32),
            vmem((2 * nz, per_owner, 8, 128), F32),
            vmem((RANK, HEAD_SIZE), F32),
            vmem((2 * nz, RANK, HEAD_SIZE), F32),
            sem((9,)),
            sem((2, 3)), sem((2, 4)),
            sem((head_count,)), sem((head_count,)),
            sem((head_count,)), sem((head_count,)),
            sem((head_count,)), sem((head_count,)),
            sem, sem,
            sem((2,)), sem((2,)),
            sem((3,)), sem((3,)),
            sem((2, nz)), sem((2 * nz,)),
            sem, sem((2 * nz,)),
            sem((2 * nz * per_owner,)), sem((2, UNITS)),
            sem((2 * nz,)), sem,
            sem((3,)), sem((3,)),
            pltpu.SemaphoreType.REGULAR((3,)),
        ],
        compiler_params=pltpu.CompilerParams(
            collective_id=0, has_side_effects=True, vmem_limit_bytes=VMEM_BYTES
        ),
    )(
        queries, layer_key_rows, layer_value_rows, output_gradient, output_row_sums,
        shifted_head_flags, inputs, flat_down, query_up_weight, flat_kv_up,
    )
    down_gradient, grad_up_q, grad_up_kv, kv_gradient, grad_inputs = pl.pallas_call(
        place,
        out_shape=(
            jax.ShapeDtypeStruct((3 * RANK, width), F32),
            jax.ShapeDtypeStruct((RANK, columns), F32),
            jax.ShapeDtypeStruct((2 * RANK, HEAD_SIZE), F32),
            jax.ShapeDtypeStruct((2, tokens, HEAD_SIZE), BF16),
            jax.ShapeDtypeStruct((tokens, width), BF16),
        ),
        in_specs=[anywhere] * 4,
        out_specs=(anywhere,) * 5,
        scratch_shapes=[
            vmem((2, tokens, HEAD_SIZE), BF16),
            vmem((tokens, width), BF16),
            vmem((4 * RANK, width), F32),
            vmem((2 * RANK, HEAD_SIZE), F32),
            sem((4,)),
            sem((5,)),
        ],
        compiler_params=pltpu.CompilerParams(vmem_limit_bytes=VMEM_BYTES),
    )(*parts)
    return (
        grad_inputs,
        kv_gradient,
        down_gradient.reshape(3, RANK, width),
        grad_up_q,
        grad_up_kv.reshape(2, RANK, HEAD_SIZE),
    )


def solution(mesh):
    placed = (
        P("seq", "head"),
        P("seq", "head"),
        P("seq", "head"),
        P("seq", "head"),
        P("head", "seq"),
        P("head"),
        P("seq", "head"),
        P(None, None, "head"),
        P(None, "head"),
        P(None, None, "head"),
    )
    return jax.shard_map(
        per_device,
        mesh=mesh,
        in_specs=placed,
        out_specs=(
            P("seq", "head"),
            P(None, "seq", "head"),
            P(None, None, "head"),
            P(None, "head"),
            P(None, None, "head"),
        ),
        check_vma=False,
    )
```

```python
import functools
import math

import jax
import jax.numpy as jnp
from jax import lax
from jax.experimental import pallas as pl
from jax.experimental.pallas import tpu as pltpu
from jax.sharding import PartitionSpec as P

HEAD_SIZE = 128
GROUP = 1024
RANK = 16
QUAD = 4
UNITS = 16
LOG2E = 1.4426950408889634
BIG = 1e30
ADAPTER_SCALE = 2.0
VMEM_BYTES = 63 * 1024 * 1024

MESH = pl.DeviceIdType.MESH
F32 = jnp.float32
BF16 = jnp.bfloat16


def dot_nn(a, b):
    return lax.dot_general(a, b, (((1,), (0,)), ((), ())), preferred_element_type=F32)


def dot_nt(a, b):
    return lax.dot_general(a, b, (((1,), (1,)), ((), ())), preferred_element_type=F32)


def kernel(
    seq_count,
    head_count,
    q_hbm, k_hbm, v_hbm, do_hbm, rs_hbm, flags_hbm, x_hbm, wd_hbm, wq_hbm, wkv_hbm,
    kv_hbm, xo_hbm, g_hbm, c_hbm,
    kv_out, x_out, g_out, c_out, up_out, q_v, do_v, x_v, wd_v, wq_v, wkv_v, rs_v,
    kwin, vwin, k_t, scores, tops, probs, dscores, own_kv, kv_send, kv_recv, relay,
    flags, down_send, down_recv, down_low, upq_send, upq_recv, upkv_send, upkv_recv,
    g_full, g_pair, c_full, c_pair, units, slots, c_sum, c_slots,
    load_sem, out_sem, win_ss, win_rs, down_ss, down_rs, upq_ss, upq_rs, upkv_ss, upkv_rs,
    relay_ss, relay_rs, kv_ss, kv_rs, pair_ss, pair_rs, rs_ss, rs_rs, c_ss, c_rs,
    ag_ss, ag_rs, cag_ss, cag_rs, fin_ss, fin_rs, known,
):
    tokens = q_v.shape[0]
    heads = q_v.shape[1] // HEAD_SIZE
    nz = seq_count // QUAD
    per_owner = UNITS // nz
    half = x_v.shape[1] // 2
    s = lax.axis_index("seq")
    hd = lax.axis_index("head")
    zi = s // QUAD
    core = s % 2
    x_lo = (s % QUAD) // 2
    sibling = s + 1 - 2 * core
    scale = HEAD_SIZE ** -0.5
    multiplier = ADAPTER_SCALE / math.sqrt(tokens * seq_count)
    pending = []

    def seq_at(by):
        return lax.rem(s + by + seq_count, seq_count)

    def head_at(by):
        return lax.rem(hd + by + head_count, head_count)

    def z_at(by):
        return lax.rem(zi + by + nz, nz)

    def chip(by, x):
        return z_at(by) * QUAD + x * 2 + core

    def remote(src, dst, ss, rs, target):
        return pltpu.make_async_remote_copy(
            src_ref=src, dst_ref=dst, send_sem=ss, recv_sem=rs,
            device_id={"seq": target}, device_id_type=MESH,
        )

    loads = [
        pltpu.make_async_copy(src, dst, load_sem.at[i])
        for i, (src, dst) in enumerate([
            (k_hbm, kwin.at[3]), (q_hbm, q_v), (x_hbm, x_v), (wd_hbm, wd_v), (v_hbm, vwin.at[3]),
            (do_hbm, do_v), (rs_hbm, rs_v), (wq_hbm, wq_v), (wkv_hbm, wkv_v), (flags_hbm, flags),
        ])
    ]
    for copy in loads:
        copy.start()

    barrier = pltpu.get_barrier_semaphore()
    near = [sibling, seq_at(2), seq_at(-2), seq_at(4), seq_at(-4)]
    for target in near:
        pl.semaphore_signal(barrier, inc=1, device_id={"seq": target}, device_id_type=MESH)
    for by in range(1, head_count):
        pl.semaphore_signal(barrier, inc=1, device_id={"head": head_at(by)}, device_id_type=MESH)
    pl.semaphore_wait(barrier, len(near) + head_count - 1)

    rounds = []
    step = 2
    while step < nz:
        rounds.append(step)
        step *= 2

    def tell(i):
        if i < len(rounds):
            for by in (2 * rounds[i], -2 * rounds[i]):
                pl.semaphore_signal(
                    known.at[i], inc=1, device_id={"seq": seq_at(by)}, device_id_type=MESH
                )

    def hear(i):
        if i < len(rounds):
            pl.semaphore_wait(known.at[i], 2)

    own = (k_hbm, v_hbm)
    win = (kwin, vwin)

    def cross(c):
        return remote(own[c], win[c].at[1], win_ss.at[c, 0], win_rs.at[c, 1], seq_at(2))

    def give(c):
        return remote(own[c], win[c].at[2], win_ss.at[c, 1], win_rs.at[c, 2], sibling)

    def forward(c, slot):
        return remote(win[c].at[1], win[c].at[slot], win_ss.at[c, 2], win_rs.at[c, slot], sibling)

    for c in range(2):
        cross(c).start()

        @pl.when(core == 0)
        def _():
            give(c).start()

    tell(0)

    def head_copy(src, dst, ss, rs, by):
        return pltpu.make_async_remote_copy(
            src_ref=src, dst_ref=dst.at[by], send_sem=ss.at[by], recv_sem=rs.at[by],
            device_id={"head": head_at(by)}, device_id_type=MESH,
        )

    def head_start(*args):
        for by in range(1, head_count):
            head_copy(*args, by).start()

        def wait():
            for by in range(1, head_count):
                head_copy(*args, by).wait_send()

        pending.append(wait)

    row_id = lax.broadcasted_iota(jnp.int32, (tokens, tokens), 0)
    col_id = lax.broadcasted_iota(jnp.int32, (tokens, tokens), 1)
    causal = jnp.where(row_id <= col_id, 0.0, -BIG).astype(F32)
    want = (1 - x_lo).astype(F32)
    even = (1 - core).astype(F32)
    c2 = scale * LOG2E

    def head_cols(ref, h):
        return ref[:, h * HEAD_SIZE : (h + 1) * HEAD_SIZE]

    def rows(j):
        return pl.ds(j * tokens, tokens)

    def score_block(j):
        for h in range(heads):
            score = dot_nt(kwin[j], head_cols(q_v, h))
            if j == 3:
                score = score + causal
            scores[h, rows(j), :] = score
            tops[j, h : h + 1, :] = jnp.max(score, axis=0, keepdims=True)
        k_t[:, j * tokens : (j + 1) * tokens] = kwin[j].astype(F32).T.astype(BF16)

    loads[0].wait()
    loads[1].wait()
    score_block(3)
    loads[2].wait()
    loads[3].wait()
    down_part = dot_nt(wd_v[...], x_v[...])
    down_send[...] = down_part.astype(BF16)
    hear(0)
    tell(1)

    def rest_of_scores(odd):
        if odd:
            give(0).wait_recv()
            score_block(2)
            cross(0).wait_recv()
            forward(0, 2).start()
            score_block(1)
            forward(0, 0).wait_recv()
            score_block(0)
        else:
            cross(0).wait_recv()
            forward(0, 0).start()
            score_block(1)
            forward(0, 2).wait_recv()
            score_block(2)

    def pass_values_on(odd):
        cross(1).wait_recv()
        forward(1, 2 if odd else 0).start()

    def relay_copy(slot, c):
        return remote(
            kv_send.at[slot, c], relay.at[c], relay_ss.at[c], relay_rs.at[c], sibling
        )

    def back_copy(c):
        return remote(
            kv_send.at[1, c], kv_recv.at[0, c], kv_ss.at[c], kv_rs.at[c], seq_at(-2)
        )

    def home_copy():
        return remote(kv_send.at[2], kv_recv.at[1], kv_ss.at[2], kv_rs.at[2], sibling)

    def attention(odd):
        order = (0, 1, 2, 3) if odd else (2, 1, 3)

        def weights(h, _):
            differs = flags[h].astype(F32) - want
            far = differs * differs * BIG
            bias = {0: far, 1: far, 2: 0.0 if odd else far, 3: 0.0}
            at = pl.ds(h, 1)
            top = None
            for j in order:
                high = tops[j, at, :] - bias[j]
                top = high if top is None else jnp.maximum(top, high)
            weight = {}
            total = None
            for j in order:
                weight[j] = jnp.exp2(scores[h, rows(j), :] * c2 - (top * c2 + bias[j]))
                part = jnp.sum(weight[j], axis=0, keepdims=True)
                total = part if total is None else total + part
            inverse = 1.0 / total
            for j in order:
                probs[h, rows(j), :] = (weight[j] * inverse).astype(BF16)
            return 0

        lax.fori_loop(0, heads, weights, 0)

    def summed(left, right, j):
        total = None
        for h in range(heads):
            part = dot_nn(left[h, rows(j), :], head_cols(right, h))
            total = part if total is None else total + part
        return total

    def value_grad(j):
        return summed(probs, do_v, j)

    def key_grad(j):
        for h in range(heads):
            p = probs[h, rows(j), :].astype(F32)
            dp = dot_nt(vwin[j], head_cols(do_v, h))
            dscores[h, rows(j), :] = (p * (dp - rs_v[h : h + 1, :])).astype(BF16)
        return summed(dscores, q_v, j) * scale

    def relayed(odd):
        slot = 0 if odd else 2
        if odd:
            forward(1, 0).wait_recv()
        else:
            forward(1, 2).wait_recv()
        kv_send[slot, 1] = value_grad(slot).astype(BF16)
        relay_copy(slot, 1).start()
        kv_send[slot, 0] = key_grad(slot).astype(BF16)
        relay_copy(slot, 0).start()

    def sent_back(c, grad):
        relay_copy(0, c).wait_recv()
        kv_send[1, c] = (grad + relay[c].astype(F32)).astype(BF16)
        back_copy(c).start()

    def split(fn):
        @pl.when(core == 1)
        def _():
            fn(True)

        @pl.when(core == 0)
        def _():
            fn(False)

    split(rest_of_scores)
    head_start(down_send, down_recv, down_ss, down_rs)
    hear(1)
    tell(2)
    for i in range(4, 10):
        loads[i].wait()
    split(pass_values_on)

    def window_sent(odd):
        for c in range(2):
            cross(c).wait_send()
            forward(c, 2 if odd else 0).wait_send()
            if not odd:
                give(c).wait_send()

    pending.append(lambda: split(window_sent))
    split(attention)
    split(relayed)
    sent_back(1, value_grad(1))
    sent_back(0, key_grad(1))

    @pl.when(core == 1)
    def _():
        give(1).wait_recv()
        kv_send[2, 0] = key_grad(2).astype(BF16)
        kv_send[2, 1] = value_grad(2).astype(BF16)
        home_copy().start()

    own_kv[0] = key_grad(3)
    own_kv[1] = value_grad(3)

    def grads_sent(odd):
        for c in range(2):
            relay_copy(0 if odd else 2, c).wait_send()
            back_copy(c).wait_send()
        if odd:
            home_copy().wait_send()

    pending.append(lambda: split(grads_sent))

    down = down_part
    for by in range(1, head_count):
        head_copy(down_send, down_recv, down_ss, down_rs, by).wait_recv()
        down = down + down_recv[by].astype(F32)
    down_low[...] = down.astype(BF16)

    def query_grads(odd):
        first = 0 if odd else tokens
        per_half = heads // 2
        acc = jnp.zeros((RANK, tokens), F32)
        for h in range(heads):
            dq = (dot_nn(k_t[:, first:], dscores[h, first:, :]) * scale).astype(BF16)
            col = (h % per_half) * HEAD_SIZE
            g_full[h // per_half, :RANK, col : col + HEAD_SIZE] = dot_nt(down_low[:RANK, :], dq)
            acc = acc + dot_nn(head_cols(wq_v, h), dq)
        upq_send[...] = acc.astype(BF16)

    split(query_grads)
    head_start(upq_send, upq_recv, upq_ss, upq_rs)
    hear(2)

    for c in range(2):
        back_copy(c).wait_recv()

    @pl.when(core == 0)
    def _():
        home_copy().wait_recv()
        own_kv[...] = own_kv[...] + kv_recv[1].astype(F32)

    dkv = (own_kv[...] + kv_recv[0].astype(F32)).astype(BF16)
    kv_out[...] = dkv
    placed = [
        pltpu.make_async_copy(src, dst, out_sem.at[i])
        for i, (src, dst) in enumerate([
            (kv_out, kv_hbm), (x_out, xo_hbm), (g_out, g_hbm), (c_out, c_hbm),
        ])
    ]
    placed[0].start()
    pending.append(placed[0].wait)
    for c in range(2):
        upkv_send[c * RANK : (c + 1) * RANK, :] = dot_nt(
            wkv_v[c * RANK : (c + 1) * RANK, :], dkv[c]
        ).astype(BF16)
    head_start(upkv_send, upkv_recv, upkv_ss, upkv_rs)
    for c in range(2):
        c_full[c] = dot_nn(down_low[(c + 1) * RANK : (c + 2) * RANK, :], dkv[c])

    part_rows = 2 * RANK

    def pair_copy(p):
        at = pl.ds(p * part_rows, part_rows)
        return remote(
            g_full.at[1 - core, at], g_pair.at[at], pair_ss.at[p], pair_rs.at[p], sibling
        )

    def pair_copy_c():
        return remote(c_full.at[1 - core], c_pair, pair_ss.at[2], pair_rs.at[2], sibling)

    pair_copy_c().start()
    pending.append(lambda: pair_copy_c().wait_send())

    def head_total(send, recv, ss, rs):
        total = send[...].astype(F32)
        for by in range(1, head_count):
            head_copy(send, recv, ss, rs, by).wait_recv()
            total = total + recv[by].astype(F32)
        return total.astype(BF16)

    def down_rows(first, last):
        for c in range(2):
            g_full[c, RANK + first : RANK + last, :] = dot_nn(
                up_out[first:last, :], x_v[:, c * half : (c + 1) * half]
            )

    def far_first(i):
        return nz // 2 + lax.rem(i + 1, 2) * (i // 2) - lax.rem(i, 2) * ((i + 1) // 2)

    def scatter_copy(p, by, x):
        slot = x * nz + by
        return remote(
            units.at[p, z_at(by)], slots.at[slot], rs_ss.at[p, by], rs_rs.at[slot], chip(by, p)
        )

    def loop(first, last, fn):
        def body(i, _):
            fn(i)
            return 0

        lax.fori_loop(first, last, body, 0)

    def at_x(p, fn):
        @pl.when(x_lo == p)
        def _():
            fn(nz - 1)

        @pl.when(x_lo != p)
        def _():
            fn(nz)

    def scatter(p):
        pair_copy(p).wait_recv()
        at = pl.ds(p * part_rows, part_rows)
        g = g_full[core, at, :] + g_pair[at, :]
        for u in range(UNITS):
            r, col = (u // 4) * 8, (u % 4) * 128
            units[p, u // per_owner, u % per_owner] = g[r : r + 8, col : col + 128]
        at_x(p, lambda n: loop(0, n, lambda i: scatter_copy(p, far_first(i), x_lo).start()))
        pending.append(
            lambda: at_x(
                p, lambda n: loop(0, n, lambda i: scatter_copy(p, far_first(i), x_lo).wait_send())
            )
        )

    up_out[:RANK, :] = head_total(upq_send, upq_recv, upq_ss, upq_rs)
    down_rows(0, RANK)
    pair_copy(0).start()
    pending.append(lambda: pair_copy(0).wait_send())
    scatter(0)

    c_owner = (nz // 2) * QUAD + 2 + core
    is_c_owner = s == c_owner

    def c_copy(slot):
        return remote(c_sum, c_slots.at[slot], c_ss, c_rs.at[slot], c_owner)

    pair_copy_c().wait_recv()
    c_sum[...] = c_full[core] + c_pair[...]

    @pl.when(jnp.logical_not(is_c_owner))
    def _():
        c_copy(x_lo * nz + zi).start()

    def c_sent():
        @pl.when(jnp.logical_not(is_c_owner))
        def _():
            c_copy(x_lo * nz + zi).wait_send()

    pending.append(c_sent)

    up_out[RANK:, :] = head_total(upkv_send, upkv_recv, upkv_ss, upkv_rs)
    down_rows(RANK, 3 * RANK)
    pair_copy(1).start()
    pending.append(lambda: pair_copy(1).wait_send())
    scatter(1)

    for c in range(4):
        cols = slice(c * half // 2, (c + 1) * half // 2)
        part = lax.dot_general(
            up_out[...], wd_v[:, cols], (((0,), (0,)), ((), ())), preferred_element_type=F32
        )
        x_out[:, cols] = (ADAPTER_SCALE * part).astype(BF16)
    placed[1].start()
    pending.append(placed[1].wait)

    def unit_ref(p, u):
        return g_out.at[
            pl.ds(pl.multiple_of(p * part_rows + (u // 4) * 8, 8), 8),
            pl.ds(pl.multiple_of(core * half + (u % 4) * 128, 128), 128),
        ]

    def gather_copy(p, owner, i, by, x):
        u = owner * per_owner + i
        ref = unit_ref(p, u)
        return remote(
            ref, ref, ag_ss.at[(x * nz + by) * per_owner + i], ag_rs.at[p, u], chip(by, x)
        )

    def each_target(p, fn):
        loop(0, nz - 1, lambda i: (fn(far_first(i), 0), fn(far_first(i), 1)))
        fn(0, 1 - p)

    def gather(p):
        @pl.when(x_lo == p)
        def _():
            total = units[p, zi]
            for by in range(0, nz):
                for x in (p, 1 - p):
                    if by == 0 and x == p:
                        continue
                    scatter_copy(p, by, x).wait_recv()
                    total = total + slots[x * nz + by]
            total = total * multiplier
            for i in range(per_owner):
                unit_ref(p, zi * per_owner + i)[...] = total[i]

            def start(by, x):
                for i in range(per_owner):
                    gather_copy(p, zi, i, by, x).start()

            each_target(p, start)

    def gather_sent():
        for p in range(2):

            @pl.when(x_lo == p)
            def _():
                def wait(by, x):
                    for i in range(per_owner):
                        gather_copy(p, zi, i, by, x).wait_send()

                each_target(p, wait)

    def c_ref():
        return c_out.at[pl.ds(pl.multiple_of(core * RANK, RANK), RANK), :]

    def c_gather_copy(by, x):
        return remote(c_ref(), c_ref(), cag_ss.at[x * nz + by], cag_rs, chip(by, x))

    gather(0)

    @pl.when(is_c_owner)
    def _():
        total = c_sum[...]
        for by in range(0, nz):
            for x in (1, 0):
                if by == 0 and x == 1:
                    continue
                slot = x * nz + z_at(by)
                c_copy(slot).wait_recv()
                total = total + c_slots[slot]
        c_out[pl.ds(pl.multiple_of(core * RANK, RANK), RANK), :] = total * multiplier
        each_target(1, lambda by, x: c_gather_copy(by, x).start())

    def c_gather_sent():
        @pl.when(is_c_owner)
        def _():
            each_target(1, lambda by, x: c_gather_copy(by, x).wait_send())

    gather(1)
    pending.append(gather_sent)
    pending.append(c_gather_sent)

    def wait_gathered(p):
        def wait(by):
            for i in range(per_owner):
                gather_copy(p, z_at(by), i, by, 0).wait_recv()

        loop(1, nz, wait)

        @pl.when(x_lo != p)
        def _():
            wait(0)

    def final_copy(p, side):
        ref = g_out.at[
            pl.ds(p * part_rows, part_rows), pl.ds(pl.multiple_of(side * half, 128), half)
        ]
        return remote(ref, ref, fin_ss.at[p], fin_rs.at[p], sibling)

    def final_copy_c(side):
        ref = c_out.at[pl.ds(pl.multiple_of(side * RANK, RANK), RANK), :]
        return remote(ref, ref, fin_ss.at[2], fin_rs.at[2], sibling)

    wait_gathered(0)
    final_copy(0, core).start()

    @pl.when(jnp.logical_not(is_c_owner))
    def _():
        c_gather_copy(0, 0).wait_recv()

    final_copy_c(core).start()
    wait_gathered(1)
    final_copy(1, core).start()

    for wait in pending:
        wait()
    final_copy_c(1 - core).wait_recv()
    placed[3].start()
    for p in range(2):
        final_copy(p, 1 - core).wait_recv()
    placed[2].start()
    final_copy_c(core).wait_send()
    for p in range(2):
        final_copy(p, core).wait_send()
    placed[3].wait()
    placed[2].wait()


def place(
    kv, x, g, c, down_o, up_q_o, up_kv_o, kv_o, x_o, kv_v, x_v, g_v, c_v, in_sems, out_sems
):
    ways = [
        (x, x_v, [(x_v, x_o)]),
        (g, g_v, [(g_v.at[RANK:], down_o), (g_v.at[:RANK], up_q_o)]),
        (kv, kv_v, [(kv_v, kv_o)]),
        (c, c_v, [(c_v, up_kv_o)]),
    ]
    arriving = [
        pltpu.make_async_copy(src, dst, in_sems.at[i]) for i, (src, dst, _) in enumerate(ways)
    ]
    for copy in arriving:
        copy.start()
    leaving = []
    for copy, (_, _, targets) in zip(arriving, ways):
        copy.wait()
        for src, dst in targets:
            leaving.append(pltpu.make_async_copy(src, dst, out_sems.at[len(leaving)]))
            leaving[-1].start()
    for copy in leaving:
        copy.wait()


def per_device(
    queries, layer_key_rows, layer_value_rows, output_gradient, output_row_sums,
    shifted_head_flags, inputs, adapter_down_weight, query_up_weight, key_value_up_weight,
):
    seq_count = lax.axis_size("seq")
    head_count = lax.axis_size("head")
    tokens, columns = queries.shape
    heads = columns // HEAD_SIZE
    width = inputs.shape[1]
    nz = seq_count // QUAD
    per_owner = UNITS // nz
    flat_down = adapter_down_weight.reshape(3 * RANK, width)
    flat_kv_up = key_value_up_weight.reshape(2 * RANK, HEAD_SIZE)
    vmem = pltpu.VMEM
    sem = pltpu.SemaphoreType.DMA
    anywhere = pl.BlockSpec(memory_space=pltpu.HBM)
    parts = pl.pallas_call(
        functools.partial(kernel, seq_count, head_count),
        out_shape=(
            jax.ShapeDtypeStruct((2, tokens, HEAD_SIZE), BF16),
            jax.ShapeDtypeStruct((tokens, width), BF16),
            jax.ShapeDtypeStruct((4 * RANK, width), F32),
            jax.ShapeDtypeStruct((2 * RANK, HEAD_SIZE), F32),
        ),
        in_specs=[anywhere] * 10,
        out_specs=(anywhere,) * 4,
        scratch_shapes=[
            vmem((2, tokens, HEAD_SIZE), BF16),
            vmem((tokens, width), BF16),
            vmem((4 * RANK, width), F32),
            vmem((2 * RANK, HEAD_SIZE), F32),
            vmem((3 * RANK, tokens), BF16),
            vmem((tokens, columns), BF16),
            vmem((tokens, columns), BF16),
            vmem((tokens, width), BF16),
            vmem((3 * RANK, width), BF16),
            vmem((RANK, columns), BF16),
            vmem((2 * RANK, HEAD_SIZE), BF16),
            vmem((heads, tokens), F32),
            vmem((4, tokens, HEAD_SIZE), BF16),
            vmem((4, tokens, HEAD_SIZE), BF16),
            vmem((HEAD_SIZE, 4 * tokens), BF16),
            vmem((heads, 4 * tokens, tokens), F32),
            vmem((4, heads, tokens), F32),
            vmem((heads, 4 * tokens, tokens), BF16),
            vmem((heads, 4 * tokens, tokens), BF16),
            vmem((2, tokens, HEAD_SIZE), F32),
            vmem((3, 2, tokens, HEAD_SIZE), BF16),
            vmem((2, 2, tokens, HEAD_SIZE), BF16),
            vmem((2, tokens, HEAD_SIZE), BF16),
            pltpu.SMEM((heads,), jnp.int32),
            vmem((3 * RANK, tokens), BF16),
            vmem((head_count, 3 * RANK, tokens), BF16),
            vmem((3 * RANK, tokens), BF16),
            vmem((RANK, tokens), BF16),
            vmem((head_count, RANK, tokens), BF16),
            vmem((2 * RANK, tokens), BF16),
            vmem((head_count, 2 * RANK, tokens), BF16),
            vmem((2, 4 * RANK, width // 2), F32),
            vmem((4 * RANK, width // 2), F32),
            vmem((2, RANK, HEAD_SIZE), F32),
            vmem((RANK, HEAD_SIZE), F32),
            vmem((2, nz, per_owner, 8, 128), F32),
            vmem((2 * nz, per_owner, 8, 128), F32),
            vmem((RANK, HEAD_SIZE), F32),
            vmem((2 * nz, RANK, HEAD_SIZE), F32),
            sem((10,)), sem((4,)),
            sem((2, 3)), sem((2, 4)),
            sem((head_count,)), sem((head_count,)),
            sem((head_count,)), sem((head_count,)),
            sem((head_count,)), sem((head_count,)),
            sem((2,)), sem((2,)),
            sem((3,)), sem((3,)),
            sem((3,)), sem((3,)),
            sem((2, nz)), sem((2 * nz,)),
            sem, sem((2 * nz,)),
            sem((2 * nz * per_owner,)), sem((2, UNITS)),
            sem((2 * nz,)), sem,
            sem((3,)), sem((3,)),
            pltpu.SemaphoreType.REGULAR((3,)),
        ],
        compiler_params=pltpu.CompilerParams(
            collective_id=0, has_side_effects=True, vmem_limit_bytes=VMEM_BYTES
        ),
    )(
        queries, layer_key_rows, layer_value_rows, output_gradient, output_row_sums,
        shifted_head_flags, inputs, flat_down, query_up_weight, flat_kv_up,
    )
    down_gradient, grad_up_q, grad_up_kv, kv_gradient, grad_inputs = pl.pallas_call(
        place,
        out_shape=(
            jax.ShapeDtypeStruct((3 * RANK, width), F32),
            jax.ShapeDtypeStruct((RANK, columns), F32),
            jax.ShapeDtypeStruct((2 * RANK, HEAD_SIZE), F32),
            jax.ShapeDtypeStruct((2, tokens, HEAD_SIZE), BF16),
            jax.ShapeDtypeStruct((tokens, width), BF16),
        ),
        in_specs=[anywhere] * 4,
        out_specs=(anywhere,) * 5,
        scratch_shapes=[
            vmem((2, tokens, HEAD_SIZE), BF16),
            vmem((tokens, width), BF16),
            vmem((4 * RANK, width), F32),
            vmem((2 * RANK, HEAD_SIZE), F32),
            sem((4,)),
            sem((5,)),
        ],
        compiler_params=pltpu.CompilerParams(vmem_limit_bytes=VMEM_BYTES),
    )(*parts)
    return (
        grad_inputs,
        kv_gradient,
        down_gradient.reshape(3, RANK, width),
        grad_up_q,
        grad_up_kv.reshape(2, RANK, HEAD_SIZE),
    )


def solution(mesh):
    placed = (
        P("seq", "head"),
        P("seq", "head"),
        P("seq", "head"),
        P("seq", "head"),
        P("head", "seq"),
        P("head"),
        P("seq", "head"),
        P(None, None, "head"),
        P(None, "head"),
        P(None, None, "head"),
    )
    return jax.shard_map(
        per_device,
        mesh=mesh,
        in_specs=placed,
        out_specs=(
            P("seq", "head"),
            P(None, "seq", "head"),
            P(None, None, "head"),
            P(None, "head"),
            P(None, None, "head"),
        ),
        check_vma=False,
    )
```

```python
import functools
import math

import jax
import jax.numpy as jnp
from jax import lax
from jax.experimental import pallas as pl
from jax.experimental.pallas import tpu as pltpu
from jax.sharding import PartitionSpec as P

HEAD_SIZE = 128
GROUP = 1024
RANK = 16
QUAD = 4
UNITS = 8
LOG2E = 1.4426950408889634
BIG = 1e30
ADAPTER_SCALE = 2.0
VMEM_BYTES = 63 * 1024 * 1024

MESH = pl.DeviceIdType.MESH
F32 = jnp.float32
BF16 = jnp.bfloat16


def dot_nn(a, b):
    return lax.dot_general(a, b, (((1,), (0,)), ((), ())), preferred_element_type=F32)


def dot_nt(a, b):
    return lax.dot_general(a, b, (((1,), (1,)), ((), ())), preferred_element_type=F32)


def kernel(
    seq_count,
    head_count,
    q_hbm, k_hbm, v_hbm, do_hbm, rs_hbm, flags_hbm, x_hbm, wd_hbm, wq_hbm, wkv_hbm,
    kv_hbm, xo_hbm, g_hbm, c_hbm,
    kv_out, x_out, g_out, c_out, g_low, c_low, up_out, q_v, do_v, x_v, wd_v, wq_v, wkv_v, rs_v,
    kwin, vwin, k_t, scores, tops, probs, dscores, own_kv, kv_send, kv_recv, relay,
    flags, down_send, down_recv, down_low, upq_send, upq_recv, upkv_send, upkv_recv,
    g_full, g_pair, c_full, c_pair, units, slots, c_sum, c_send, c_slots,
    load_sem, out_sem, win_ss, win_rs, down_ss, down_rs, upq_ss, upq_rs, upkv_ss, upkv_rs,
    relay_ss, relay_rs, kv_ss, kv_rs, pair_ss, pair_rs, rs_ss, rs_rs, c_ss, c_rs,
    ag_ss, ag_rs, cag_ss, cag_rs, fin_ss, fin_rs, known,
):
    tokens = q_v.shape[0]
    heads = q_v.shape[1] // HEAD_SIZE
    nz = seq_count // QUAD
    owners = min(nz, UNITS)
    stride = nz // owners
    per_owner = UNITS // owners
    half = x_v.shape[1] // 2
    s = lax.axis_index("seq")
    hd = lax.axis_index("head")
    zi = s // QUAD
    core = s % 2
    x_lo = (s % QUAD) // 2
    sibling = s + 1 - 2 * core
    scale = HEAD_SIZE ** -0.5
    multiplier = ADAPTER_SCALE / math.sqrt(tokens * seq_count)
    pending = []

    def seq_at(by):
        return lax.rem(s + by + seq_count, seq_count)

    def head_at(by):
        return lax.rem(hd + by + head_count, head_count)

    def z_at(by):
        return lax.rem(zi + by + nz, nz)

    def chip(by, x):
        return z_at(by) * QUAD + x * 2 + core

    def remote(src, dst, ss, rs, target):
        return pltpu.make_async_remote_copy(
            src_ref=src, dst_ref=dst, send_sem=ss, recv_sem=rs,
            device_id={"seq": target}, device_id_type=MESH,
        )

    loads = [
        pltpu.make_async_copy(src, dst, load_sem.at[i])
        for i, (src, dst) in enumerate([
            (k_hbm, kwin.at[3]), (q_hbm, q_v), (x_hbm, x_v), (wd_hbm, wd_v), (v_hbm, vwin.at[3]),
            (do_hbm, do_v), (rs_hbm, rs_v), (wq_hbm, wq_v), (wkv_hbm, wkv_v), (flags_hbm, flags),
        ])
    ]
    for copy in loads:
        copy.start()

    barrier = pltpu.get_barrier_semaphore()
    near = [sibling, seq_at(2), seq_at(-2), seq_at(4), seq_at(-4)]
    for target in near:
        pl.semaphore_signal(barrier, inc=1, device_id={"seq": target}, device_id_type=MESH)
    for by in range(1, head_count):
        pl.semaphore_signal(barrier, inc=1, device_id={"head": head_at(by)}, device_id_type=MESH)
    pl.semaphore_wait(barrier, len(near) + head_count - 1)

    rounds = []
    step = 2
    while step < nz:
        rounds.append(step)
        step *= 2

    def tell(i):
        if i < len(rounds):
            for by in (2 * rounds[i], -2 * rounds[i]):
                pl.semaphore_signal(
                    known.at[i], inc=1, device_id={"seq": seq_at(by)}, device_id_type=MESH
                )

    def hear(i):
        if i < len(rounds):
            pl.semaphore_wait(known.at[i], 2)

    own = (k_hbm, v_hbm)
    win = (kwin, vwin)

    def cross(c):
        return remote(own[c], win[c].at[1], win_ss.at[c, 0], win_rs.at[c, 1], seq_at(2))

    def give(c):
        return remote(own[c], win[c].at[2], win_ss.at[c, 1], win_rs.at[c, 2], sibling)

    def forward(c, slot):
        return remote(win[c].at[1], win[c].at[slot], win_ss.at[c, 2], win_rs.at[c, slot], sibling)

    for c in range(2):
        cross(c).start()

        @pl.when(core == 0)
        def _():
            give(c).start()

    tell(0)

    def head_copy(src, dst, ss, rs, by):
        return pltpu.make_async_remote_copy(
            src_ref=src, dst_ref=dst.at[by], send_sem=ss.at[by], recv_sem=rs.at[by],
            device_id={"head": head_at(by)}, device_id_type=MESH,
        )

    def head_start(*args):
        for by in range(1, head_count):
            head_copy(*args, by).start()

        def wait():
            for by in range(1, head_count):
                head_copy(*args, by).wait_send()

        pending.append(wait)

    row_id = lax.broadcasted_iota(jnp.int32, (tokens, tokens), 0)
    col_id = lax.broadcasted_iota(jnp.int32, (tokens, tokens), 1)
    causal = jnp.where(row_id <= col_id, 0.0, -BIG).astype(F32)
    want = (1 - x_lo).astype(F32)
    even = (1 - core).astype(F32)
    c2 = scale * LOG2E

    def head_cols(ref, h):
        return ref[:, h * HEAD_SIZE : (h + 1) * HEAD_SIZE]

    def rows(j):
        return pl.ds(j * tokens, tokens)

    def score_block(j):
        for h in range(heads):
            score = dot_nt(kwin[j], head_cols(q_v, h))
            if j == 3:
                score = score + causal
            scores[h, rows(j), :] = score
            tops[j, h : h + 1, :] = jnp.max(score, axis=0, keepdims=True)
        k_t[:, j * tokens : (j + 1) * tokens] = kwin[j].astype(F32).T.astype(BF16)

    loads[0].wait()
    loads[1].wait()
    score_block(3)
    loads[2].wait()
    loads[3].wait()
    down_part = dot_nt(wd_v[...], x_v[...])
    down_send[...] = down_part.astype(BF16)
    hear(0)
    tell(1)

    def rest_of_scores(odd):
        if odd:
            give(0).wait_recv()
            score_block(2)
            cross(0).wait_recv()
            forward(0, 2).start()
            score_block(1)
            forward(0, 0).wait_recv()
            score_block(0)
        else:
            cross(0).wait_recv()
            forward(0, 0).start()
            score_block(1)
            forward(0, 2).wait_recv()
            score_block(2)

    def pass_values_on(odd):
        cross(1).wait_recv()
        forward(1, 2 if odd else 0).start()

    def relay_copy(slot, c):
        return remote(
            kv_send.at[slot, c], relay.at[c], relay_ss.at[c], relay_rs.at[c], sibling
        )

    def back_copy(c):
        return remote(
            kv_send.at[1, c], kv_recv.at[0, c], kv_ss.at[c], kv_rs.at[c], seq_at(-2)
        )

    def home_copy():
        return remote(kv_send.at[2], kv_recv.at[1], kv_ss.at[2], kv_rs.at[2], sibling)

    def attention(odd):
        order = (0, 1, 2, 3) if odd else (2, 1, 3)

        def weights(h, _):
            differs = flags[h].astype(F32) - want
            far = differs * differs * BIG
            bias = {0: far, 1: far, 2: 0.0 if odd else far, 3: 0.0}
            at = pl.ds(h, 1)
            top = None
            for j in order:
                high = tops[j, at, :] - bias[j]
                top = high if top is None else jnp.maximum(top, high)
            weight = {}
            total = None
            for j in order:
                weight[j] = jnp.exp2(scores[h, rows(j), :] * c2 - (top * c2 + bias[j]))
                part = jnp.sum(weight[j], axis=0, keepdims=True)
                total = part if total is None else total + part
            inverse = 1.0 / total
            for j in order:
                probs[h, rows(j), :] = (weight[j] * inverse).astype(BF16)
            return 0

        lax.fori_loop(0, heads, weights, 0)

    def summed(left, right, j):
        total = None
        for h in range(heads):
            part = dot_nn(left[h, rows(j), :], head_cols(right, h))
            total = part if total is None else total + part
        return total

    def value_grad(j):
        return summed(probs, do_v, j)

    def key_grad(j):
        for h in range(heads):
            p = probs[h, rows(j), :].astype(F32)
            dp = dot_nt(vwin[j], head_cols(do_v, h))
            dscores[h, rows(j), :] = (p * (dp - rs_v[h : h + 1, :])).astype(BF16)
        return summed(dscores, q_v, j) * scale

    def relayed(odd):
        slot = 0 if odd else 2
        if odd:
            forward(1, 0).wait_recv()
        else:
            forward(1, 2).wait_recv()
        kv_send[slot, 1] = value_grad(slot).astype(BF16)
        relay_copy(slot, 1).start()
        kv_send[slot, 0] = key_grad(slot).astype(BF16)
        relay_copy(slot, 0).start()

    def sent_back(c, grad):
        relay_copy(0, c).wait_recv()
        kv_send[1, c] = (grad + relay[c].astype(F32)).astype(BF16)
        back_copy(c).start()

    def split(fn):
        @pl.when(core == 1)
        def _():
            fn(True)

        @pl.when(core == 0)
        def _():
            fn(False)

    split(rest_of_scores)
    head_start(down_send, down_recv, down_ss, down_rs)
    hear(1)
    tell(2)
    for i in range(4, 10):
        loads[i].wait()
    split(pass_values_on)

    def window_sent(odd):
        for c in range(2):
            cross(c).wait_send()
            forward(c, 2 if odd else 0).wait_send()
            if not odd:
                give(c).wait_send()

    pending.append(lambda: split(window_sent))
    split(attention)
    split(relayed)
    sent_back(1, value_grad(1))
    sent_back(0, key_grad(1))

    @pl.when(core == 1)
    def _():
        give(1).wait_recv()
        kv_send[2, 0] = key_grad(2).astype(BF16)
        kv_send[2, 1] = value_grad(2).astype(BF16)
        home_copy().start()

    own_kv[0] = key_grad(3)
    own_kv[1] = value_grad(3)

    def grads_sent(odd):
        for c in range(2):
            relay_copy(0 if odd else 2, c).wait_send()
            back_copy(c).wait_send()
        if odd:
            home_copy().wait_send()

    pending.append(lambda: split(grads_sent))

    down = down_part
    for by in range(1, head_count):
        head_copy(down_send, down_recv, down_ss, down_rs, by).wait_recv()
        down = down + down_recv[by].astype(F32)
    down_low[...] = down.astype(BF16)

    def query_grads(odd):
        first = 0 if odd else tokens
        per_half = heads // 2
        acc = jnp.zeros((RANK, tokens), F32)
        for h in range(heads):
            dq = (dot_nn(k_t[:, first:], dscores[h, first:, :]) * scale).astype(BF16)
            col = (h % per_half) * HEAD_SIZE
            g_full[h // per_half, :RANK, col : col + HEAD_SIZE] = dot_nt(down_low[:RANK, :], dq)
            acc = acc + dot_nn(head_cols(wq_v, h), dq)
        upq_send[...] = acc.astype(BF16)

    split(query_grads)
    head_start(upq_send, upq_recv, upq_ss, upq_rs)
    hear(2)

    for c in range(2):
        back_copy(c).wait_recv()

    @pl.when(core == 0)
    def _():
        home_copy().wait_recv()
        own_kv[...] = own_kv[...] + kv_recv[1].astype(F32)

    dkv = (own_kv[...] + kv_recv[0].astype(F32)).astype(BF16)
    kv_out[...] = dkv
    placed = [
        pltpu.make_async_copy(src, dst, out_sem.at[i])
        for i, (src, dst) in enumerate([
            (kv_out, kv_hbm), (x_out, xo_hbm), (g_out, g_hbm), (c_out, c_hbm),
        ])
    ]
    placed[0].start()
    pending.append(placed[0].wait)
    for c in range(2):
        upkv_send[c * RANK : (c + 1) * RANK, :] = dot_nt(
            wkv_v[c * RANK : (c + 1) * RANK, :], dkv[c]
        ).astype(BF16)
    head_start(upkv_send, upkv_recv, upkv_ss, upkv_rs)
    for c in range(2):
        c_full[c] = dot_nn(down_low[(c + 1) * RANK : (c + 2) * RANK, :], dkv[c])

    part_rows = 2 * RANK

    def pair_copy(p):
        at = pl.ds(p * part_rows, part_rows)
        return remote(
            g_full.at[1 - core, at], g_pair.at[at], pair_ss.at[p], pair_rs.at[p], sibling
        )

    def pair_copy_c():
        return remote(c_full.at[1 - core], c_pair, pair_ss.at[2], pair_rs.at[2], sibling)

    pair_copy_c().start()
    pending.append(lambda: pair_copy_c().wait_send())

    def head_total(send, recv, ss, rs):
        total = send[...].astype(F32)
        for by in range(1, head_count):
            head_copy(send, recv, ss, rs, by).wait_recv()
            total = total + recv[by].astype(F32)
        return total.astype(BF16)

    def down_rows(first, last):
        for c in range(2):
            g_full[c, RANK + first : RANK + last, :] = dot_nn(
                up_out[first:last, :], x_v[:, c * half : (c + 1) * half]
            )

    def far_first(n, i):
        return n // 2 + lax.rem(i + 1, 2) * (i // 2) - lax.rem(i, 2) * ((i + 1) // 2)

    def owner_at(by):
        return lax.rem(zi // stride + by, owners)

    def scatter_copy(p, owner):
        slot = x_lo * nz + zi
        return remote(
            units.at[p, owner], slots.at[slot], rs_ss.at[p, owner], rs_rs.at[slot],
            owner * stride * QUAD + p * 2 + core,
        )

    def arrived(z, x):
        slot = x * nz + z
        remote(units.at[0, 0], slots.at[slot], rs_ss.at[0, 0], rs_rs.at[slot], sibling).wait_recv()
        return slots[slot].astype(F32)

    def loop(first, last, fn):
        def body(i, _):
            fn(i)
            return 0

        lax.fori_loop(first, last, body, 0)

    def is_owner(p):
        return jnp.logical_and(x_lo == p, lax.rem(zi, stride) == 0)

    def each_owner(p, fn):
        loop(0, owners - 1, lambda i: fn(owner_at(far_first(owners, i))))

        @pl.when(jnp.logical_not(is_owner(p)))
        def _():
            fn(zi // stride)

    def scatter(p):
        pair_copy(p).wait_recv()
        at = pl.ds(p * part_rows, part_rows)
        g = (g_full[core, at, :] + g_pair[at, :]).astype(BF16)
        for u in range(UNITS):
            r, col = (u // 4) * 16, (u % 4) * 128
            units[p, u // per_owner, u % per_owner] = g[r : r + 16, col : col + 128]
        each_owner(p, lambda owner: scatter_copy(p, owner).start())
        pending.append(lambda: each_owner(p, lambda owner: scatter_copy(p, owner).wait_send()))

    up_out[:RANK, :] = head_total(upq_send, upq_recv, upq_ss, upq_rs)
    down_rows(0, RANK)
    pair_copy(0).start()
    pending.append(lambda: pair_copy(0).wait_send())
    scatter(0)

    c_owner = ((nz // 2 + 1) % nz) * QUAD + 2 + core
    is_c_owner = s == c_owner

    def c_copy(slot):
        return remote(c_send, c_slots.at[slot], c_ss, c_rs.at[slot], c_owner)

    pair_copy_c().wait_recv()
    c_sum[...] = c_full[core] + c_pair[...]
    c_send[...] = c_sum[...].astype(BF16)

    @pl.when(jnp.logical_not(is_c_owner))
    def _():
        c_copy(x_lo * nz + zi).start()

    def c_sent():
        @pl.when(jnp.logical_not(is_c_owner))
        def _():
            c_copy(x_lo * nz + zi).wait_send()

    pending.append(c_sent)

    up_out[RANK:, :] = head_total(upkv_send, upkv_recv, upkv_ss, upkv_rs)
    down_rows(RANK, 3 * RANK)
    pair_copy(1).start()
    pending.append(lambda: pair_copy(1).wait_send())
    scatter(1)

    for c in range(4):
        cols = slice(c * half // 2, (c + 1) * half // 2)
        part = lax.dot_general(
            up_out[...], wd_v[:, cols], (((0,), (0,)), ((), ())), preferred_element_type=F32
        )
        x_out[:, cols] = (ADAPTER_SCALE * part).astype(BF16)
    placed[1].start()
    pending.append(placed[1].wait)

    def unit_ref(p, u):
        return g_low.at[
            pl.ds(pl.multiple_of(p * part_rows + (u // 4) * 16, 16), 16),
            pl.ds(pl.multiple_of(core * half + (u % 4) * 128, 128), 128),
        ]

    def gather_copy(p, owner, i, by, x):
        u = owner * per_owner + i
        ref = unit_ref(p, u)
        return remote(
            ref, ref, ag_ss.at[(x * nz + by) * per_owner + i], ag_rs.at[p, u], chip(by, x)
        )

    def each_target(p, fn):
        loop(0, nz - 1, lambda i: (fn(far_first(nz, i), 0), fn(far_first(nz, i), 1)))
        fn(0, 1 - p)

    def gather(p):
        @pl.when(is_owner(p))
        def _():
            mine = zi // stride
            total = units[p, mine].astype(F32)
            for by in range(0, nz):
                for x in (p, 1 - p):
                    if by == 0 and x == p:
                        continue
                    total = total + arrived(z_at(by), x)
            total = (total * multiplier).astype(BF16)
            for i in range(per_owner):
                unit_ref(p, mine * per_owner + i)[...] = total[i]

            def start(by, x):
                for i in range(per_owner):
                    gather_copy(p, mine, i, by, x).start()

            each_target(p, start)

    def gather_sent():
        for p in range(2):

            @pl.when(is_owner(p))
            def _():
                def wait(by, x):
                    for i in range(per_owner):
                        gather_copy(p, zi // stride, i, by, x).wait_send()

                each_target(p, wait)

    def c_ref():
        return c_low.at[pl.ds(pl.multiple_of(core * RANK, RANK), RANK), :]

    def c_gather_copy(by, x):
        return remote(c_ref(), c_ref(), cag_ss.at[x * nz + by], cag_rs, chip(by, x))

    gather(0)

    @pl.when(is_c_owner)
    def _():
        total = c_sum[...]
        for by in range(0, nz):
            for x in (1, 0):
                if by == 0 and x == 1:
                    continue
                slot = x * nz + z_at(by)
                c_copy(slot).wait_recv()
                total = total + c_slots[slot].astype(F32)
        c_ref()[...] = (total * multiplier).astype(BF16)
        each_target(1, lambda by, x: c_gather_copy(by, x).start())

    def c_gather_sent():
        @pl.when(is_c_owner)
        def _():
            each_target(1, lambda by, x: c_gather_copy(by, x).wait_send())

    gather(1)
    pending.append(gather_sent)
    pending.append(c_gather_sent)

    def wait_gathered(p):
        def wait(owner):
            for i in range(per_owner):
                gather_copy(p, owner, i, 0, 0).wait_recv()

        each_owner(p, wait)

    def final_copy(p, side):
        ref = g_low.at[
            pl.ds(p * part_rows, part_rows), pl.ds(pl.multiple_of(side * half, 128), half)
        ]
        return remote(ref, ref, fin_ss.at[p], fin_rs.at[p], sibling)

    def final_copy_c(side):
        ref = c_low.at[pl.ds(pl.multiple_of(side * RANK, RANK), RANK), :]
        return remote(ref, ref, fin_ss.at[2], fin_rs.at[2], sibling)

    wait_gathered(0)
    final_copy(0, core).start()

    @pl.when(jnp.logical_not(is_c_owner))
    def _():
        c_gather_copy(0, 0).wait_recv()

    final_copy_c(core).start()
    wait_gathered(1)
    final_copy(1, core).start()

    for wait in pending:
        wait()
    final_copy_c(1 - core).wait_recv()
    c_out[...] = c_low[...].astype(F32)
    placed[3].start()
    for p in range(2):
        final_copy(p, 1 - core).wait_recv()
    g_out[...] = g_low[...].astype(F32)
    placed[2].start()
    final_copy_c(core).wait_send()
    for p in range(2):
        final_copy(p, core).wait_send()
    placed[3].wait()
    placed[2].wait()


def place(
    kv, x, g, c, down_o, up_q_o, up_kv_o, kv_o, x_o, kv_v, x_v, g_v, c_v, in_sems, out_sems
):
    ways = [
        (x, x_v, [(x_v, x_o)]),
        (g, g_v, [(g_v.at[RANK:], down_o), (g_v.at[:RANK], up_q_o)]),
        (kv, kv_v, [(kv_v, kv_o)]),
        (c, c_v, [(c_v, up_kv_o)]),
    ]
    arriving = [
        pltpu.make_async_copy(src, dst, in_sems.at[i]) for i, (src, dst, _) in enumerate(ways)
    ]
    for copy in arriving:
        copy.start()
    leaving = []
    for copy, (_, _, targets) in zip(arriving, ways):
        copy.wait()
        for src, dst in targets:
            leaving.append(pltpu.make_async_copy(src, dst, out_sems.at[len(leaving)]))
            leaving[-1].start()
    for copy in leaving:
        copy.wait()


def per_device(
    queries, layer_key_rows, layer_value_rows, output_gradient, output_row_sums,
    shifted_head_flags, inputs, adapter_down_weight, query_up_weight, key_value_up_weight,
):
    seq_count = lax.axis_size("seq")
    head_count = lax.axis_size("head")
    tokens, columns = queries.shape
    heads = columns // HEAD_SIZE
    width = inputs.shape[1]
    nz = seq_count // QUAD
    owners = min(nz, UNITS)
    per_owner = UNITS // owners
    flat_down = adapter_down_weight.reshape(3 * RANK, width)
    flat_kv_up = key_value_up_weight.reshape(2 * RANK, HEAD_SIZE)
    vmem = pltpu.VMEM
    sem = pltpu.SemaphoreType.DMA
    anywhere = pl.BlockSpec(memory_space=pltpu.HBM)
    parts = pl.pallas_call(
        functools.partial(kernel, seq_count, head_count),
        out_shape=(
            jax.ShapeDtypeStruct((2, tokens, HEAD_SIZE), BF16),
            jax.ShapeDtypeStruct((tokens, width), BF16),
            jax.ShapeDtypeStruct((4 * RANK, width), F32),
            jax.ShapeDtypeStruct((2 * RANK, HEAD_SIZE), F32),
        ),
        in_specs=[anywhere] * 10,
        out_specs=(anywhere,) * 4,
        scratch_shapes=[
            vmem((2, tokens, HEAD_SIZE), BF16),
            vmem((tokens, width), BF16),
            vmem((4 * RANK, width), F32),
            vmem((2 * RANK, HEAD_SIZE), F32),
            vmem((4 * RANK, width), BF16),
            vmem((2 * RANK, HEAD_SIZE), BF16),
            vmem((3 * RANK, tokens), BF16),
            vmem((tokens, columns), BF16),
            vmem((tokens, columns), BF16),
            vmem((tokens, width), BF16),
            vmem((3 * RANK, width), BF16),
            vmem((RANK, columns), BF16),
            vmem((2 * RANK, HEAD_SIZE), BF16),
            vmem((heads, tokens), F32),
            vmem((4, tokens, HEAD_SIZE), BF16),
            vmem((4, tokens, HEAD_SIZE), BF16),
            vmem((HEAD_SIZE, 4 * tokens), BF16),
            vmem((heads, 4 * tokens, tokens), F32),
            vmem((4, heads, tokens), F32),
            vmem((heads, 4 * tokens, tokens), BF16),
            vmem((heads, 4 * tokens, tokens), BF16),
            vmem((2, tokens, HEAD_SIZE), F32),
            vmem((3, 2, tokens, HEAD_SIZE), BF16),
            vmem((2, 2, tokens, HEAD_SIZE), BF16),
            vmem((2, tokens, HEAD_SIZE), BF16),
            pltpu.SMEM((heads,), jnp.int32),
            vmem((3 * RANK, tokens), BF16),
            vmem((head_count, 3 * RANK, tokens), BF16),
            vmem((3 * RANK, tokens), BF16),
            vmem((RANK, tokens), BF16),
            vmem((head_count, RANK, tokens), BF16),
            vmem((2 * RANK, tokens), BF16),
            vmem((head_count, 2 * RANK, tokens), BF16),
            vmem((2, 4 * RANK, width // 2), F32),
            vmem((4 * RANK, width // 2), F32),
            vmem((2, RANK, HEAD_SIZE), F32),
            vmem((RANK, HEAD_SIZE), F32),
            vmem((2, owners, per_owner, 16, 128), BF16),
            vmem((2 * nz, per_owner, 16, 128), BF16),
            vmem((RANK, HEAD_SIZE), F32),
            vmem((RANK, HEAD_SIZE), BF16),
            vmem((2 * nz, RANK, HEAD_SIZE), BF16),
            sem((10,)), sem((4,)),
            sem((2, 3)), sem((2, 4)),
            sem((head_count,)), sem((head_count,)),
            sem((head_count,)), sem((head_count,)),
            sem((head_count,)), sem((head_count,)),
            sem((2,)), sem((2,)),
            sem((3,)), sem((3,)),
            sem((3,)), sem((3,)),
            sem((2, owners)), sem((2 * nz,)),
            sem, sem((2 * nz,)),
            sem((2 * nz * per_owner,)), sem((2, UNITS)),
            sem((2 * nz,)), sem,
            sem((3,)), sem((3,)),
            pltpu.SemaphoreType.REGULAR((3,)),
        ],
        compiler_params=pltpu.CompilerParams(
            collective_id=0, has_side_effects=True, vmem_limit_bytes=VMEM_BYTES
        ),
    )(
        queries, layer_key_rows, layer_value_rows, output_gradient, output_row_sums,
        shifted_head_flags, inputs, flat_down, query_up_weight, flat_kv_up,
    )
    down_gradient, grad_up_q, grad_up_kv, kv_gradient, grad_inputs = pl.pallas_call(
        place,
        out_shape=(
            jax.ShapeDtypeStruct((3 * RANK, width), F32),
            jax.ShapeDtypeStruct((RANK, columns), F32),
            jax.ShapeDtypeStruct((2 * RANK, HEAD_SIZE), F32),
            jax.ShapeDtypeStruct((2, tokens, HEAD_SIZE), BF16),
            jax.ShapeDtypeStruct((tokens, width), BF16),
        ),
        in_specs=[anywhere] * 4,
        out_specs=(anywhere,) * 5,
        scratch_shapes=[
            vmem((2, tokens, HEAD_SIZE), BF16),
            vmem((tokens, width), BF16),
            vmem((4 * RANK, width), F32),
            vmem((2 * RANK, HEAD_SIZE), F32),
            sem((4,)),
            sem((5,)),
        ],
        compiler_params=pltpu.CompilerParams(vmem_limit_bytes=VMEM_BYTES),
    )(*parts)
    return (
        grad_inputs,
        kv_gradient,
        down_gradient.reshape(3, RANK, width),
        grad_up_q,
        grad_up_kv.reshape(2, RANK, HEAD_SIZE),
    )


def solution(mesh):
    placed = (
        P("seq", "head"),
        P("seq", "head"),
        P("seq", "head"),
        P("seq", "head"),
        P("head", "seq"),
        P("head"),
        P("seq", "head"),
        P(None, None, "head"),
        P(None, "head"),
        P(None, None, "head"),
    )
    return jax.shard_map(
        per_device,
        mesh=mesh,
        in_specs=placed,
        out_specs=(
            P("seq", "head"),
            P(None, "seq", "head"),
            P(None, None, "head"),
            P(None, "head"),
            P(None, None, "head"),
        ),
        check_vma=False,
    )
```

```python
import functools
import math

import jax
import jax.numpy as jnp
from jax import lax
from jax.experimental import pallas as pl
from jax.experimental.pallas import tpu as pltpu
from jax.sharding import PartitionSpec as P

HEAD_SIZE = 128
GROUP = 1024
RANK = 16
QUAD = 4
ROW = 4
UNITS = 8
LOG2E = 1.4426950408889634
BIG = 1e30
ADAPTER_SCALE = 2.0
VMEM_BYTES = 63 * 1024 * 1024

MESH = pl.DeviceIdType.MESH
F32 = jnp.float32
BF16 = jnp.bfloat16


def dot_nn(a, b):
    return lax.dot_general(a, b, (((1,), (0,)), ((), ())), preferred_element_type=F32)


def dot_nt(a, b):
    return lax.dot_general(a, b, (((1,), (1,)), ((), ())), preferred_element_type=F32)


def kernel(
    seq_count,
    head_count,
    q_hbm, k_hbm, v_hbm, do_hbm, rs_hbm, flags_hbm, x_hbm, wd_hbm, wq_hbm, wkv_hbm,
    kv_hbm, xo_hbm, g_hbm, c_hbm,
    kv_out, x_out, g_out, c_out, g_low, c_low, up_out, q_v, do_v, x_v, wd_v, wq_v, wkv_v, rs_v,
    kwin, vwin, k_t, scores, tops, probs, dscores, own_kv, kv_send, kv_recv, relay,
    flags, down_send, down_recv, down_low, up_send, up_recv, near_send, near_recv,
    g_full, g_pair, c_full, c_pair, units, slots, c_sum, c_send, c_slots,
    load_sem, out_sem, win_ss, win_rs, down_ss, down_rs, up_ss, up_rs, near_ss, near_rs,
    relay_ss, relay_rs, kv_ss, kv_rs, pair_ss, pair_rs, rs_ss, rs_rs, c_ss, c_rs,
    ag_ss, ag_rs, cag_ss, cag_rs, fin_ss, fin_rs, known,
):
    tokens = q_v.shape[0]
    heads = q_v.shape[1] // HEAD_SIZE
    nz = seq_count // QUAD
    owners = min(nz, UNITS)
    stride = nz // owners
    per_owner = UNITS // owners
    half = x_v.shape[1] // 2
    s = lax.axis_index("seq")
    hd = lax.axis_index("head")
    zi = s // QUAD
    core = s % 2
    x_lo = (s % QUAD) // 2
    sibling = s + 1 - 2 * core
    scale = HEAD_SIZE ** -0.5
    multiplier = ADAPTER_SCALE / math.sqrt(tokens * seq_count)
    pending = []

    def seq_at(by):
        return lax.rem(s + by + seq_count, seq_count)

    def head_at(by):
        return lax.rem(hd + by + head_count, head_count)

    in_row = min(ROW, head_count)

    def row_at(by):
        return hd // in_row * in_row + lax.rem(hd % in_row + by + in_row, in_row)

    other_row = lax.rem(hd + in_row, head_count)

    def z_at(by):
        return lax.rem(zi + by + nz, nz)

    def chip(by, x):
        return z_at(by) * QUAD + x * 2 + core

    def remote(src, dst, ss, rs, target):
        return pltpu.make_async_remote_copy(
            src_ref=src, dst_ref=dst, send_sem=ss, recv_sem=rs,
            device_id={"seq": target}, device_id_type=MESH,
        )

    barrier = pltpu.get_barrier_semaphore()
    near = [sibling, seq_at(2), seq_at(-2), seq_at(4), seq_at(-4)]
    for target in near:
        pl.semaphore_signal(barrier, inc=1, device_id={"seq": target}, device_id_type=MESH)
    near_heads = [row_at(1), row_at(-1)] + ([other_row] if head_count > ROW else [])
    for target in near_heads:
        pl.semaphore_signal(barrier, inc=1, device_id={"head": target}, device_id_type=MESH)

    loads = [
        pltpu.make_async_copy(src, dst, load_sem.at[i])
        for i, (src, dst) in enumerate([
            (k_hbm, kwin.at[3]), (q_hbm, q_v), (x_hbm, x_v), (wd_hbm, wd_v), (v_hbm, vwin.at[3]),
            (do_hbm, do_v), (rs_hbm, rs_v), (wq_hbm, wq_v), (wkv_hbm, wkv_v), (flags_hbm, flags),
        ])
    ]
    for copy in loads:
        copy.start()

    pl.semaphore_wait(barrier, len(near) + len(near_heads))

    rounds = []
    step = 2
    while step < nz:
        rounds.append(step)
        step *= 2

    def tell(i):
        if i < len(rounds):
            for by in (2 * rounds[i], -2 * rounds[i]):
                pl.semaphore_signal(
                    known.at[i], inc=1, device_id={"seq": seq_at(by)}, device_id_type=MESH
                )

    def hear(i):
        if i < len(rounds):
            pl.semaphore_wait(known.at[i], 2)

    def tell_heads(i):
        targets = [row_at(1), row_at(-1)] if i == 0 else [other_row]
        if i == 0 or head_count > ROW:
            for target in targets:
                pl.semaphore_signal(
                    known.at[3 + i], inc=1, device_id={"head": target}, device_id_type=MESH
                )

    def hear_heads(i):
        if i == 0 or head_count > ROW:
            pl.semaphore_wait(known.at[3 + i], 2 - i)

    own = (k_hbm, v_hbm)
    win = (kwin, vwin)

    def cross(c):
        return remote(own[c], win[c].at[1], win_ss.at[c, 0], win_rs.at[c, 1], seq_at(2))

    def give(c):
        return remote(own[c], win[c].at[2], win_ss.at[c, 1], win_rs.at[c, 2], sibling)

    def forward(c, slot):
        return remote(win[c].at[1], win[c].at[slot], win_ss.at[c, 2], win_rs.at[c, slot], sibling)

    for c in range(2):
        cross(c).start()

        @pl.when(core == 0)
        def _():
            give(c).start()

    tell(0)
    tell_heads(0)

    def head_copy(src, dst, ss, rs, by):
        return pltpu.make_async_remote_copy(
            src_ref=src, dst_ref=dst.at[by], send_sem=ss.at[by], recv_sem=rs.at[by],
            device_id={"head": head_at(by)}, device_id_type=MESH,
        )

    def head_start(*args):
        for by in range(1, head_count):
            head_copy(*args, by).start()

        def wait():
            for by in range(1, head_count):
                head_copy(*args, by).wait_send()

        pending.append(wait)

    row_id = lax.broadcasted_iota(jnp.int32, (tokens, tokens), 0)
    col_id = lax.broadcasted_iota(jnp.int32, (tokens, tokens), 1)
    causal = jnp.where(row_id <= col_id, 0.0, -BIG).astype(F32)
    want = (1 - x_lo).astype(F32)
    even = (1 - core).astype(F32)
    c2 = scale * LOG2E

    def head_cols(ref, h):
        return ref[:, h * HEAD_SIZE : (h + 1) * HEAD_SIZE]

    def rows(j):
        return pl.ds(j * tokens, tokens)

    def score_block(j):
        for h in range(heads):
            score = dot_nt(kwin[j], head_cols(q_v, h))
            if j == 3:
                score = score + causal
            scores[h, rows(j), :] = score
            tops[j, h : h + 1, :] = jnp.max(score, axis=0, keepdims=True)
        k_t[:, j * tokens : (j + 1) * tokens] = kwin[j].astype(F32).T.astype(BF16)

    loads[0].wait()
    loads[1].wait()
    score_block(3)
    loads[2].wait()
    loads[3].wait()
    down_part = dot_nt(wd_v[...], x_v[...])
    down_send[...] = down_part.astype(BF16)
    hear(0)
    tell(1)
    hear_heads(0)
    tell_heads(1)

    def rest_of_scores(odd):
        if odd:
            give(0).wait_recv()
            score_block(2)
            cross(0).wait_recv()
            forward(0, 2).start()
            score_block(1)
            forward(0, 0).wait_recv()
            score_block(0)
        else:
            cross(0).wait_recv()
            forward(0, 0).start()
            score_block(1)
            forward(0, 2).wait_recv()
            score_block(2)

    def pass_values_on(odd):
        cross(1).wait_recv()
        forward(1, 2 if odd else 0).start()

    def relay_copy(slot, c):
        return remote(
            kv_send.at[slot, c], relay.at[c], relay_ss.at[c], relay_rs.at[c], sibling
        )

    def back_copy(c):
        return remote(
            kv_send.at[1, c], kv_recv.at[0, c], kv_ss.at[c], kv_rs.at[c], seq_at(-2)
        )

    def near_copy():
        return remote(near_send, near_recv, near_ss, near_rs, seq_at(-2))

    def projected(grads):
        return [
            dot_nt(wkv_v[c * RANK : (c + 1) * RANK, :], grads[c]) for c in range(2)
        ]

    def home_copy():
        return remote(kv_send.at[2], kv_recv.at[1], kv_ss.at[2], kv_rs.at[2], sibling)

    def attention(odd):
        order = (0, 1, 2, 3) if odd else (2, 1, 3)

        def weights(h, _):
            differs = flags[h].astype(F32) - want
            far = differs * differs * BIG
            bias = {0: far, 1: far, 2: 0.0 if odd else far, 3: 0.0}
            at = pl.ds(h, 1)
            top = None
            for j in order:
                high = tops[j, at, :] - bias[j]
                top = high if top is None else jnp.maximum(top, high)
            weight = {}
            total = None
            for j in order:
                weight[j] = jnp.exp2(scores[h, rows(j), :] * c2 - (top * c2 + bias[j]))
                part = jnp.sum(weight[j], axis=0, keepdims=True)
                total = part if total is None else total + part
            inverse = 1.0 / total
            for j in order:
                probs[h, rows(j), :] = (weight[j] * inverse).astype(BF16)
            return 0

        lax.fori_loop(0, heads, weights, 0)

    def summed(left, right, j):
        total = None
        for h in range(heads):
            part = dot_nn(left[h, rows(j), :], head_cols(right, h))
            total = part if total is None else total + part
        return total

    def value_grad(j):
        return summed(probs, do_v, j)

    def key_grad(j):
        for h in range(heads):
            p = probs[h, rows(j), :].astype(F32)
            dp = dot_nt(vwin[j], head_cols(do_v, h))
            dscores[h, rows(j), :] = (p * (dp - rs_v[h : h + 1, :])).astype(BF16)
        return summed(dscores, q_v, j) * scale

    def relayed(odd):
        slot = 0 if odd else 2
        if odd:
            forward(1, 0).wait_recv()
        else:
            forward(1, 2).wait_recv()
        kv_send[slot, 1] = value_grad(slot).astype(BF16)
        relay_copy(slot, 1).start()
        kv_send[slot, 0] = key_grad(slot).astype(BF16)
        relay_copy(slot, 0).start()

    def sent_back(c, grad):
        relay_copy(0, c).wait_recv()
        kv_send[1, c] = (grad + relay[c].astype(F32)).astype(BF16)
        if c == 0:
            for i, part in enumerate(projected(kv_send[1])):
                near_send[i * RANK : (i + 1) * RANK, :] = part.astype(BF16)
            near_copy().start()
        back_copy(c).start()

    def split(fn):
        @pl.when(core == 1)
        def _():
            fn(True)

        @pl.when(core == 0)
        def _():
            fn(False)

    split(rest_of_scores)
    hear_heads(1)
    head_start(down_send, down_recv, down_ss, down_rs)
    hear(1)
    tell(2)
    for i in range(4, 10):
        loads[i].wait()
    split(pass_values_on)

    def window_sent(odd):
        for c in range(2):
            cross(c).wait_send()
            forward(c, 2 if odd else 0).wait_send()
            if not odd:
                give(c).wait_send()

    pending.append(lambda: split(window_sent))
    split(attention)
    split(relayed)
    sent_back(1, value_grad(1))
    sent_back(0, key_grad(1))

    @pl.when(core == 1)
    def _():
        give(1).wait_recv()
        kv_send[2, 0] = key_grad(2).astype(BF16)
        kv_send[2, 1] = value_grad(2).astype(BF16)
        home_copy().start()

    own_kv[0] = key_grad(3)
    own_kv[1] = value_grad(3)

    def grads_sent(odd):
        for c in range(2):
            relay_copy(0 if odd else 2, c).wait_send()
            back_copy(c).wait_send()
        near_copy().wait_send()
        if odd:
            home_copy().wait_send()

    pending.append(lambda: split(grads_sent))

    down = down_part
    for by in range(1, head_count):
        head_copy(down_send, down_recv, down_ss, down_rs, by).wait_recv()
        down = down + down_recv[by].astype(F32)
    down_low[...] = down.astype(BF16)

    def query_grads(odd):
        first = 0 if odd else tokens
        per_half = heads // 2
        acc = jnp.zeros((RANK, tokens), F32)
        for h in range(heads):
            dq = (dot_nn(k_t[:, first:], dscores[h, first:, :]) * scale).astype(BF16)
            col = (h % per_half) * HEAD_SIZE
            g_full[h // per_half, :RANK, col : col + HEAD_SIZE] = dot_nt(down_low[:RANK, :], dq)
            acc = acc + dot_nn(head_cols(wq_v, h), dq)
        up_send[:RANK, :] = acc.astype(BF16)

    split(query_grads)
    hear(2)

    @pl.when(core == 0)
    def _():
        home_copy().wait_recv()
        own_kv[...] = own_kv[...] + kv_recv[1].astype(F32)

    own_part = projected(own_kv[...].astype(BF16))
    near_copy().wait_recv()
    for c in range(2):
        at = slice((c + 1) * RANK, (c + 2) * RANK)
        up_send[at, :] = (
            own_part[c] + near_recv[c * RANK : (c + 1) * RANK, :].astype(F32)
        ).astype(BF16)
    head_start(up_send, up_recv, up_ss, up_rs)

    for c in range(2):
        back_copy(c).wait_recv()
    dkv = (own_kv[...] + kv_recv[0].astype(F32)).astype(BF16)
    kv_out[...] = dkv
    placed = [
        pltpu.make_async_copy(src, dst, out_sem.at[i])
        for i, (src, dst) in enumerate([
            (kv_out, kv_hbm), (x_out, xo_hbm), (g_out, g_hbm), (c_out, c_hbm),
        ])
    ]
    placed[0].start()
    pending.append(placed[0].wait)
    for c in range(2):
        c_full[c] = dot_nn(down_low[(c + 1) * RANK : (c + 2) * RANK, :], dkv[c])

    part_rows = 2 * RANK

    def pair_copy(p):
        at = pl.ds(p * part_rows, part_rows)
        return remote(
            g_full.at[1 - core, at], g_pair.at[at], pair_ss.at[p], pair_rs.at[p], sibling
        )

    def pair_copy_c():
        return remote(c_full.at[1 - core], c_pair, pair_ss.at[2], pair_rs.at[2], sibling)

    pair_copy_c().start()
    pending.append(lambda: pair_copy_c().wait_send())

    def far_first(n, i):
        return n // 2 + lax.rem(i + 1, 2) * (i // 2) - lax.rem(i, 2) * ((i + 1) // 2)

    def owner_at(by):
        return lax.rem(zi // stride + by, owners)

    def scatter_copy(p, owner):
        slot = x_lo * nz + zi
        return remote(
            units.at[p, owner], slots.at[slot], rs_ss.at[p, owner], rs_rs.at[slot],
            owner * stride * QUAD + p * 2 + core,
        )

    def arrived(z, x):
        slot = x * nz + z
        remote(units.at[0, 0], slots.at[slot], rs_ss.at[0, 0], rs_rs.at[slot], sibling).wait_recv()
        return slots[slot].astype(F32)

    def loop(first, last, fn):
        def body(i, _):
            fn(i)
            return 0

        lax.fori_loop(first, last, body, 0)

    def is_owner(p):
        return jnp.logical_and(x_lo == p, lax.rem(zi, stride) == 0)

    def each_owner(p, fn):
        loop(0, owners - 1, lambda i: fn(owner_at(far_first(owners, i))))

        @pl.when(jnp.logical_not(is_owner(p)))
        def _():
            fn(zi // stride)

    def scatter(p):
        pair_copy(p).wait_recv()
        at = pl.ds(p * part_rows, part_rows)
        g = (g_full[core, at, :] + g_pair[at, :]).astype(BF16)
        for u in range(UNITS):
            r, col = (u // 4) * 16, (u % 4) * 128
            units[p, u // per_owner, u % per_owner] = g[r : r + 16, col : col + 128]
        each_owner(p, lambda owner: scatter_copy(p, owner).start())
        pending.append(lambda: each_owner(p, lambda owner: scatter_copy(p, owner).wait_send()))

    c_owner = ((nz // 2 + 1) % nz) * QUAD + 2 + core
    is_c_owner = s == c_owner

    def c_copy(slot):
        return remote(c_send, c_slots.at[slot], c_ss, c_rs.at[slot], c_owner)

    pair_copy_c().wait_recv()
    c_sum[...] = c_full[core] + c_pair[...]
    c_send[...] = c_sum[...].astype(BF16)

    @pl.when(jnp.logical_not(is_c_owner))
    def _():
        c_copy(x_lo * nz + zi).start()

    def c_sent():
        @pl.when(jnp.logical_not(is_c_owner))
        def _():
            c_copy(x_lo * nz + zi).wait_send()

    pending.append(c_sent)

    up = up_send[...].astype(F32)
    for by in range(1, head_count):
        head_copy(up_send, up_recv, up_ss, up_rs, by).wait_recv()
        up = up + up_recv[by].astype(F32)
    up_out[...] = up.astype(BF16)

    def down_rows(c):
        g_full[c, RANK:, :] = dot_nn(up_out[...], x_v[:, c * half : (c + 1) * half])

    def pair_sums(side):
        down_rows(1 - side)
        for p in range(2):
            pair_copy(p).start()
        down_rows(side)

    @pl.when(core == 0)
    def _():
        pair_sums(0)

    @pl.when(core == 1)
    def _():
        pair_sums(1)

    for p in range(2):
        pending.append(lambda p=p: pair_copy(p).wait_send())
    for p in range(2):
        scatter(p)

    for c in range(4):
        cols = slice(c * half // 2, (c + 1) * half // 2)
        part = lax.dot_general(
            up_out[...], wd_v[:, cols], (((0,), (0,)), ((), ())), preferred_element_type=F32
        )
        x_out[:, cols] = (ADAPTER_SCALE * part).astype(BF16)
    placed[1].start()
    pending.append(placed[1].wait)

    def unit_ref(p, u):
        return g_low.at[
            pl.ds(pl.multiple_of(p * part_rows + (u // 4) * 16, 16), 16),
            pl.ds(pl.multiple_of(core * half + (u % 4) * 128, 128), 128),
        ]

    def gather_copy(p, owner, i, by, x):
        u = owner * per_owner + i
        ref = unit_ref(p, u)
        return remote(
            ref, ref, ag_ss.at[(x * nz + by) * per_owner + i], ag_rs.at[p, u], chip(by, x)
        )

    def each_target(p, fn):
        loop(0, nz - 1, lambda i: (fn(far_first(nz, i), 0), fn(far_first(nz, i), 1)))
        fn(0, 1 - p)

    def gather(p):
        @pl.when(is_owner(p))
        def _():
            mine = zi // stride
            total = units[p, mine].astype(F32)
            for by in range(0, nz):
                for x in (p, 1 - p):
                    if by == 0 and x == p:
                        continue
                    total = total + arrived(z_at(by), x)
            total = (total * multiplier).astype(BF16)
            for i in range(per_owner):
                unit_ref(p, mine * per_owner + i)[...] = total[i]

            def start(by, x):
                for i in range(per_owner):
                    gather_copy(p, mine, i, by, x).start()

            each_target(p, start)

    def gather_sent():
        for p in range(2):

            @pl.when(is_owner(p))
            def _():
                def wait(by, x):
                    for i in range(per_owner):
                        gather_copy(p, zi // stride, i, by, x).wait_send()

                each_target(p, wait)

    def c_ref():
        return c_low.at[pl.ds(pl.multiple_of(core * RANK, RANK), RANK), :]

    def c_gather_copy(by, x):
        return remote(c_ref(), c_ref(), cag_ss.at[x * nz + by], cag_rs, chip(by, x))

    gather(0)

    @pl.when(is_c_owner)
    def _():
        total = c_sum[...]
        for by in range(0, nz):
            for x in (1, 0):
                if by == 0 and x == 1:
                    continue
                slot = x * nz + z_at(by)
                c_copy(slot).wait_recv()
                total = total + c_slots[slot].astype(F32)
        c_ref()[...] = (total * multiplier).astype(BF16)
        each_target(1, lambda by, x: c_gather_copy(by, x).start())

    def c_gather_sent():
        @pl.when(is_c_owner)
        def _():
            each_target(1, lambda by, x: c_gather_copy(by, x).wait_send())

    gather(1)
    for wait in pending:
        wait()

    def wait_gathered(p):
        def wait(owner):
            for i in range(per_owner):
                gather_copy(p, owner, i, 0, 0).wait_recv()

        each_owner(p, wait)

    def final_copy(p, side):
        ref = g_low.at[
            pl.ds(p * part_rows, part_rows), pl.ds(pl.multiple_of(side * half, 128), half)
        ]
        return remote(ref, ref, fin_ss.at[p], fin_rs.at[p], sibling)

    def final_copy_c(side):
        ref = c_low.at[pl.ds(pl.multiple_of(side * RANK, RANK), RANK), :]
        return remote(ref, ref, fin_ss.at[2], fin_rs.at[2], sibling)

    wait_gathered(0)
    final_copy(0, core).start()

    @pl.when(jnp.logical_not(is_c_owner))
    def _():
        c_gather_copy(0, 0).wait_recv()

    final_copy_c(core).start()
    wait_gathered(1)
    final_copy(1, core).start()

    gather_sent()
    c_gather_sent()
    final_copy_c(1 - core).wait_recv()
    c_out[...] = c_low[...].astype(F32)
    placed[3].start()
    for p in range(2):
        final_copy(p, 1 - core).wait_recv()
    g_out[...] = g_low[...].astype(F32)
    placed[2].start()
    final_copy_c(core).wait_send()
    for p in range(2):
        final_copy(p, core).wait_send()
    placed[3].wait()
    placed[2].wait()


def place(
    kv, x, g, c, down_o, up_q_o, up_kv_o, kv_o, x_o, kv_v, x_v, g_v, c_v, in_sems, out_sems
):
    ways = [
        (x, x_v, [(x_v, x_o)]),
        (g, g_v, [(g_v.at[RANK:], down_o), (g_v.at[:RANK], up_q_o)]),
        (kv, kv_v, [(kv_v, kv_o)]),
        (c, c_v, [(c_v, up_kv_o)]),
    ]
    arriving = [
        pltpu.make_async_copy(src, dst, in_sems.at[i]) for i, (src, dst, _) in enumerate(ways)
    ]
    for copy in arriving:
        copy.start()
    leaving = []
    for copy, (_, _, targets) in zip(arriving, ways):
        copy.wait()
        for src, dst in targets:
            leaving.append(pltpu.make_async_copy(src, dst, out_sems.at[len(leaving)]))
            leaving[-1].start()
    for copy in leaving:
        copy.wait()


def per_device(
    queries, layer_key_rows, layer_value_rows, output_gradient, output_row_sums,
    shifted_head_flags, inputs, adapter_down_weight, query_up_weight, key_value_up_weight,
):
    seq_count = lax.axis_size("seq")
    head_count = lax.axis_size("head")
    tokens, columns = queries.shape
    heads = columns // HEAD_SIZE
    width = inputs.shape[1]
    nz = seq_count // QUAD
    owners = min(nz, UNITS)
    per_owner = UNITS // owners
    flat_down = adapter_down_weight.reshape(3 * RANK, width)
    flat_kv_up = key_value_up_weight.reshape(2 * RANK, HEAD_SIZE)
    vmem = pltpu.VMEM
    sem = pltpu.SemaphoreType.DMA
    anywhere = pl.BlockSpec(memory_space=pltpu.HBM)
    parts = pl.pallas_call(
        functools.partial(kernel, seq_count, head_count),
        out_shape=(
            jax.ShapeDtypeStruct((2, tokens, HEAD_SIZE), BF16),
            jax.ShapeDtypeStruct((tokens, width), BF16),
            jax.ShapeDtypeStruct((4 * RANK, width), F32),
            jax.ShapeDtypeStruct((2 * RANK, HEAD_SIZE), F32),
        ),
        in_specs=[anywhere] * 10,
        out_specs=(anywhere,) * 4,
        scratch_shapes=[
            vmem((2, tokens, HEAD_SIZE), BF16),
            vmem((tokens, width), BF16),
            vmem((4 * RANK, width), F32),
            vmem((2 * RANK, HEAD_SIZE), F32),
            vmem((4 * RANK, width), BF16),
            vmem((2 * RANK, HEAD_SIZE), BF16),
            vmem((3 * RANK, tokens), BF16),
            vmem((tokens, columns), BF16),
            vmem((tokens, columns), BF16),
            vmem((tokens, width), BF16),
            vmem((3 * RANK, width), BF16),
            vmem((RANK, columns), BF16),
            vmem((2 * RANK, HEAD_SIZE), BF16),
            vmem((heads, tokens), F32),
            vmem((4, tokens, HEAD_SIZE), BF16),
            vmem((4, tokens, HEAD_SIZE), BF16),
            vmem((HEAD_SIZE, 4 * tokens), BF16),
            vmem((heads, 4 * tokens, tokens), F32),
            vmem((4, heads, tokens), F32),
            vmem((heads, 4 * tokens, tokens), BF16),
            vmem((heads, 4 * tokens, tokens), BF16),
            vmem((2, tokens, HEAD_SIZE), F32),
            vmem((3, 2, tokens, HEAD_SIZE), BF16),
            vmem((2, 2, tokens, HEAD_SIZE), BF16),
            vmem((2, tokens, HEAD_SIZE), BF16),
            pltpu.SMEM((heads,), jnp.int32),
            vmem((3 * RANK, tokens), BF16),
            vmem((head_count, 3 * RANK, tokens), BF16),
            vmem((3 * RANK, tokens), BF16),
            vmem((3 * RANK, tokens), BF16),
            vmem((head_count, 3 * RANK, tokens), BF16),
            vmem((2 * RANK, tokens), BF16),
            vmem((2 * RANK, tokens), BF16),
            vmem((2, 4 * RANK, width // 2), F32),
            vmem((4 * RANK, width // 2), F32),
            vmem((2, RANK, HEAD_SIZE), F32),
            vmem((RANK, HEAD_SIZE), F32),
            vmem((2, owners, per_owner, 16, 128), BF16),
            vmem((2 * nz, per_owner, 16, 128), BF16),
            vmem((RANK, HEAD_SIZE), F32),
            vmem((RANK, HEAD_SIZE), BF16),
            vmem((2 * nz, RANK, HEAD_SIZE), BF16),
            sem((10,)), sem((4,)),
            sem((2, 3)), sem((2, 4)),
            sem((head_count,)), sem((head_count,)),
            sem((head_count,)), sem((head_count,)),
            sem, sem,
            sem((2,)), sem((2,)),
            sem((3,)), sem((3,)),
            sem((3,)), sem((3,)),
            sem((2, owners)), sem((2 * nz,)),
            sem, sem((2 * nz,)),
            sem((2 * nz * per_owner,)), sem((2, UNITS)),
            sem((2 * nz,)), sem,
            sem((3,)), sem((3,)),
            pltpu.SemaphoreType.REGULAR((5,)),
        ],
        compiler_params=pltpu.CompilerParams(
            collective_id=0, has_side_effects=True, vmem_limit_bytes=VMEM_BYTES
        ),
    )(
        queries, layer_key_rows, layer_value_rows, output_gradient, output_row_sums,
        shifted_head_flags, inputs, flat_down, query_up_weight, flat_kv_up,
    )
    down_gradient, grad_up_q, grad_up_kv, kv_gradient, grad_inputs = pl.pallas_call(
        place,
        out_shape=(
            jax.ShapeDtypeStruct((3 * RANK, width), F32),
            jax.ShapeDtypeStruct((RANK, columns), F32),
            jax.ShapeDtypeStruct((2 * RANK, HEAD_SIZE), F32),
            jax.ShapeDtypeStruct((2, tokens, HEAD_SIZE), BF16),
            jax.ShapeDtypeStruct((tokens, width), BF16),
        ),
        in_specs=[anywhere] * 4,
        out_specs=(anywhere,) * 5,
        scratch_shapes=[
            vmem((2, tokens, HEAD_SIZE), BF16),
            vmem((tokens, width), BF16),
            vmem((4 * RANK, width), F32),
            vmem((2 * RANK, HEAD_SIZE), F32),
            sem((4,)),
            sem((5,)),
        ],
        compiler_params=pltpu.CompilerParams(vmem_limit_bytes=VMEM_BYTES),
    )(*parts)
    return (
        grad_inputs,
        kv_gradient,
        down_gradient.reshape(3, RANK, width),
        grad_up_q,
        grad_up_kv.reshape(2, RANK, HEAD_SIZE),
    )


def solution(mesh):
    placed = (
        P("seq", "head"),
        P("seq", "head"),
        P("seq", "head"),
        P("seq", "head"),
        P("head", "seq"),
        P("head"),
        P("seq", "head"),
        P(None, None, "head"),
        P(None, "head"),
        P(None, None, "head"),
    )
    return jax.shard_map(
        per_device,
        mesh=mesh,
        in_specs=placed,
        out_specs=(
            P("seq", "head"),
            P(None, "seq", "head"),
            P(None, None, "head"),
            P(None, "head"),
            P(None, None, "head"),
        ),
        check_vma=False,
    )
```

```python
import functools
import math

import jax
import jax.numpy as jnp
from jax import lax
from jax.experimental import pallas as pl
from jax.experimental.pallas import tpu as pltpu
from jax.sharding import PartitionSpec as P

HEAD_SIZE = 128
GROUP = 1024
RANK = 16
QUAD = 4
ROW = 4
UNITS = 4
LOG2E = 1.4426950408889634
BIG = 1e30
ADAPTER_SCALE = 2.0
VMEM_BYTES = 63 * 1024 * 1024

MESH = pl.DeviceIdType.MESH
F32 = jnp.float32
BF16 = jnp.bfloat16


def dot_nn(a, b):
    return lax.dot_general(a, b, (((1,), (0,)), ((), ())), preferred_element_type=F32)


def dot_nt(a, b):
    return lax.dot_general(a, b, (((1,), (1,)), ((), ())), preferred_element_type=F32)


def kernel(
    seq_count,
    head_count,
    q_hbm, k_hbm, v_hbm, do_hbm, rs_hbm, flags_hbm, x_hbm, wd_hbm, wq_hbm, wkv_hbm,
    kv_hbm, xo_hbm, g_hbm, c_hbm,
    kv_out, x_out, g_out, c_out, g_low, c_low, up_out, q_v, do_v, x_v, wd_v, wq_v, wkv_v, rs_v,
    kwin, vwin, k_t, scores, tops, probs, dscores, own_kv, kv_send, kv_recv, relay,
    flags, down_send, down_recv, down_low, up_send, up_recv, near_send, near_recv,
    g_full, g_pair, c_full, c_pair, units, slots, c_sum, c_send, c_slots,
    load_sem, out_sem, win_ss, win_rs, down_ss, down_rs, up_ss, up_rs, near_ss, near_rs,
    relay_ss, relay_rs, kv_ss, kv_rs, pair_ss, pair_rs, rs_ss, rs_rs, c_ss, c_rs,
    ag_ss, ag_rs, cag_ss, cag_rs, fin_ss, fin_rs, known,
):
    tokens = q_v.shape[0]
    heads = q_v.shape[1] // HEAD_SIZE
    nz = seq_count // QUAD
    owners = min(nz, UNITS)
    stride = nz // owners
    per_owner = UNITS // owners
    half = x_v.shape[1] // 2
    s = lax.axis_index("seq")
    hd = lax.axis_index("head")
    zi = s // QUAD
    core = s % 2
    x_lo = (s % QUAD) // 2
    sibling = s + 1 - 2 * core
    scale = HEAD_SIZE ** -0.5
    multiplier = ADAPTER_SCALE / math.sqrt(tokens * seq_count)
    pending = []

    def seq_at(by):
        return lax.rem(s + by + seq_count, seq_count)

    def head_at(by):
        return lax.rem(hd + by + head_count, head_count)

    in_row = min(ROW, head_count)

    def row_at(by):
        return hd // in_row * in_row + lax.rem(hd % in_row + by + in_row, in_row)

    other_row = lax.rem(hd + in_row, head_count)

    def z_at(by):
        return lax.rem(zi + by + nz, nz)

    def chip(by, x):
        return z_at(by) * QUAD + x * 2 + core

    def remote(src, dst, ss, rs, target):
        return pltpu.make_async_remote_copy(
            src_ref=src, dst_ref=dst, send_sem=ss, recv_sem=rs,
            device_id={"seq": target}, device_id_type=MESH,
        )

    barrier = pltpu.get_barrier_semaphore()
    near = [sibling, seq_at(2), seq_at(-2), seq_at(4), seq_at(-4)]
    for target in near:
        pl.semaphore_signal(barrier, inc=1, device_id={"seq": target}, device_id_type=MESH)
    near_heads = [row_at(1), row_at(-1)] + ([other_row] if head_count > ROW else [])
    for target in near_heads:
        pl.semaphore_signal(barrier, inc=1, device_id={"head": target}, device_id_type=MESH)

    loads = [
        pltpu.make_async_copy(src, dst, load_sem.at[i])
        for i, (src, dst) in enumerate([
            (k_hbm, kwin.at[3]), (q_hbm, q_v), (x_hbm, x_v), (wd_hbm, wd_v), (v_hbm, vwin.at[3]),
            (do_hbm, do_v), (rs_hbm, rs_v), (wq_hbm, wq_v), (wkv_hbm, wkv_v), (flags_hbm, flags),
        ])
    ]
    for copy in loads:
        copy.start()

    pl.semaphore_wait(barrier, len(near) + len(near_heads))

    rounds = []
    step = 2
    while step < nz:
        rounds.append(step)
        step *= 2

    def tell(i):
        if i < len(rounds):
            for by in (2 * rounds[i], -2 * rounds[i]):
                pl.semaphore_signal(
                    known.at[i], inc=1, device_id={"seq": seq_at(by)}, device_id_type=MESH
                )

    def hear(i):
        if i < len(rounds):
            pl.semaphore_wait(known.at[i], 2)

    def tell_heads(i):
        targets = [row_at(1), row_at(-1)] if i == 0 else [other_row]
        if i == 0 or head_count > ROW:
            for target in targets:
                pl.semaphore_signal(
                    known.at[3 + i], inc=1, device_id={"head": target}, device_id_type=MESH
                )

    def hear_heads(i):
        if i == 0 or head_count > ROW:
            pl.semaphore_wait(known.at[3 + i], 2 - i)

    own = (k_hbm, v_hbm)
    win = (kwin, vwin)

    def cross(c):
        return remote(own[c], win[c].at[1], win_ss.at[c, 0], win_rs.at[c, 1], seq_at(2))

    def give(c):
        return remote(own[c], win[c].at[2], win_ss.at[c, 1], win_rs.at[c, 2], sibling)

    def forward(c, slot):
        return remote(win[c].at[1], win[c].at[slot], win_ss.at[c, 2], win_rs.at[c, slot], sibling)

    for c in range(2):
        cross(c).start()

        @pl.when(core == 0)
        def _():
            give(c).start()

    tell(0)
    tell_heads(0)

    def head_copy(src, dst, ss, rs, by):
        return pltpu.make_async_remote_copy(
            src_ref=src, dst_ref=dst.at[by], send_sem=ss.at[by], recv_sem=rs.at[by],
            device_id={"head": head_at(by)}, device_id_type=MESH,
        )

    def head_start(*args):
        for by in range(1, head_count):
            head_copy(*args, by).start()

        def wait():
            for by in range(1, head_count):
                head_copy(*args, by).wait_send()

        pending.append(wait)

    row_id = lax.broadcasted_iota(jnp.int32, (tokens, tokens), 0)
    col_id = lax.broadcasted_iota(jnp.int32, (tokens, tokens), 1)
    causal = jnp.where(row_id <= col_id, 0.0, -BIG).astype(F32)
    want = (1 - x_lo).astype(F32)
    even = (1 - core).astype(F32)
    c2 = scale * LOG2E

    def head_cols(ref, h):
        return ref[:, h * HEAD_SIZE : (h + 1) * HEAD_SIZE]

    def rows(j):
        return pl.ds(j * tokens, tokens)

    def score_block(j):
        for h in range(heads):
            score = dot_nt(kwin[j], head_cols(q_v, h))
            if j == 3:
                score = score + causal
            scores[h, rows(j), :] = score
            tops[j, h : h + 1, :] = jnp.max(score, axis=0, keepdims=True)
        k_t[:, j * tokens : (j + 1) * tokens] = kwin[j].astype(F32).T.astype(BF16)

    loads[0].wait()
    loads[1].wait()
    score_block(3)
    loads[2].wait()
    loads[3].wait()
    down_part = dot_nt(wd_v[...], x_v[...])
    down_send[...] = down_part.astype(BF16)
    hear(0)
    tell(1)
    hear_heads(0)
    tell_heads(1)

    def rest_of_scores(odd):
        if odd:
            give(0).wait_recv()
            score_block(2)
            cross(0).wait_recv()
            forward(0, 2).start()
            score_block(1)
            forward(0, 0).wait_recv()
            score_block(0)
        else:
            cross(0).wait_recv()
            forward(0, 0).start()
            score_block(1)
            forward(0, 2).wait_recv()
            score_block(2)

    def pass_values_on(odd):
        cross(1).wait_recv()
        forward(1, 2 if odd else 0).start()

    def relay_copy(slot, c):
        return remote(
            kv_send.at[slot, c], relay.at[c], relay_ss.at[c], relay_rs.at[c], sibling
        )

    def back_copy(c):
        return remote(
            kv_send.at[1, c], kv_recv.at[0, c], kv_ss.at[c], kv_rs.at[c], seq_at(-2)
        )

    def near_copy():
        return remote(near_send, near_recv, near_ss, near_rs, seq_at(-2))

    def projected(grads):
        return [
            dot_nt(wkv_v[c * RANK : (c + 1) * RANK, :], grads[c]) for c in range(2)
        ]

    def home_copy():
        return remote(kv_send.at[2], kv_recv.at[1], kv_ss.at[2], kv_rs.at[2], sibling)

    def attention(odd):
        order = (0, 1, 2, 3) if odd else (2, 1, 3)

        def weights(h, _):
            differs = flags[h].astype(F32) - want
            far = differs * differs * BIG
            bias = {0: far, 1: far, 2: 0.0 if odd else far, 3: 0.0}
            at = pl.ds(h, 1)
            top = None
            for j in order:
                high = tops[j, at, :] - bias[j]
                top = high if top is None else jnp.maximum(top, high)
            weight = {}
            total = None
            for j in order:
                weight[j] = jnp.exp2(scores[h, rows(j), :] * c2 - (top * c2 + bias[j]))
                part = jnp.sum(weight[j], axis=0, keepdims=True)
                total = part if total is None else total + part
            inverse = 1.0 / total
            for j in order:
                probs[h, rows(j), :] = (weight[j] * inverse).astype(BF16)
            return 0

        lax.fori_loop(0, heads, weights, 0)

    def summed(left, right, j):
        total = None
        for h in range(heads):
            part = dot_nn(left[h, rows(j), :], head_cols(right, h))
            total = part if total is None else total + part
        return total

    def value_grad(j):
        return summed(probs, do_v, j)

    def key_grad(j):
        for h in range(heads):
            p = probs[h, rows(j), :].astype(F32)
            dp = dot_nt(vwin[j], head_cols(do_v, h))
            dscores[h, rows(j), :] = (p * (dp - rs_v[h : h + 1, :])).astype(BF16)
        return summed(dscores, q_v, j) * scale

    def relayed(odd):
        slot = 0 if odd else 2
        if odd:
            forward(1, 0).wait_recv()
        else:
            forward(1, 2).wait_recv()
        kv_send[slot, 1] = value_grad(slot).astype(BF16)
        relay_copy(slot, 1).start()
        kv_send[slot, 0] = key_grad(slot).astype(BF16)
        relay_copy(slot, 0).start()

    def sent_back(c, grad):
        relay_copy(0, c).wait_recv()
        kv_send[1, c] = (grad + relay[c].astype(F32)).astype(BF16)
        if c == 0:
            for i, part in enumerate(projected(kv_send[1])):
                near_send[i * RANK : (i + 1) * RANK, :] = part.astype(BF16)
            near_copy().start()
        back_copy(c).start()

    def split(fn):
        @pl.when(core == 1)
        def _():
            fn(True)

        @pl.when(core == 0)
        def _():
            fn(False)

    split(rest_of_scores)
    hear_heads(1)
    head_start(down_send, down_recv, down_ss, down_rs)
    hear(1)
    tell(2)
    for i in range(4, 10):
        loads[i].wait()
    split(pass_values_on)

    def window_sent(odd):
        for c in range(2):
            cross(c).wait_send()
            forward(c, 2 if odd else 0).wait_send()
            if not odd:
                give(c).wait_send()

    pending.append(lambda: split(window_sent))
    split(attention)
    split(relayed)
    sent_back(1, value_grad(1))
    sent_back(0, key_grad(1))

    @pl.when(core == 1)
    def _():
        give(1).wait_recv()
        kv_send[2, 0] = key_grad(2).astype(BF16)
        kv_send[2, 1] = value_grad(2).astype(BF16)
        home_copy().start()

    own_kv[0] = key_grad(3)
    own_kv[1] = value_grad(3)

    def grads_sent(odd):
        for c in range(2):
            relay_copy(0 if odd else 2, c).wait_send()
            back_copy(c).wait_send()
        near_copy().wait_send()
        if odd:
            home_copy().wait_send()

    pending.append(lambda: split(grads_sent))

    down = down_part
    for by in range(1, head_count):
        head_copy(down_send, down_recv, down_ss, down_rs, by).wait_recv()
        down = down + down_recv[by].astype(F32)
    down_low[...] = down.astype(BF16)

    def query_grads(odd):
        first = 0 if odd else tokens
        per_half = heads // 2
        acc = jnp.zeros((RANK, tokens), F32)
        for h in range(heads):
            dq = (dot_nn(k_t[:, first:], dscores[h, first:, :]) * scale).astype(BF16)
            col = (h % per_half) * HEAD_SIZE
            g_full[h // per_half, :RANK, col : col + HEAD_SIZE] = dot_nt(down_low[:RANK, :], dq)
            acc = acc + dot_nn(head_cols(wq_v, h), dq)
        up_send[:RANK, :] = acc.astype(BF16)

    split(query_grads)
    hear(2)

    @pl.when(core == 0)
    def _():
        home_copy().wait_recv()
        own_kv[...] = own_kv[...] + kv_recv[1].astype(F32)

    own_part = projected(own_kv[...].astype(BF16))
    near_copy().wait_recv()
    for c in range(2):
        at = slice((c + 1) * RANK, (c + 2) * RANK)
        up_send[at, :] = (
            own_part[c] + near_recv[c * RANK : (c + 1) * RANK, :].astype(F32)
        ).astype(BF16)
    head_start(up_send, up_recv, up_ss, up_rs)

    for c in range(2):
        back_copy(c).wait_recv()
    dkv = (own_kv[...] + kv_recv[0].astype(F32)).astype(BF16)
    kv_out[...] = dkv
    placed = [
        pltpu.make_async_copy(src, dst, out_sem.at[i])
        for i, (src, dst) in enumerate([
            (kv_out, kv_hbm), (x_out, xo_hbm), (g_out, g_hbm), (c_out, c_hbm),
        ])
    ]
    placed[0].start()
    pending.append(placed[0].wait)
    for c in range(2):
        c_full[c] = dot_nn(down_low[(c + 1) * RANK : (c + 2) * RANK, :], dkv[c])

    part_rows = 2 * RANK

    def pair_copy(p):
        at = pl.ds(p * part_rows, part_rows)
        return remote(
            g_full.at[1 - core, at], g_pair.at[at], pair_ss.at[p], pair_rs.at[p], sibling
        )

    def pair_copy_c():
        return remote(c_full.at[1 - core], c_pair, pair_ss.at[2], pair_rs.at[2], sibling)

    pair_copy_c().start()
    pending.append(lambda: pair_copy_c().wait_send())

    def far_first(n, i):
        return n // 2 + lax.rem(i + 1, 2) * (i // 2) - lax.rem(i, 2) * ((i + 1) // 2)

    def owner_at(by):
        return lax.rem(zi // stride + by, owners)

    def scatter_copy(p, owner):
        slot = x_lo * nz + zi
        return remote(
            units.at[p, owner], slots.at[slot], rs_ss.at[p, owner], rs_rs.at[slot],
            (owner * stride + p * (stride // 2)) * QUAD + p * 2 + core,
        )

    def arrived(z, x):
        slot = x * nz + z
        remote(units.at[0, 0], slots.at[slot], rs_ss.at[0, 0], rs_rs.at[slot], sibling).wait_recv()
        return slots[slot].astype(F32)

    def loop(first, last, fn):
        def body(i, _):
            fn(i)
            return 0

        lax.fori_loop(first, last, body, 0)

    def is_owner(p):
        return jnp.logical_and(x_lo == p, lax.rem(zi, stride) == p * (stride // 2))

    def each_owner(p, fn):
        loop(0, owners - 1, lambda i: fn(owner_at(far_first(owners, i))))

        @pl.when(jnp.logical_not(is_owner(p)))
        def _():
            fn(zi // stride)

    def scatter(p):
        pair_copy(p).wait_recv()
        at = pl.ds(p * part_rows, part_rows)
        g = (g_full[core, at, :] + g_pair[at, :]).astype(BF16)
        for u in range(UNITS):
            units[p, u // per_owner, u % per_owner] = g[:, u * 128 : (u + 1) * 128]
        each_owner(p, lambda owner: scatter_copy(p, owner).start())
        pending.append(lambda: each_owner(p, lambda owner: scatter_copy(p, owner).wait_send()))

    c_owner = ((nz // 2 + 1) % nz) * QUAD + 2 + core
    is_c_owner = s == c_owner

    def c_copy(slot):
        return remote(c_send, c_slots.at[slot], c_ss, c_rs.at[slot], c_owner)

    pair_copy_c().wait_recv()
    c_sum[...] = c_full[core] + c_pair[...]
    c_send[...] = c_sum[...].astype(BF16)

    @pl.when(jnp.logical_not(is_c_owner))
    def _():
        c_copy(x_lo * nz + zi).start()

    def c_sent():
        @pl.when(jnp.logical_not(is_c_owner))
        def _():
            c_copy(x_lo * nz + zi).wait_send()

    pending.append(c_sent)

    up = up_send[...].astype(F32)
    for by in range(1, head_count):
        head_copy(up_send, up_recv, up_ss, up_rs, by).wait_recv()
        up = up + up_recv[by].astype(F32)
    up_out[...] = up.astype(BF16)

    def down_rows(c):
        g_full[c, RANK:, :] = dot_nn(up_out[...], x_v[:, c * half : (c + 1) * half])

    def pair_sums(side):
        down_rows(1 - side)
        for p in range(2):
            pair_copy(p).start()
        down_rows(side)

    @pl.when(core == 0)
    def _():
        pair_sums(0)

    @pl.when(core == 1)
    def _():
        pair_sums(1)

    for p in range(2):
        pending.append(lambda p=p: pair_copy(p).wait_send())
    for p in range(2):
        scatter(p)

    for c in range(4):
        cols = slice(c * half // 2, (c + 1) * half // 2)
        part = lax.dot_general(
            up_out[...], wd_v[:, cols], (((0,), (0,)), ((), ())), preferred_element_type=F32
        )
        x_out[:, cols] = (ADAPTER_SCALE * part).astype(BF16)
    placed[1].start()
    pending.append(placed[1].wait)

    def unit_ref(p, u):
        return g_low.at[
            pl.ds(p * part_rows, part_rows),
            pl.ds(pl.multiple_of(core * half + u * 128, 128), 128),
        ]

    def gather_copy(p, owner, i, by, x):
        u = owner * per_owner + i
        ref = unit_ref(p, u)
        return remote(
            ref, ref, ag_ss.at[(x * nz + by) * per_owner + i], ag_rs.at[p, u], chip(by, x)
        )

    def each_target(p, fn):
        loop(0, nz - 1, lambda i: (fn(far_first(nz, i), 0), fn(far_first(nz, i), 1)))
        fn(0, 1 - p)

    def gather(p):
        @pl.when(is_owner(p))
        def _():
            mine = zi // stride
            total = units[p, mine].astype(F32)
            for by in range(0, nz):
                for x in (p, 1 - p):
                    if by == 0 and x == p:
                        continue
                    total = total + arrived(z_at(by), x)
            total = (total * multiplier).astype(BF16)
            for i in range(per_owner):
                unit_ref(p, mine * per_owner + i)[...] = total[i]

            def start(by, x):
                for i in range(per_owner):
                    gather_copy(p, mine, i, by, x).start()

            each_target(p, start)

    def gather_sent():
        for p in range(2):

            @pl.when(is_owner(p))
            def _():
                def wait(by, x):
                    for i in range(per_owner):
                        gather_copy(p, zi // stride, i, by, x).wait_send()

                each_target(p, wait)

    def c_ref():
        return c_low.at[pl.ds(pl.multiple_of(core * RANK, RANK), RANK), :]

    def c_gather_copy(by, x):
        return remote(c_ref(), c_ref(), cag_ss.at[x * nz + by], cag_rs, chip(by, x))

    gather(0)

    @pl.when(is_c_owner)
    def _():
        total = c_sum[...]
        for by in range(0, nz):
            for x in (1, 0):
                if by == 0 and x == 1:
                    continue
                slot = x * nz + z_at(by)
                c_copy(slot).wait_recv()
                total = total + c_slots[slot].astype(F32)
        c_ref()[...] = (total * multiplier).astype(BF16)
        each_target(1, lambda by, x: c_gather_copy(by, x).start())

    def c_gather_sent():
        @pl.when(is_c_owner)
        def _():
            each_target(1, lambda by, x: c_gather_copy(by, x).wait_send())

    gather(1)
    for wait in pending:
        wait()

    def wait_gathered(p):
        def wait(owner):
            for i in range(per_owner):
                gather_copy(p, owner, i, 0, 0).wait_recv()

        each_owner(p, wait)

    def final_copy(p, side):
        ref = g_low.at[
            pl.ds(p * part_rows, part_rows), pl.ds(pl.multiple_of(side * half, 128), half)
        ]
        return remote(ref, ref, fin_ss.at[p], fin_rs.at[p], sibling)

    def final_copy_c(side):
        ref = c_low.at[pl.ds(pl.multiple_of(side * RANK, RANK), RANK), :]
        return remote(ref, ref, fin_ss.at[2], fin_rs.at[2], sibling)

    wait_gathered(0)
    final_copy(0, core).start()

    @pl.when(jnp.logical_not(is_c_owner))
    def _():
        c_gather_copy(0, 0).wait_recv()

    final_copy_c(core).start()
    wait_gathered(1)
    final_copy(1, core).start()

    gather_sent()
    c_gather_sent()
    final_copy_c(1 - core).wait_recv()
    c_out[...] = c_low[...].astype(F32)
    placed[3].start()
    for p in range(2):
        final_copy(p, 1 - core).wait_recv()
    g_out[...] = g_low[...].astype(F32)
    placed[2].start()
    final_copy_c(core).wait_send()
    for p in range(2):
        final_copy(p, core).wait_send()
    placed[3].wait()
    placed[2].wait()


def place(
    kv, x, g, c, down_o, up_q_o, up_kv_o, kv_o, x_o, kv_v, x_v, g_v, c_v, in_sems, out_sems
):
    ways = [
        (x, x_v, [(x_v, x_o)]),
        (g, g_v, [(g_v.at[RANK:], down_o), (g_v.at[:RANK], up_q_o)]),
        (kv, kv_v, [(kv_v, kv_o)]),
        (c, c_v, [(c_v, up_kv_o)]),
    ]
    arriving = [
        pltpu.make_async_copy(src, dst, in_sems.at[i]) for i, (src, dst, _) in enumerate(ways)
    ]
    for copy in arriving:
        copy.start()
    leaving = []
    for copy, (_, _, targets) in zip(arriving, ways):
        copy.wait()
        for src, dst in targets:
            leaving.append(pltpu.make_async_copy(src, dst, out_sems.at[len(leaving)]))
            leaving[-1].start()
    for copy in leaving:
        copy.wait()


def per_device(
    queries, layer_key_rows, layer_value_rows, output_gradient, output_row_sums,
    shifted_head_flags, inputs, adapter_down_weight, query_up_weight, key_value_up_weight,
):
    seq_count = lax.axis_size("seq")
    head_count = lax.axis_size("head")
    tokens, columns = queries.shape
    heads = columns // HEAD_SIZE
    width = inputs.shape[1]
    nz = seq_count // QUAD
    owners = min(nz, UNITS)
    per_owner = UNITS // owners
    flat_down = adapter_down_weight.reshape(3 * RANK, width)
    flat_kv_up = key_value_up_weight.reshape(2 * RANK, HEAD_SIZE)
    vmem = pltpu.VMEM
    sem = pltpu.SemaphoreType.DMA
    anywhere = pl.BlockSpec(memory_space=pltpu.HBM)
    parts = pl.pallas_call(
        functools.partial(kernel, seq_count, head_count),
        out_shape=(
            jax.ShapeDtypeStruct((2, tokens, HEAD_SIZE), BF16),
            jax.ShapeDtypeStruct((tokens, width), BF16),
            jax.ShapeDtypeStruct((4 * RANK, width), F32),
            jax.ShapeDtypeStruct((2 * RANK, HEAD_SIZE), F32),
        ),
        in_specs=[anywhere] * 10,
        out_specs=(anywhere,) * 4,
        scratch_shapes=[
            vmem((2, tokens, HEAD_SIZE), BF16),
            vmem((tokens, width), BF16),
            vmem((4 * RANK, width), F32),
            vmem((2 * RANK, HEAD_SIZE), F32),
            vmem((4 * RANK, width), BF16),
            vmem((2 * RANK, HEAD_SIZE), BF16),
            vmem((3 * RANK, tokens), BF16),
            vmem((tokens, columns), BF16),
            vmem((tokens, columns), BF16),
            vmem((tokens, width), BF16),
            vmem((3 * RANK, width), BF16),
            vmem((RANK, columns), BF16),
            vmem((2 * RANK, HEAD_SIZE), BF16),
            vmem((heads, tokens), F32),
            vmem((4, tokens, HEAD_SIZE), BF16),
            vmem((4, tokens, HEAD_SIZE), BF16),
            vmem((HEAD_SIZE, 4 * tokens), BF16),
            vmem((heads, 4 * tokens, tokens), F32),
            vmem((4, heads, tokens), F32),
            vmem((heads, 4 * tokens, tokens), BF16),
            vmem((heads, 4 * tokens, tokens), BF16),
            vmem((2, tokens, HEAD_SIZE), F32),
            vmem((3, 2, tokens, HEAD_SIZE), BF16),
            vmem((2, 2, tokens, HEAD_SIZE), BF16),
            vmem((2, tokens, HEAD_SIZE), BF16),
            pltpu.SMEM((heads,), jnp.int32),
            vmem((3 * RANK, tokens), BF16),
            vmem((head_count, 3 * RANK, tokens), BF16),
            vmem((3 * RANK, tokens), BF16),
            vmem((3 * RANK, tokens), BF16),
            vmem((head_count, 3 * RANK, tokens), BF16),
            vmem((2 * RANK, tokens), BF16),
            vmem((2 * RANK, tokens), BF16),
            vmem((2, 4 * RANK, width // 2), F32),
            vmem((4 * RANK, width // 2), F32),
            vmem((2, RANK, HEAD_SIZE), F32),
            vmem((RANK, HEAD_SIZE), F32),
            vmem((2, owners, per_owner, 2 * RANK, 128), BF16),
            vmem((2 * nz, per_owner, 2 * RANK, 128), BF16),
            vmem((RANK, HEAD_SIZE), F32),
            vmem((RANK, HEAD_SIZE), BF16),
            vmem((2 * nz, RANK, HEAD_SIZE), BF16),
            sem((10,)), sem((4,)),
            sem((2, 3)), sem((2, 4)),
            sem((head_count,)), sem((head_count,)),
            sem((head_count,)), sem((head_count,)),
            sem, sem,
            sem((2,)), sem((2,)),
            sem((3,)), sem((3,)),
            sem((3,)), sem((3,)),
            sem((2, owners)), sem((2 * nz,)),
            sem, sem((2 * nz,)),
            sem((2 * nz * per_owner,)), sem((2, UNITS)),
            sem((2 * nz,)), sem,
            sem((3,)), sem((3,)),
            pltpu.SemaphoreType.REGULAR((5,)),
        ],
        compiler_params=pltpu.CompilerParams(
            collective_id=0, has_side_effects=True, vmem_limit_bytes=VMEM_BYTES
        ),
    )(
        queries, layer_key_rows, layer_value_rows, output_gradient, output_row_sums,
        shifted_head_flags, inputs, flat_down, query_up_weight, flat_kv_up,
    )
    down_gradient, grad_up_q, grad_up_kv, kv_gradient, grad_inputs = pl.pallas_call(
        place,
        out_shape=(
            jax.ShapeDtypeStruct((3 * RANK, width), F32),
            jax.ShapeDtypeStruct((RANK, columns), F32),
            jax.ShapeDtypeStruct((2 * RANK, HEAD_SIZE), F32),
            jax.ShapeDtypeStruct((2, tokens, HEAD_SIZE), BF16),
            jax.ShapeDtypeStruct((tokens, width), BF16),
        ),
        in_specs=[anywhere] * 4,
        out_specs=(anywhere,) * 5,
        scratch_shapes=[
            vmem((2, tokens, HEAD_SIZE), BF16),
            vmem((tokens, width), BF16),
            vmem((4 * RANK, width), F32),
            vmem((2 * RANK, HEAD_SIZE), F32),
            sem((4,)),
            sem((5,)),
        ],
        compiler_params=pltpu.CompilerParams(vmem_limit_bytes=VMEM_BYTES),
    )(*parts)
    return (
        grad_inputs,
        kv_gradient,
        down_gradient.reshape(3, RANK, width),
        grad_up_q,
        grad_up_kv.reshape(2, RANK, HEAD_SIZE),
    )


def solution(mesh):
    placed = (
        P("seq", "head"),
        P("seq", "head"),
        P("seq", "head"),
        P("seq", "head"),
        P("head", "seq"),
        P("head"),
        P("seq", "head"),
        P(None, None, "head"),
        P(None, "head"),
        P(None, None, "head"),
    )
    return jax.shard_map(
        per_device,
        mesh=mesh,
        in_specs=placed,
        out_specs=(
            P("seq", "head"),
            P(None, "seq", "head"),
            P(None, None, "head"),
            P(None, "head"),
            P(None, None, "head"),
        ),
        check_vma=False,
    )
```

```python
import functools
import math

import jax
import jax.numpy as jnp
from jax import lax
from jax.experimental import pallas as pl
from jax.experimental.pallas import tpu as pltpu
from jax.sharding import PartitionSpec as P

HEAD_SIZE = 128
GROUP = 1024
RANK = 16
QUAD = 4
ROW = 4
UNITS = 4
LOG2E = 1.4426950408889634
BIG = 1e30
ADAPTER_SCALE = 2.0
VMEM_BYTES = 63 * 1024 * 1024

MESH = pl.DeviceIdType.MESH
F32 = jnp.float32
BF16 = jnp.bfloat16


def dot_nn(a, b):
    return lax.dot_general(a, b, (((1,), (0,)), ((), ())), preferred_element_type=F32)


def dot_nt(a, b):
    return lax.dot_general(a, b, (((1,), (1,)), ((), ())), preferred_element_type=F32)


def kernel(
    seq_count,
    head_count,
    q_hbm, k_hbm, v_hbm, do_hbm, rs_hbm, flags_hbm, x_hbm, wd_hbm, wq_hbm, wkv_hbm,
    kv_hbm, xo_hbm, g_hbm, c_hbm,
    kv_out, x_out, g_low, c_low, up_out, q_v, do_v, x_v, wd_v, wq_v, wkv_v, rs_v,
    kwin, vwin, k_t, scores, tops, probs, dscores, own_kv, kv_send, kv_recv, relay,
    flags, down_send, down_recv, down_low, up_send, up_recv, near_send, near_recv,
    g_full, g_pair, c_full, c_pair, units, slots, c_sum, c_send, c_slots,
    load_sem, out_sem, win_ss, win_rs, down_ss, down_rs, up_ss, up_rs, near_ss, near_rs,
    relay_ss, relay_rs, kv_ss, kv_rs, pair_ss, pair_rs, rs_ss, rs_rs, c_ss, c_rs,
    ag_ss, ag_rs, cag_ss, cag_rs, fin_ss, fin_rs, known,
):
    tokens = q_v.shape[0]
    heads = q_v.shape[1] // HEAD_SIZE
    nz = seq_count // QUAD
    owners = min(nz, UNITS)
    stride = nz // owners
    per_owner = UNITS // owners
    half = x_v.shape[1] // 2
    s = lax.axis_index("seq")
    hd = lax.axis_index("head")
    zi = s // QUAD
    core = s % 2
    x_lo = (s % QUAD) // 2
    sibling = s + 1 - 2 * core
    scale = HEAD_SIZE ** -0.5
    multiplier = ADAPTER_SCALE / math.sqrt(tokens * seq_count)
    pending = []

    def seq_at(by):
        return lax.rem(s + by + seq_count, seq_count)

    def head_at(by):
        return lax.rem(hd + by + head_count, head_count)

    in_row = min(ROW, head_count)

    def row_at(by):
        return hd // in_row * in_row + lax.rem(hd % in_row + by + in_row, in_row)

    other_row = lax.rem(hd + in_row, head_count)

    def z_at(by):
        return lax.rem(zi + by + nz, nz)

    def chip(by, x):
        return z_at(by) * QUAD + x * 2 + core

    def remote(src, dst, ss, rs, target):
        return pltpu.make_async_remote_copy(
            src_ref=src, dst_ref=dst, send_sem=ss, recv_sem=rs,
            device_id={"seq": target}, device_id_type=MESH,
        )

    barrier = pltpu.get_barrier_semaphore()
    near = [sibling, seq_at(2), seq_at(-2), seq_at(4), seq_at(-4)]
    for target in near:
        pl.semaphore_signal(barrier, inc=1, device_id={"seq": target}, device_id_type=MESH)
    near_heads = [row_at(1), row_at(-1)] + ([other_row] if head_count > ROW else [])
    for target in near_heads:
        pl.semaphore_signal(barrier, inc=1, device_id={"head": target}, device_id_type=MESH)

    loads = [
        pltpu.make_async_copy(src, dst, load_sem.at[i])
        for i, (src, dst) in enumerate([
            (k_hbm, kwin.at[3]), (q_hbm, q_v), (x_hbm, x_v), (wd_hbm, wd_v), (v_hbm, vwin.at[3]),
            (do_hbm, do_v), (rs_hbm, rs_v), (wq_hbm, wq_v), (wkv_hbm, wkv_v), (flags_hbm, flags),
        ])
    ]
    for copy in loads:
        copy.start()

    pl.semaphore_wait(barrier, len(near) + len(near_heads))

    rounds = []
    step = 2
    while step < nz:
        rounds.append(step)
        step *= 2

    def tell(i):
        if i < len(rounds):
            for by in (2 * rounds[i], -2 * rounds[i]):
                pl.semaphore_signal(
                    known.at[i], inc=1, device_id={"seq": seq_at(by)}, device_id_type=MESH
                )

    def hear(i):
        if i < len(rounds):
            pl.semaphore_wait(known.at[i], 2)

    def tell_heads(i):
        targets = [row_at(1), row_at(-1)] if i == 0 else [other_row]
        if i == 0 or head_count > ROW:
            for target in targets:
                pl.semaphore_signal(
                    known.at[3 + i], inc=1, device_id={"head": target}, device_id_type=MESH
                )

    def hear_heads(i):
        if i == 0 or head_count > ROW:
            pl.semaphore_wait(known.at[3 + i], 2 - i)

    own = (k_hbm, v_hbm)
    win = (kwin, vwin)

    def cross(c):
        return remote(own[c], win[c].at[1], win_ss.at[c, 0], win_rs.at[c, 1], seq_at(2))

    def give(c):
        return remote(own[c], win[c].at[2], win_ss.at[c, 1], win_rs.at[c, 2], sibling)

    def forward(c, slot):
        return remote(win[c].at[1], win[c].at[slot], win_ss.at[c, 2], win_rs.at[c, slot], sibling)

    for c in range(2):
        cross(c).start()

        @pl.when(core == 0)
        def _():
            give(c).start()

    tell(0)
    tell_heads(0)

    def head_copy(src, dst, ss, rs, by):
        return pltpu.make_async_remote_copy(
            src_ref=src, dst_ref=dst.at[by], send_sem=ss.at[by], recv_sem=rs.at[by],
            device_id={"head": head_at(by)}, device_id_type=MESH,
        )

    def head_start(*args):
        for by in range(1, head_count):
            head_copy(*args, by).start()

        def wait():
            for by in range(1, head_count):
                head_copy(*args, by).wait_send()

        pending.append(wait)

    row_id = lax.broadcasted_iota(jnp.int32, (tokens, tokens), 0)
    col_id = lax.broadcasted_iota(jnp.int32, (tokens, tokens), 1)
    causal = jnp.where(row_id <= col_id, 0.0, -BIG).astype(F32)
    want = (1 - x_lo).astype(F32)
    even = (1 - core).astype(F32)
    c2 = scale * LOG2E

    def head_cols(ref, h):
        return ref[:, h * HEAD_SIZE : (h + 1) * HEAD_SIZE]

    def rows(j):
        return pl.ds(j * tokens, tokens)

    def score_block(j):
        for h in range(heads):
            score = dot_nt(kwin[j], head_cols(q_v, h))
            if j == 3:
                score = score + causal
            scores[h, rows(j), :] = score
            tops[j, h : h + 1, :] = jnp.max(score, axis=0, keepdims=True)
        k_t[:, j * tokens : (j + 1) * tokens] = kwin[j].astype(F32).T.astype(BF16)

    loads[0].wait()
    loads[1].wait()
    score_block(3)
    loads[2].wait()
    loads[3].wait()
    down_part = dot_nt(wd_v[...], x_v[...])
    down_send[...] = down_part.astype(BF16)
    hear(0)
    tell(1)
    hear_heads(0)
    tell_heads(1)

    def rest_of_scores(odd):
        if odd:
            give(0).wait_recv()
            score_block(2)
            cross(0).wait_recv()
            forward(0, 2).start()
            score_block(1)
            forward(0, 0).wait_recv()
            score_block(0)
        else:
            cross(0).wait_recv()
            forward(0, 0).start()
            score_block(1)
            forward(0, 2).wait_recv()
            score_block(2)

    def pass_values_on(odd):
        cross(1).wait_recv()
        forward(1, 2 if odd else 0).start()

    def relay_copy(slot, c):
        return remote(
            kv_send.at[slot, c], relay.at[c], relay_ss.at[c], relay_rs.at[c], sibling
        )

    def back_copy(c):
        return remote(
            kv_send.at[1, c], kv_recv.at[0, c], kv_ss.at[c], kv_rs.at[c], seq_at(-2)
        )

    def near_copy():
        return remote(near_send, near_recv, near_ss, near_rs, seq_at(-2))

    def projected(grads):
        return [
            dot_nt(wkv_v[c * RANK : (c + 1) * RANK, :], grads[c]) for c in range(2)
        ]

    def home_copy():
        return remote(kv_send.at[2], kv_recv.at[1], kv_ss.at[2], kv_rs.at[2], sibling)

    def attention(odd):
        order = (0, 1, 2, 3) if odd else (2, 1, 3)

        def weights(h, _):
            differs = flags[h].astype(F32) - want
            far = differs * differs * BIG
            bias = {0: far, 1: far, 2: 0.0 if odd else far, 3: 0.0}
            at = pl.ds(h, 1)
            top = None
            for j in order:
                high = tops[j, at, :] - bias[j]
                top = high if top is None else jnp.maximum(top, high)
            weight = {}
            total = None
            for j in order:
                weight[j] = jnp.exp2(scores[h, rows(j), :] * c2 - (top * c2 + bias[j]))
                part = jnp.sum(weight[j], axis=0, keepdims=True)
                total = part if total is None else total + part
            inverse = 1.0 / total
            for j in order:
                probs[h, rows(j), :] = (weight[j] * inverse).astype(BF16)
            return 0

        lax.fori_loop(0, heads, weights, 0)

    def summed(left, right, j):
        total = None
        for h in range(heads):
            part = dot_nn(left[h, rows(j), :], head_cols(right, h))
            total = part if total is None else total + part
        return total

    def value_grad(j):
        return summed(probs, do_v, j)

    def key_grad(j):
        for h in range(heads):
            p = probs[h, rows(j), :].astype(F32)
            dp = dot_nt(vwin[j], head_cols(do_v, h))
            dscores[h, rows(j), :] = (p * (dp - rs_v[h : h + 1, :])).astype(BF16)
        return summed(dscores, q_v, j) * scale

    def relayed(odd):
        slot = 0 if odd else 2
        if odd:
            forward(1, 0).wait_recv()
        else:
            forward(1, 2).wait_recv()
        kv_send[slot, 1] = value_grad(slot).astype(BF16)
        relay_copy(slot, 1).start()
        kv_send[slot, 0] = key_grad(slot).astype(BF16)
        relay_copy(slot, 0).start()

    def sent_back(c, grad):
        relay_copy(0, c).wait_recv()
        kv_send[1, c] = (grad + relay[c].astype(F32)).astype(BF16)
        if c == 0:
            for i, part in enumerate(projected(kv_send[1])):
                near_send[i * RANK : (i + 1) * RANK, :] = part.astype(BF16)
            near_copy().start()
        back_copy(c).start()

    def split(fn):
        @pl.when(core == 1)
        def _():
            fn(True)

        @pl.when(core == 0)
        def _():
            fn(False)

    split(rest_of_scores)
    hear_heads(1)
    head_start(down_send, down_recv, down_ss, down_rs)
    hear(1)
    tell(2)
    for i in range(4, 10):
        loads[i].wait()
    split(pass_values_on)

    def window_sent(odd):
        for c in range(2):
            cross(c).wait_send()
            forward(c, 2 if odd else 0).wait_send()
            if not odd:
                give(c).wait_send()

    pending.append(lambda: split(window_sent))
    split(attention)
    split(relayed)
    sent_back(1, value_grad(1))
    sent_back(0, key_grad(1))

    @pl.when(core == 1)
    def _():
        give(1).wait_recv()
        kv_send[2, 0] = key_grad(2).astype(BF16)
        kv_send[2, 1] = value_grad(2).astype(BF16)
        home_copy().start()

    own_kv[0] = key_grad(3)
    own_kv[1] = value_grad(3)

    def grads_sent(odd):
        for c in range(2):
            relay_copy(0 if odd else 2, c).wait_send()
            back_copy(c).wait_send()
        near_copy().wait_send()
        if odd:
            home_copy().wait_send()

    pending.append(lambda: split(grads_sent))

    down = down_part
    for by in range(1, head_count):
        head_copy(down_send, down_recv, down_ss, down_rs, by).wait_recv()
        down = down + down_recv[by].astype(F32)
    down_low[...] = down.astype(BF16)

    def query_grads(odd):
        first = 0 if odd else tokens
        per_half = heads // 2
        acc = jnp.zeros((RANK, tokens), F32)
        for h in range(heads):
            dq = (dot_nn(k_t[:, first:], dscores[h, first:, :]) * scale).astype(BF16)
            col = (h % per_half) * HEAD_SIZE
            g_full[h // per_half, :RANK, col : col + HEAD_SIZE] = dot_nt(down_low[:RANK, :], dq)
            acc = acc + dot_nn(head_cols(wq_v, h), dq)
        up_send[:RANK, :] = acc.astype(BF16)

    split(query_grads)
    hear(2)

    @pl.when(core == 0)
    def _():
        home_copy().wait_recv()
        own_kv[...] = own_kv[...] + kv_recv[1].astype(F32)

    own_part = projected(own_kv[...].astype(BF16))
    near_copy().wait_recv()
    for c in range(2):
        at = slice((c + 1) * RANK, (c + 2) * RANK)
        up_send[at, :] = (
            own_part[c] + near_recv[c * RANK : (c + 1) * RANK, :].astype(F32)
        ).astype(BF16)
    head_start(up_send, up_recv, up_ss, up_rs)

    for c in range(2):
        back_copy(c).wait_recv()
    dkv = (own_kv[...] + kv_recv[0].astype(F32)).astype(BF16)
    kv_out[...] = dkv
    placed = [
        pltpu.make_async_copy(src, dst, out_sem.at[i])
        for i, (src, dst) in enumerate([
            (kv_out, kv_hbm), (x_out, xo_hbm), (g_low, g_hbm), (c_low, c_hbm),
        ])
    ]
    placed[0].start()
    pending.append(placed[0].wait)
    for c in range(2):
        c_full[c] = dot_nn(down_low[(c + 1) * RANK : (c + 2) * RANK, :], dkv[c])

    part_rows = 2 * RANK

    def pair_copy(p):
        at = pl.ds(p * part_rows, part_rows)
        return remote(
            g_full.at[1 - core, at], g_pair.at[at], pair_ss.at[p], pair_rs.at[p], sibling
        )

    def pair_copy_c():
        return remote(c_full.at[1 - core], c_pair, pair_ss.at[2], pair_rs.at[2], sibling)

    pair_copy_c().start()
    pending.append(lambda: pair_copy_c().wait_send())

    def far_first(n, i):
        return n // 2 + lax.rem(i + 1, 2) * (i // 2) - lax.rem(i, 2) * ((i + 1) // 2)

    def owner_at(by):
        return lax.rem(zi // stride + by, owners)

    def scatter_copy(p, owner):
        slot = x_lo * nz + zi
        return remote(
            units.at[p, owner], slots.at[slot], rs_ss.at[p, owner], rs_rs.at[slot],
            (owner * stride + p * (stride // 2)) * QUAD + p * 2 + core,
        )

    def arrived(z, x):
        slot = x * nz + z
        remote(units.at[0, 0], slots.at[slot], rs_ss.at[0, 0], rs_rs.at[slot], sibling).wait_recv()
        return slots[slot].astype(F32)

    def loop(first, last, fn):
        def body(i, _):
            fn(i)
            return 0

        lax.fori_loop(first, last, body, 0)

    def is_owner(p):
        return jnp.logical_and(x_lo == p, lax.rem(zi, stride) == p * (stride // 2))

    def each_owner(p, fn):
        loop(0, owners - 1, lambda i: fn(owner_at(far_first(owners, i))))

        @pl.when(jnp.logical_not(is_owner(p)))
        def _():
            fn(zi // stride)

    def scatter(p):
        pair_copy(p).wait_recv()
        at = pl.ds(p * part_rows, part_rows)
        g = (g_full[core, at, :] + g_pair[at, :]).astype(BF16)
        for u in range(UNITS):
            units[p, u // per_owner, u % per_owner] = g[:, u * 128 : (u + 1) * 128]
        each_owner(p, lambda owner: scatter_copy(p, owner).start())
        pending.append(lambda: each_owner(p, lambda owner: scatter_copy(p, owner).wait_send()))

    c_owner = ((nz // 2 + 1) % nz) * QUAD + 2 + core
    is_c_owner = s == c_owner

    def c_copy(slot):
        return remote(c_send, c_slots.at[slot], c_ss, c_rs.at[slot], c_owner)

    pair_copy_c().wait_recv()
    c_sum[...] = c_full[core] + c_pair[...]
    c_send[...] = c_sum[...].astype(BF16)

    @pl.when(jnp.logical_not(is_c_owner))
    def _():
        c_copy(x_lo * nz + zi).start()

    def c_sent():
        @pl.when(jnp.logical_not(is_c_owner))
        def _():
            c_copy(x_lo * nz + zi).wait_send()

    pending.append(c_sent)

    up = up_send[...].astype(F32)
    for by in range(1, head_count):
        head_copy(up_send, up_recv, up_ss, up_rs, by).wait_recv()
        up = up + up_recv[by].astype(F32)
    up_out[...] = up.astype(BF16)

    def down_rows(c):
        g_full[c, RANK:, :] = dot_nn(up_out[...], x_v[:, c * half : (c + 1) * half])

    def pair_sums(side):
        down_rows(1 - side)
        for p in range(2):
            pair_copy(p).start()
        down_rows(side)

    @pl.when(core == 0)
    def _():
        pair_sums(0)

    @pl.when(core == 1)
    def _():
        pair_sums(1)

    for p in range(2):
        pending.append(lambda p=p: pair_copy(p).wait_send())
    for p in range(2):
        scatter(p)

    for c in range(4):
        cols = slice(c * half // 2, (c + 1) * half // 2)
        part = lax.dot_general(
            up_out[...], wd_v[:, cols], (((0,), (0,)), ((), ())), preferred_element_type=F32
        )
        x_out[:, cols] = (ADAPTER_SCALE * part).astype(BF16)
    placed[1].start()
    pending.append(placed[1].wait)

    def unit_ref(p, u):
        return g_low.at[
            pl.ds(p * part_rows, part_rows),
            pl.ds(pl.multiple_of(core * half + u * 128, 128), 128),
        ]

    def gather_copy(p, owner, i, by, x):
        u = owner * per_owner + i
        ref = unit_ref(p, u)
        return remote(
            ref, ref, ag_ss.at[(x * nz + by) * per_owner + i], ag_rs.at[p, u], chip(by, x)
        )

    def each_target(p, fn):
        loop(0, nz - 1, lambda i: (fn(far_first(nz, i), 0), fn(far_first(nz, i), 1)))
        fn(0, 1 - p)

    def gather(p):
        @pl.when(is_owner(p))
        def _():
            mine = zi // stride
            total = units[p, mine].astype(F32)
            for by in range(0, nz):
                for x in (p, 1 - p):
                    if by == 0 and x == p:
                        continue
                    total = total + arrived(z_at(by), x)
            total = (total * multiplier).astype(BF16)
            for i in range(per_owner):
                unit_ref(p, mine * per_owner + i)[...] = total[i]

            def start(by, x):
                for i in range(per_owner):
                    gather_copy(p, mine, i, by, x).start()

            each_target(p, start)

    def gather_sent():
        for p in range(2):

            @pl.when(is_owner(p))
            def _():
                def wait(by, x):
                    for i in range(per_owner):
                        gather_copy(p, zi // stride, i, by, x).wait_send()

                each_target(p, wait)

    def c_ref():
        return c_low.at[pl.ds(pl.multiple_of(core * RANK, RANK), RANK), :]

    def c_gather_copy(by, x):
        return remote(c_ref(), c_ref(), cag_ss.at[x * nz + by], cag_rs, chip(by, x))

    gather(0)

    @pl.when(is_c_owner)
    def _():
        total = c_sum[...]
        for by in range(0, nz):
            for x in (1, 0):
                if by == 0 and x == 1:
                    continue
                slot = x * nz + z_at(by)
                c_copy(slot).wait_recv()
                total = total + c_slots[slot].astype(F32)
        c_ref()[...] = (total * multiplier).astype(BF16)
        each_target(1, lambda by, x: c_gather_copy(by, x).start())

    def c_gather_sent():
        @pl.when(is_c_owner)
        def _():
            each_target(1, lambda by, x: c_gather_copy(by, x).wait_send())

    gather(1)
    for wait in pending:
        wait()

    def wait_gathered(p):
        def wait(owner):
            for i in range(per_owner):
                gather_copy(p, owner, i, 0, 0).wait_recv()

        each_owner(p, wait)

    def final_copy(p, side):
        ref = g_low.at[
            pl.ds(p * part_rows, part_rows), pl.ds(pl.multiple_of(side * half, 128), half)
        ]
        return remote(ref, ref, fin_ss.at[p], fin_rs.at[p], sibling)

    def final_copy_c(side):
        ref = c_low.at[pl.ds(pl.multiple_of(side * RANK, RANK), RANK), :]
        return remote(ref, ref, fin_ss.at[2], fin_rs.at[2], sibling)

    wait_gathered(0)
    final_copy(0, core).start()

    @pl.when(jnp.logical_not(is_c_owner))
    def _():
        c_gather_copy(0, 0).wait_recv()

    final_copy_c(core).start()
    wait_gathered(1)
    final_copy(1, core).start()

    gather_sent()
    c_gather_sent()
    final_copy_c(1 - core).wait_recv()
    placed[3].start()
    for p in range(2):
        final_copy(p, 1 - core).wait_recv()
    placed[2].start()
    final_copy_c(core).wait_send()
    for p in range(2):
        final_copy(p, core).wait_send()
    placed[3].wait()
    placed[2].wait()


def place(
    kv, x, g, c, down_o, up_q_o, up_kv_o, kv_o, x_o, kv_v, x_v, g_v, c_v, g_w, c_w, in_sems, out_sems
):
    ways = [
        (x, x_v, [(x_v, x_o)]),
        (g, g_v, [(g_w.at[RANK:], down_o), (g_w.at[:RANK], up_q_o)]),
        (kv, kv_v, [(kv_v, kv_o)]),
        (c, c_v, [(c_w, up_kv_o)]),
    ]
    arriving = [
        pltpu.make_async_copy(src, dst, in_sems.at[i]) for i, (src, dst, _) in enumerate(ways)
    ]
    for copy in arriving:
        copy.start()
    leaving = []
    wide = {1: (g_v, g_w), 3: (c_v, c_w)}
    for i, (copy, (_, _, targets)) in enumerate(zip(arriving, ways)):
        copy.wait()
        if i in wide:
            wide[i][1][...] = wide[i][0][...].astype(F32)
        for src, dst in targets:
            leaving.append(pltpu.make_async_copy(src, dst, out_sems.at[len(leaving)]))
            leaving[-1].start()
    for copy in leaving:
        copy.wait()


def per_device(
    queries, layer_key_rows, layer_value_rows, output_gradient, output_row_sums,
    shifted_head_flags, inputs, adapter_down_weight, query_up_weight, key_value_up_weight,
):
    seq_count = lax.axis_size("seq")
    head_count = lax.axis_size("head")
    tokens, columns = queries.shape
    heads = columns // HEAD_SIZE
    width = inputs.shape[1]
    nz = seq_count // QUAD
    owners = min(nz, UNITS)
    per_owner = UNITS // owners
    flat_down = adapter_down_weight.reshape(3 * RANK, width)
    flat_kv_up = key_value_up_weight.reshape(2 * RANK, HEAD_SIZE)
    vmem = pltpu.VMEM
    sem = pltpu.SemaphoreType.DMA
    anywhere = pl.BlockSpec(memory_space=pltpu.HBM)
    parts = pl.pallas_call(
        functools.partial(kernel, seq_count, head_count),
        out_shape=(
            jax.ShapeDtypeStruct((2, tokens, HEAD_SIZE), BF16),
            jax.ShapeDtypeStruct((tokens, width), BF16),
            jax.ShapeDtypeStruct((4 * RANK, width), BF16),
            jax.ShapeDtypeStruct((2 * RANK, HEAD_SIZE), BF16),
        ),
        in_specs=[anywhere] * 10,
        out_specs=(anywhere,) * 4,
        scratch_shapes=[
            vmem((2, tokens, HEAD_SIZE), BF16),
            vmem((tokens, width), BF16),
            vmem((4 * RANK, width), BF16),
            vmem((2 * RANK, HEAD_SIZE), BF16),
            vmem((3 * RANK, tokens), BF16),
            vmem((tokens, columns), BF16),
            vmem((tokens, columns), BF16),
            vmem((tokens, width), BF16),
            vmem((3 * RANK, width), BF16),
            vmem((RANK, columns), BF16),
            vmem((2 * RANK, HEAD_SIZE), BF16),
            vmem((heads, tokens), F32),
            vmem((4, tokens, HEAD_SIZE), BF16),
            vmem((4, tokens, HEAD_SIZE), BF16),
            vmem((HEAD_SIZE, 4 * tokens), BF16),
            vmem((heads, 4 * tokens, tokens), F32),
            vmem((4, heads, tokens), F32),
            vmem((heads, 4 * tokens, tokens), BF16),
            vmem((heads, 4 * tokens, tokens), BF16),
            vmem((2, tokens, HEAD_SIZE), F32),
            vmem((3, 2, tokens, HEAD_SIZE), BF16),
            vmem((2, 2, tokens, HEAD_SIZE), BF16),
            vmem((2, tokens, HEAD_SIZE), BF16),
            pltpu.SMEM((heads,), jnp.int32),
            vmem((3 * RANK, tokens), BF16),
            vmem((head_count, 3 * RANK, tokens), BF16),
            vmem((3 * RANK, tokens), BF16),
            vmem((3 * RANK, tokens), BF16),
            vmem((head_count, 3 * RANK, tokens), BF16),
            vmem((2 * RANK, tokens), BF16),
            vmem((2 * RANK, tokens), BF16),
            vmem((2, 4 * RANK, width // 2), F32),
            vmem((4 * RANK, width // 2), F32),
            vmem((2, RANK, HEAD_SIZE), F32),
            vmem((RANK, HEAD_SIZE), F32),
            vmem((2, owners, per_owner, 2 * RANK, 128), BF16),
            vmem((2 * nz, per_owner, 2 * RANK, 128), BF16),
            vmem((RANK, HEAD_SIZE), F32),
            vmem((RANK, HEAD_SIZE), BF16),
            vmem((2 * nz, RANK, HEAD_SIZE), BF16),
            sem((10,)), sem((4,)),
            sem((2, 3)), sem((2, 4)),
            sem((head_count,)), sem((head_count,)),
            sem((head_count,)), sem((head_count,)),
            sem, sem,
            sem((2,)), sem((2,)),
            sem((3,)), sem((3,)),
            sem((3,)), sem((3,)),
            sem((2, owners)), sem((2 * nz,)),
            sem, sem((2 * nz,)),
            sem((2 * nz * per_owner,)), sem((2, UNITS)),
            sem((2 * nz,)), sem,
            sem((3,)), sem((3,)),
            pltpu.SemaphoreType.REGULAR((5,)),
        ],
        compiler_params=pltpu.CompilerParams(
            collective_id=0, has_side_effects=True, vmem_limit_bytes=VMEM_BYTES
        ),
    )(
        queries, layer_key_rows, layer_value_rows, output_gradient, output_row_sums,
        shifted_head_flags, inputs, flat_down, query_up_weight, flat_kv_up,
    )
    down_gradient, grad_up_q, grad_up_kv, kv_gradient, grad_inputs = pl.pallas_call(
        place,
        out_shape=(
            jax.ShapeDtypeStruct((3 * RANK, width), F32),
            jax.ShapeDtypeStruct((RANK, columns), F32),
            jax.ShapeDtypeStruct((2 * RANK, HEAD_SIZE), F32),
            jax.ShapeDtypeStruct((2, tokens, HEAD_SIZE), BF16),
            jax.ShapeDtypeStruct((tokens, width), BF16),
        ),
        in_specs=[anywhere] * 4,
        out_specs=(anywhere,) * 5,
        scratch_shapes=[
            vmem((2, tokens, HEAD_SIZE), BF16),
            vmem((tokens, width), BF16),
            vmem((4 * RANK, width), BF16),
            vmem((2 * RANK, HEAD_SIZE), BF16),
            vmem((4 * RANK, width), F32),
            vmem((2 * RANK, HEAD_SIZE), F32),
            sem((4,)),
            sem((5,)),
        ],
        compiler_params=pltpu.CompilerParams(vmem_limit_bytes=VMEM_BYTES),
    )(*parts)
    return (
        grad_inputs,
        kv_gradient,
        down_gradient.reshape(3, RANK, width),
        grad_up_q,
        grad_up_kv.reshape(2, RANK, HEAD_SIZE),
    )


def solution(mesh):
    placed = (
        P("seq", "head"),
        P("seq", "head"),
        P("seq", "head"),
        P("seq", "head"),
        P("head", "seq"),
        P("head"),
        P("seq", "head"),
        P(None, None, "head"),
        P(None, "head"),
        P(None, None, "head"),
    )
    return jax.shard_map(
        per_device,
        mesh=mesh,
        in_specs=placed,
        out_specs=(
            P("seq", "head"),
            P(None, "seq", "head"),
            P(None, None, "head"),
            P(None, "head"),
            P(None, None, "head"),
        ),
        check_vma=False,
    )
```
